128 devices in a mesh: dp: 8 (over x, z_hi), sq: 8 (over z_lo, y), hd: 2 (over core).
Axes of the slice: x: 4, y: 4, z: 4 (z_hi: 2, z_lo: 2; z = z_hi * 2 + z_lo), core: 2. Of those that a mesh axis runs over, the one named last changes fastest.
Arguments:
- inputs: bfloat16 [8, 2048, 1536], P('dp', ('sq', 'hd')), may hold values from -6 to 6
- norm_gain: float32 [1536], replicated, may hold values from 0.5 to 1.5
- w_query: bfloat16 [1536, 1536], P(('sq', 'hd')), may hold values from -0.15625 to 0.15625
- w_key: bfloat16 [1536, 512], P(('sq', 'hd')), may hold values from -0.15625 to 0.15625
- w_value: bfloat16 [1536, 512], P(('sq', 'hd')), may hold values from -0.15625 to 0.15625
- w_out: bfloat16 [1536, 1536], P(('sq', 'hd')), may hold values from -0.625 to 0.625
- query_gain: float32 [64], replicated, may hold values from 0.5 to 1.5
- key_gain: float32 [64], replicated, may hold values from 0.5 to 1.5
- ffn_gain: float32 [1536], replicated, may hold values from 0.5 to 1.5
- w_gate: bfloat16 [1536, 6912], P(('sq', 'hd')), may hold values from -0.15625 to 0.15625
- w_up: bfloat16 [1536, 6912], P(('sq', 'hd')), may hold values from -0.15625 to 0.15625
- w_down: bfloat16 [6912, 1536], P(('sq', 'hd')), may hold values from -0.078125 to 0.078125
- cotangent: bfloat16 [8, 2048, 1536], P('dp', ('sq', 'hd')), may hold values from -6 to 6
Outputs:
- output: bfloat16 [8, 2048, 1536], P('dp', ('sq', 'hd'))
- input_grad: float32 [8, 2048, 1536], P('dp', ('sq', 'hd'))
- norm_gain_grad: float32 [1536], replicated
- w_query_grad: float32 [1536, 1536], P(('sq', 'hd'))
- w_key_grad: float32 [1536, 512], P(('sq', 'hd'))
- w_value_grad: float32 [1536, 512], P(('sq', 'hd'))
- w_out_grad: float32 [1536, 1536], P(('sq', 'hd'))
- query_gain_grad: float32 [64], replicated
- key_gain_grad: float32 [64], replicated
- ffn_gain_grad: float32 [1536], replicated
- w_gate_grad: float32 [1536, 6912], P(('sq', 'hd'))
- w_up_grad: float32 [1536, 6912], P(('sq', 'hd'))
- w_down_grad: float32 [6912, 1536], P(('sq', 'hd'))
The draws below stay inside these ranges and needn't reach their ends.
All inputs are finite; a program needn't handle non-finite values.
Results may differ from the reference program's by a relative error of at most 0.025.
Values may be sent and summed in bfloat16 or wider, within the bound.
No kernel may reach another device: no remote copies, remote signals or barrier semaphores. Data moves between devices by JAX's collectives and lax.ppermute only.
A program may use at most 256 MiB of HBM per device.

```python
import jax
import jax.numpy as jnp
from jax import lax

D = 1536
HQ = 24
HK = 8
HS = 64
FF = 6912
LENGTH = 2048
SEQS = 8


def steps_of(own_key, extent, pieces, smallest, top_value):
    level, own = 1.0, jax.random.fold_in(own_key, 6)
    for dim, blocks in pieces:
        draws = jnp.exp(jax.random.uniform(jax.random.fold_in(own, dim), (blocks,), jnp.float32, smallest / len(pieces), top_value / len(pieces)))
        level = level * jnp.repeat(draws, extent[dim] // blocks).reshape([-1 if axis == dim else 1 for axis in range(len(extent))])
    return level


def centred(rng, extent, spread, limit, pieces=(), kind=jnp.bfloat16):
    array = jax.random.normal(rng, extent, jnp.float32) * spread
    if len(pieces) > 0:
        array = steps_of(rng, extent, pieces, -0.22, 0.18) * array
    return jnp.clip(array, min=-limit, max=limit).astype(kind)


def setup_inputs(seed: int = 0) -> dict:
    arg_keys = jax.random.split(jax.random.key(seed), 14)
    inputs = centred(arg_keys[0], (SEQS, LENGTH, D), 1.0, 6.0, ((0, 8), (1, 16)))
    norm_gain = jnp.clip(1.0 + 0.1 * jax.random.normal(arg_keys[1], (D,), jnp.float32), 0.5, 1.5)
    w_query = centred(arg_keys[2], (D, HQ * HS), D ** -0.5, 0.15625, ((0, 16),))
    w_key = centred(arg_keys[3], (D, HK * HS), D ** -0.5, 0.15625, ((0, 16),))
    w_value = centred(arg_keys[4], (D, HK * HS), D ** -0.5, 0.15625, ((0, 16),))
    w_out = centred(arg_keys[5], (HQ * HS, D), (HQ * HS // 16) ** -0.5, 0.625, ((0, 16),))
    query_gain = jnp.clip(1.0 + 0.1 * jax.random.normal(arg_keys[6], (HS,), jnp.float32), 0.5, 1.5)
    key_gain = jnp.clip(1.0 + 0.1 * jax.random.normal(arg_keys[7], (HS,), jnp.float32), 0.5, 1.5)
    ffn_gain = jnp.clip(1.0 + 0.1 * jax.random.normal(arg_keys[8], (D,), jnp.float32), 0.5, 1.5)
    w_gate = centred(arg_keys[9], (D, FF), D ** -0.5, 0.15625, ((0, 16),))
    w_up = centred(arg_keys[10], (D, FF), D ** -0.5, 0.15625, ((0, 16),))
    w_down = centred(arg_keys[11], (FF, D), FF ** -0.5, 0.078125, ((0, 16),))
    cotangent = centred(arg_keys[12], (SEQS, LENGTH, D), 1.0, 6.0, ((0, 8), (1, 16)))
    return dict(inputs=inputs, norm_gain=norm_gain, w_query=w_query, w_key=w_key, w_value=w_value, w_out=w_out, query_gain=query_gain, key_gain=key_gain, ffn_gain=ffn_gain, w_gate=w_gate, w_up=w_up, w_down=w_down, cotangent=cotangent)


EPSILON = 1e-05
ROPE_BASE = 1000000.0
SCORE_SCALE = 0.125
MASKED = -1e+30
PRECISE = lax.Precision.HIGHEST

@jax.custom_vjp
def low(v):
    return lax.optimization_barrier(v.astype(jnp.bfloat16)).astype(jnp.float32)

@jax.custom_vjp
def low_back(v):
    return v

def low_keep(v):
    return (low(v), None)

def low_pass(kept, grad):
    return (grad,)

def back_keep(v):
    return (v, None)

def back_low(kept, grad):
    return (low(grad),)
low.defvjp(low_keep, low_pass)
low_back.defvjp(back_keep, back_low)

def matmul(left, right):
    return jnp.dot(left, right, precision=PRECISE, preferred_element_type=jnp.float32)

def rms_norm(values, gain):
    factor = lax.rsqrt(lax.optimization_barrier(jnp.mean(values * values, axis=-1, keepdims=True)) + EPSILON)
    return values * factor * gain

def rope_tables(positions, width):
    half = width // 2
    freqs = ROPE_BASE ** (-jnp.arange(half, dtype=jnp.float32) * 2.0 / width)
    angles = positions[:, None].astype(jnp.float32) * freqs[None, :]
    return (jnp.cos(angles)[:, None, :], jnp.sin(angles)[:, None, :])

def rotate(values, cosine, sine):
    half = values.shape[-1] // 2
    first = values[..., :half]
    second = values[..., half:]
    return jnp.concatenate([first * cosine - second * sine, second * cosine + first * sine], axis=-1)

def one_sequence(tokens, norm_gain, w_query, w_key, w_value, w_out, query_gain, key_gain, ffn_gain, w_gate, w_up, w_down):
    length = tokens.shape[0]
    group = HQ // HK
    normed = low(rms_norm(tokens, norm_gain))
    query_lin = low(low_back(matmul(normed, w_query))).reshape(length, HQ, HS)
    key_lin = low(low_back(matmul(normed, w_key))).reshape(length, HK, HS)
    value_lin = low(low_back(matmul(normed, w_value))).reshape(length, HK, HS)
    positions = jnp.arange(length, dtype=jnp.int32)
    cosine, sine = rope_tables(positions, HS)
    query_rot = low(rotate(rms_norm(query_lin, query_gain), cosine, sine)).reshape(length, HK, group, HS)
    key_rot = low(rotate(rms_norm(key_lin, key_gain), cosine, sine))
    block_rows = min(512, length)

    def attend(start):
        query_block = lax.dynamic_slice_in_dim(query_rot, start, block_rows, 0)
        scores = jnp.einsum('qhgd,khd->hgqk', query_block, key_rot, precision=PRECISE) * SCORE_SCALE
        scores = low_back(scores)
        rows = start + jnp.arange(block_rows, dtype=jnp.int32)
        scores = jnp.where(rows[:, None] >= positions[None, :], scores, MASKED)
        peak = lax.optimization_barrier(jnp.max(scores, axis=-1, keepdims=True))
        exponent = jnp.exp(scores - peak)
        weights = low(exponent / lax.optimization_barrier(jnp.sum(exponent, axis=-1, keepdims=True)))
        result = jnp.einsum('hgqk,khd->qhgd', weights, value_lin, precision=PRECISE)
        return result.reshape(block_rows, HQ * HS)
    starts = jnp.arange(length // block_rows, dtype=jnp.int32) * block_rows
    attended = lax.map(jax.checkpoint(attend), starts).reshape(length, HQ * HS)
    attended = low(low_back(attended))
    middle = tokens + low_back(matmul(attended, w_out))
    ffn_in = low(rms_norm(middle, ffn_gain))
    gate = low_back(matmul(ffn_in, w_gate))
    up = low_back(matmul(ffn_in, w_up))
    hidden = low(jax.nn.silu(gate) * up)
    return middle + matmul(hidden, w_down)

def reference(inputs, norm_gain, w_query, w_key, w_value, w_out, query_gain, key_gain, ffn_gain, w_gate, w_up, w_down, cotangent):
    params = tuple((weight.astype(jnp.float32) for weight in (norm_gain, w_query, w_key, w_value, w_out, query_gain, key_gain, ffn_gain, w_gate, w_up, w_down)))

    def forward(sequences, *weights):

        def step(carry, sequence):
            return (carry, one_sequence(sequence, *weights))
        _, outputs = lax.scan(jax.checkpoint(step), jnp.zeros((), jnp.float32), sequences)
        return outputs
    output, pullback = jax.vjp(forward, inputs.astype(jnp.float32), *params)
    grads = pullback(cotangent.astype(jnp.float32))
    return (output.astype(jnp.bfloat16), grads[0], grads[1], grads[2], grads[3], grads[4], grads[5], grads[6], grads[7], grads[8], grads[9], grads[10], grads[11])
```

```python
import jax
import jax.numpy as jnp
from jax import lax
from jax.experimental import pallas as pl
from jax.experimental.pallas import tpu as pltpu
from jax.sharding import PartitionSpec as P

HQ = 24
HK = 8
HS = 64
GROUP = HQ // HK

EPSILON = 1e-05
ROPE_BASE = 1000000.0
SCORE_SCALE = 0.125

RING = 4
OFFSETS = ((2, 1), (2, 0), (1, 1), (3, 1), (1, 0), (3, 0), (0, 1))
BLOCK = 128
ROWS = GROUP * BLOCK


def rms_forward(values, gain):
    factor = lax.rsqrt(jnp.mean(values * values, axis=-1, keepdims=True) + EPSILON)
    return values * factor * gain


def rms_backward(values, gain, grad_out):
    factor = lax.rsqrt(jnp.mean(values * values, axis=-1, keepdims=True) + EPSILON)
    normal = values * factor
    scaled = grad_out * gain
    grad_in = factor * (scaled - normal * jnp.mean(scaled * normal, axis=-1, keepdims=True))
    grad_gain = jnp.sum(grad_out * normal, axis=0)
    return (grad_in, grad_gain)


def dot(left, right, contract):
    return lax.dot_general(
        left, right, (((contract[0],), (contract[1],)), ((), ())), preferred_element_type=jnp.float32
    )


def neighbour(index, dy, dz):
    return (index // RING + dz) % 2 * RING + (index % RING + dy) % RING


def shift(array, dy, dz):
    return lax.ppermute(array, "sq", [(i, neighbour(i, dy, dz)) for i in range(2 * RING)])


def place(buffer, array, index):
    return lax.dynamic_update_index_in_dim(buffer, array, index, 0)


def gather_blocks(array):
    me = lax.axis_index("sq")
    arrived = [shift(array, dy, dz) for dy, dz in OFFSETS]
    whole = place(jnp.zeros((2 * RING, *array.shape), array.dtype), array, me)
    for (dy, dz), block in zip(OFFSETS, arrived):
        whole = place(whole, block, neighbour(me, -dy, dz))
    return whole


def exchange_blocks(blocks):
    me = lax.axis_index("sq")
    whole = jnp.zeros_like(blocks)
    whole = place(whole, lax.dynamic_index_in_dim(blocks, me, 0, keepdims=False), me)
    arrived = [
        shift(lax.dynamic_index_in_dim(blocks, neighbour(me, dy, dz), 0, keepdims=False), dy, dz)
        for dy, dz in OFFSETS
    ]
    for (dy, dz), block in zip(OFFSETS, arrived):
        whole = place(whole, block, neighbour(me, -dy, dz))
    return whole


def scatter_sum(parts):
    me = lax.axis_index("sq")
    arrived = [
        shift(lax.dynamic_index_in_dim(parts, neighbour(me, dy, dz), 0, keepdims=False), dy, dz)
        for dy, dz in OFFSETS
    ]
    total = lax.dynamic_index_in_dim(parts, me, 0, keepdims=False).astype(jnp.float32)
    for block in arrived:
        total = total + block.astype(jnp.float32)
    return total


def shift_x(array, dx):
    return lax.ppermute(array, "dp", [(i, (i + 2 * dx) % (2 * RING)) for i in range(2 * RING)])


def other_z(array):
    return lax.ppermute(array, "dp", [(i, i ^ 1) for i in range(2 * RING)])


def sequence_scatter(pieces):
    me = lax.axis_index("dp")
    x, z = me // 2, me % 2
    pieces = pieces.reshape(RING, 2, *pieces.shape[1:])
    take = lambda i: lax.dynamic_index_in_dim(pieces, i % RING, 0, keepdims=False)
    arrived = [shift_x(take(x + dx), dx) for dx in (2, 1, 3)]
    total = take(x).astype(jnp.float32)
    for block in arrived:
        total = total + block.astype(jnp.float32)
    total = total.astype(jnp.bfloat16)
    mine = lax.dynamic_index_in_dim(total, z, 0, keepdims=False)
    came = other_z(lax.dynamic_index_in_dim(total, 1 - z, 0, keepdims=False))
    return (mine.astype(jnp.float32) + came.astype(jnp.float32)).astype(jnp.bfloat16)


def sequence_gather(piece):
    me = lax.axis_index("dp")
    x, z = me // 2, me % 2
    came = other_z(piece)
    pair = jnp.stack([jnp.where(z == 0, piece, came), jnp.where(z == 0, came, piece)])
    arrived = [shift_x(pair, dx) for dx in (2, 1, 3)]
    whole = place(jnp.zeros((RING, *pair.shape), pair.dtype), pair, x)
    for dx, block in zip((2, 1, 3), arrived):
        whole = place(whole, block, (x - dx) % RING)
    return whole.reshape(2 * RING, *piece.shape)


def sum_everywhere(terms):
    for axis, count in (("hd", 2), ("sq", 8), ("dp", 8)):
        step = 1
        while step < count:
            terms = terms + lax.ppermute(terms, axis, [(i, i ^ step) for i in range(count)])
            step *= 2
    return terms


def after(array, *earlier):
    return lax.optimization_barrier((array, *earlier))[0]


def partner(array):
    return lax.ppermute(array, "hd", [(0, 1), (1, 0)])


def both_cores(array, axis):
    other = partner(array)
    first = lax.axis_index("hd") == 0
    return jnp.stack([jnp.where(first, array, other), jnp.where(first, other, array)], axis=axis)


def sum_cores(terms, axis):
    hd = lax.axis_index("hd")
    mine = lax.dynamic_index_in_dim(terms, hd, axis, keepdims=False)
    other = lax.dynamic_index_in_dim(terms, 1 - hd, axis, keepdims=False)
    return (mine.astype(jnp.float32) + partner(other).astype(jnp.float32)).astype(jnp.bfloat16)


def turn(values, cosine, sine):
    first, second = values[: HS // 2], values[HS // 2 :]
    return jnp.concatenate([first * cosine - second * sine, second * cosine + first * sine], axis=0)


def unturn(grads, cosine, sine):
    first, second = grads[: HS // 2], grads[HS // 2 :]
    return jnp.concatenate([first * cosine + second * sine, second * cosine - first * sine], axis=0)


def head_norm(values, gain):
    return values * lax.rsqrt(jnp.mean(values * values, axis=0, keepdims=True) + EPSILON) * gain


def head_norm_back(values, gain, grad_out):
    factor = lax.rsqrt(jnp.mean(values * values, axis=0, keepdims=True) + EPSILON)
    normal = values * factor
    scaled = grad_out * gain
    grad_in = factor * (scaled - normal * jnp.mean(scaled * normal, axis=0, keepdims=True))
    return grad_in, grad_out * normal


def allowed_keys(hd):
    key = lax.broadcasted_iota(jnp.int32, (2 * BLOCK, ROWS), 0)
    query = lax.broadcasted_iota(jnp.int32, (2 * BLOCK, ROWS), 1) % BLOCK
    bound = jnp.where(key < BLOCK, key, jnp.where(hd == 1, -1, BLOCK))
    return bound <= query


def attend_kernel(
    hd_ref, own_ref, other_ref, cos_ref, sin_ref, cos2_ref, sin2_ref, qgain_ref, kgain_ref,
    blocks_ref, att_ref, out_ref, lse_ref, q_ref, kt_ref, k_ref, v_ref, vt_ref,
):
    count = own_ref.shape[1] // BLOCK
    qgain, kgain = qgain_ref[...], kgain_ref[...]
    vt_ref[HS:, :] = jnp.ones((HS, vt_ref.shape[1]), jnp.bfloat16)
    for c in range(count):
        cols = slice(c * BLOCK, (c + 1) * BLOCK)
        sides = (
            (own_ref[GROUP * HS :, cols], cos_ref[:, cols], sin_ref[:, cols]),
            (other_ref[:, cols], cos2_ref[:, cols], sin2_ref[:, cols]),
        )
        for side, (pair, cosine, sine) in enumerate(sides):
            pair = pair.astype(jnp.float32)
            place_at = slice((2 * c + side) * BLOCK, (2 * c + side + 1) * BLOCK)
            key = turn(head_norm(pair[:HS], kgain), cosine, sine)
            kt_ref[:, place_at] = key.astype(jnp.bfloat16)
            k_ref[place_at, :] = key.T.astype(jnp.bfloat16)
            vt_ref[:HS, place_at] = pair[HS:].astype(jnp.bfloat16)
            v_ref[place_at, :] = pair[HS:].T.astype(jnp.bfloat16)
        for head in range(GROUP):
            query = own_ref[head * HS : (head + 1) * HS, cols].astype(jnp.float32)
            query = turn(head_norm(query, qgain), cos_ref[:, cols], sin_ref[:, cols])
            q_ref[c, :, head * BLOCK : (head + 1) * BLOCK] = (query * SCORE_SCALE).astype(jnp.bfloat16)
    allowed = allowed_keys(hd_ref[0])
    for i in range(count):
        query = q_ref[i]
        total = jnp.zeros((2 * HS, ROWS), jnp.float32)
        for c in range(i + 1):
            keys = slice(2 * c * BLOCK, 2 * (c + 1) * BLOCK)
            weights = jnp.exp(dot(k_ref[keys, :], query, (1, 0)))
            if c == i:
                weights = jnp.where(allowed, weights, 0.0)
            total = total + dot(vt_ref[:, keys], weights.astype(jnp.bfloat16), (1, 0))
        norm = total[HS : HS + 1]
        result = total[:HS] / norm
        lse_ref[i : i + 1, :] = jnp.log(norm)
        out_ref[i] = result
        for head in range(GROUP):
            part = result[:, head * BLOCK : (head + 1) * BLOCK].astype(jnp.bfloat16)
            att_ref[head * HS : (head + 1) * HS, i * BLOCK : (i + 1) * BLOCK] = part
            blocks_ref[i, head * HS : (head + 1) * HS, :] = part


def attend_back_kernel(
    hd_ref, own_ref, grad_ref, cos_ref, sin_ref, qgain_ref, out_ref, lse_ref, q_ref, kt_ref, k_ref, v_ref,
    qgrad_ref, kv_own_ref, kv_other_ref, gain_ref, dk_ref, dv_ref,
):
    count = own_ref.shape[1] // BLOCK
    qgain = qgain_ref[...]
    allowed = allowed_keys(hd_ref[0])
    gain_total = jnp.zeros((HS, BLOCK), jnp.float32)
    for i in range(count):
        cols = slice(i * BLOCK, (i + 1) * BLOCK)
        query = q_ref[i]
        grad = jnp.concatenate([grad_ref[i, head * HS : (head + 1) * HS, :] for head in range(GROUP)], axis=1)
        delta = jnp.sum(grad.astype(jnp.float32) * out_ref[i], axis=0, keepdims=True)
        lse = lse_ref[i : i + 1, :]
        query_grad = jnp.zeros((HS, ROWS), jnp.float32)
        for c in range(i + 1):
            keys = slice(2 * c * BLOCK, 2 * (c + 1) * BLOCK)
            weights = jnp.exp(dot(k_ref[keys, :], query, (1, 0)) - lse)
            if c == i:
                weights = jnp.where(allowed, weights, 0.0)
            prob_grad = dot(v_ref[keys, :], grad, (1, 0))
            score_grad = (weights * (prob_grad - delta)).astype(jnp.bfloat16)
            value_part = dot(weights.astype(jnp.bfloat16), grad, (1, 1))
            key_part = dot(score_grad, query, (1, 1))
            if c == i:
                dv_ref[keys, :] = value_part
                dk_ref[keys, :] = key_part
            else:
                dv_ref[keys, :] += value_part
                dk_ref[keys, :] += key_part
            query_grad = query_grad + dot(kt_ref[:, keys], score_grad, (1, 0))
        for head in range(GROUP):
            turned = query_grad[:, head * BLOCK : (head + 1) * BLOCK] * SCORE_SCALE
            back = unturn(turned, cos_ref[:, cols], sin_ref[:, cols])
            rows = slice(head * HS, (head + 1) * HS)
            lin, gain_part = head_norm_back(own_ref[rows, cols].astype(jnp.float32), qgain, back)
            qgrad_ref[rows, cols] = lin.astype(jnp.bfloat16)
            gain_total = gain_total + gain_part
    gain_ref[...] = gain_total
    for c in range(count):
        cols = slice(c * BLOCK, (c + 1) * BLOCK)
        for source, rows in ((dk_ref, slice(0, HS)), (dv_ref, slice(HS, 2 * HS))):
            kv_own_ref[rows, cols] = source[2 * c * BLOCK : (2 * c + 1) * BLOCK, :].T
            kv_other_ref[rows, cols] = source[(2 * c + 1) * BLOCK : (2 * c + 2) * BLOCK, :].T.astype(jnp.bfloat16)


def key_back_kernel(
    own_ref, kv_own_ref, kv_came_ref, cos_ref, sin_ref, kgain_ref, qgrad_ref, grad_ref, blocks_ref, gain_ref
):
    total = kv_own_ref[...] + kv_came_ref[...].astype(jnp.float32)
    back = unturn(total[:HS], cos_ref[...], sin_ref[...])
    key = own_ref[GROUP * HS : (GROUP + 1) * HS, :].astype(jnp.float32)
    lin, gain_part = head_norm_back(key, kgain_ref[...], back)
    grad_ref[: GROUP * HS, :] = qgrad_ref[...]
    grad_ref[GROUP * HS : (GROUP + 1) * HS, :] = lin.astype(jnp.bfloat16)
    grad_ref[(GROUP + 1) * HS :, :] = total[HS:].astype(jnp.bfloat16)
    for i in range(own_ref.shape[1] // BLOCK):
        blocks_ref[i] = grad_ref[:, i * BLOCK : (i + 1) * BLOCK]
    gain_ref[...] = jnp.sum(gain_part, axis=1, keepdims=True)


def call(kernel, outs, scratch, args, flops):
    smem = pl.BlockSpec(memory_space=pltpu.SMEM)
    vmem = pl.BlockSpec(memory_space=pltpu.VMEM)
    return pl.pallas_call(
        kernel,
        out_shape=[jax.ShapeDtypeStruct(shape, dtype) for shape, dtype in outs],
        in_specs=[smem if a.dtype == jnp.int32 else vmem for a in args],
        out_specs=[vmem for _ in outs],
        scratch_shapes=scratch,
        compiler_params=pltpu.CompilerParams(vmem_limit_bytes=40 * 1024 * 1024),
        cost_estimate=pl.CostEstimate(flops=flops, bytes_accessed=8 * 1024 * 1024, transcendentals=0),
    )(*args)


def rope_tables(positions):
    half = HS // 2
    freqs = ROPE_BASE ** (-jnp.arange(half, dtype=jnp.float32) * 2.0 / HS)
    angles = freqs[:, None] * positions[None, :].astype(jnp.float32)
    return jnp.cos(angles), jnp.sin(angles)


def on_device(
    inputs,
    norm_gain,
    w_query,
    w_key,
    w_value,
    w_out,
    query_gain,
    key_gain,
    ffn_gain,
    w_gate,
    w_up,
    w_down,
    cotangent,
):
    f32, bf16 = jnp.float32, jnp.bfloat16
    tokens = inputs[0]
    out_grad = cotangent[0]
    rows, width = tokens.shape
    chips = 2 * RING
    held = w_gate.shape[0]
    ffn = w_gate.shape[1] // chips
    seen = chips * rows
    hd = lax.axis_index("hd")
    tokens32 = tokens.astype(f32)

    by_chip = lambda w: w.reshape(held, chips, -1).transpose(1, 0, 2)
    joint_blocks = jnp.concatenate([by_chip(w_query), by_chip(w_key), by_chip(w_value)], axis=2)

    normed = rms_forward(tokens32, norm_gain).astype(bf16)
    normed_all = gather_blocks(normed).reshape(seen, width)
    w_joint_own = both_cores(exchange_blocks(joint_blocks), 1).reshape(width, -1)

    joint = dot(w_joint_own, normed_all, (0, 1)).astype(bf16)
    other_kv = partner(joint[GROUP * HS :])
    base = jnp.arange(seen, dtype=jnp.int32)
    base = base // BLOCK * (2 * BLOCK) + base % BLOCK
    cosine, sine = rope_tables(base + hd * BLOCK)
    cosine2, sine2 = rope_tables(base + (1 - hd) * BLOCK)
    hd_flag = jnp.reshape(hd, (1,)).astype(jnp.int32)
    qgain, kgain = query_gain[:, None], key_gain[:, None]
    heads_width = GROUP * HS
    att_blocks, att, att32, lse, q_rot, kt_rot, k_rot, v_nat = call(
        attend_kernel,
        [
            ((chips, heads_width, BLOCK), bf16),
            ((heads_width, seen), bf16),
            ((chips, HS, ROWS), f32),
            ((chips, ROWS), f32),
            ((chips, HS, ROWS), bf16),
            ((HS, 2 * seen), bf16),
            ((2 * seen, HS), bf16),
            ((2 * seen, HS), bf16),
        ],
        [pltpu.VMEM((2 * HS, 2 * seen), bf16)],
        (hd_flag, joint, other_kv, cosine, sine, cosine2, sine2, qgain, kgain),
        20_000_000_000,
    )
    attended = lax.all_to_all(att_blocks, "sq", split_axis=0, concat_axis=0, tiled=True)
    attended = attended.reshape(chips * heads_width, rows)

    w_out_all = lax.all_gather(after(w_out, normed_all), ("sq", "hd"), axis=0, tiled=True)
    grad_all = lax.all_gather(after(out_grad, w_out_all), "sq", axis=0, tiled=True)
    w_joint_rows = jnp.concatenate([w_query, w_key, w_value], axis=1)
    w_joint_all = lax.all_gather(after(w_joint_rows, grad_all), ("sq", "hd"), axis=0, tiled=True)

    gate_up_blocks = jnp.stack([by_chip(w_gate), by_chip(w_up)], axis=1)
    w_gate_up = both_cores(exchange_blocks(after(gate_up_blocks, normed_all)), 2)
    w_gate_own = w_gate_up[:, 0].reshape(width, ffn)
    w_up_own = w_gate_up[:, 1].reshape(width, ffn)
    w_down_own = both_cores(w_down, 0).reshape(ffn, width)

    middle = tokens32 + dot(attended, w_out_all, (0, 0))
    ffn_in = rms_forward(middle, ffn_gain).astype(bf16)
    ffn_all = gather_blocks(ffn_in).reshape(seen, width)
    hidden_grad = lax.optimization_barrier(dot(grad_all, w_down_own, (1, 1)))

    gate = dot(ffn_all, w_gate_own, (1, 0))
    up_val = dot(ffn_all, w_up_own, (1, 0))
    sigmoid = jax.nn.sigmoid(gate)
    hidden = (gate * sigmoid * up_val).astype(bf16)
    gate_grad = (hidden_grad * up_val * sigmoid * (1.0 + gate * (1.0 - sigmoid))).astype(bf16)
    up_grad = (hidden_grad * gate * sigmoid).astype(bf16)
    ffn_part = (dot(gate_grad, w_gate_own, (1, 1)) + dot(up_grad, w_up_own, (1, 1))).astype(bf16)
    ffn_in_grad = scatter_sum(ffn_part.reshape(chips, rows, width))

    out_part = dot(hidden, w_down_own, (1, 0)).astype(bf16)
    out_sum = lax.psum_scatter(out_part, "sq", scatter_dimension=0, tiled=True)
    output = (middle + out_sum.astype(f32)).astype(bf16)

    down_terms = dot(hidden, grad_all, (0, 0)).astype(bf16)
    down_sum = sum_cores(down_terms.reshape(2, ffn // 2, width), 0)
    gate_terms = dot(ffn_all, gate_grad, (0, 0)).astype(bf16).reshape(chips, 2, held, ffn)
    up_terms = dot(ffn_all, up_grad, (0, 0)).astype(bf16).reshape(chips, 2, held, ffn)
    gate_up_sum = sum_cores(jnp.stack([gate_terms, up_terms]), 2)
    down_half, quarter, few = ffn // 4, width // 4, held // 4
    down_pieces = down_sum.reshape(2, down_half, 4, quarter).transpose(0, 2, 1, 3)
    w_down_grad = sequence_gather(sequence_scatter(down_pieces.reshape(8, down_half, quarter)))
    w_down_grad = w_down_grad.reshape(2, 4, down_half, quarter).transpose(0, 2, 1, 3)
    w_down_grad = w_down_grad.reshape(ffn // 2, width).astype(f32)
    gate_up_pieces = gate_up_sum.reshape(2, chips, 4, few, ffn).transpose(0, 2, 1, 3, 4)
    gate_up_mine = sequence_scatter(gate_up_pieces.reshape(8, chips, few, ffn))
    gate_up_grad = sequence_gather(exchange_blocks(gate_up_mine))
    gate_up_grad = gate_up_grad.reshape(2, 4, chips, few, ffn).transpose(0, 1, 3, 2, 4)
    gate_up_grad = gate_up_grad.reshape(2, held, chips * ffn).astype(f32)

    middle_part, ffn_gain_part = rms_backward(middle, ffn_gain, ffn_in_grad)
    middle_grad = out_grad.astype(f32) + middle_part
    branch_grad = middle_grad.astype(bf16)
    att_grad = dot(w_out_all, branch_grad, (1, 1)).astype(bf16).reshape(chips, heads_width, rows)
    att_grad = lax.all_to_all(att_grad, "sq", split_axis=0, concat_axis=0, tiled=True)

    q_grad, kv_own, kv_other, qgain_part = call(
        attend_back_kernel,
        [
            ((heads_width, seen), bf16),
            ((2 * HS, seen), f32),
            ((2 * HS, seen), bf16),
            ((HS, BLOCK), f32),
        ],
        [pltpu.VMEM((2 * seen, HS), f32), pltpu.VMEM((2 * seen, HS), f32)],
        (hd_flag, joint, att_grad, cosine, sine, qgain, att32, lse, q_rot, kt_rot, k_rot, v_nat),
        40_000_000_000,
    )
    joint_grad, joint_grad_blocks, kgain_part = call(
        key_back_kernel,
        [(joint.shape, bf16), ((chips, joint.shape[0], BLOCK), bf16), ((HS, 1), f32)],
        [],
        (joint, kv_own, partner(kv_other), cosine, sine, kgain, q_grad),
        1_000_000_000,
    )
    came = lax.all_to_all(joint_grad_blocks, "sq", split_axis=0, concat_axis=0, tiled=True)
    key_at, value_at = heads_width, heads_width + HS
    came = jnp.concatenate(
        [
            came[:, :key_at].reshape(-1, rows),
            came[:, key_at:value_at].reshape(-1, rows),
            came[:, value_at:].reshape(-1, rows),
        ]
    )
    normed_grad = dot(came, w_joint_all, (0, 1))
    input_part, norm_gain_part = rms_backward(tokens32, norm_gain, normed_grad)
    input_grad = middle_grad + input_part

    branch_all = lax.all_gather(branch_grad, "sq", axis=0, tiled=True)
    out_terms = dot(att, branch_all, (1, 0)).astype(bf16)
    out_w_sum = sum_cores(out_terms.reshape(2, held, width), 0)
    out_pieces = out_w_sum.reshape(2, held // 2, 4, quarter).transpose(0, 2, 1, 3)
    w_out_grad = sequence_gather(sequence_scatter(out_pieces.reshape(8, held // 2, quarter)))
    w_out_grad = w_out_grad.reshape(2, 4, held // 2, quarter).transpose(0, 2, 1, 3)
    w_out_grad = w_out_grad.reshape(held, width).astype(f32)
    joint_terms = dot(normed_all, joint_grad, (0, 1)).astype(bf16).reshape(chips, 2, held, -1)
    joint_sum = sum_cores(joint_terms, 1)
    joint_pieces = joint_sum.reshape(chips, 8, held // 8, -1).transpose(1, 0, 2, 3)
    joint_mine = exchange_blocks(sequence_scatter(joint_pieces))
    w_joint_grad = sequence_gather(joint_mine)
    w_joint_grad = w_joint_grad.transpose(0, 2, 1, 3).reshape(held, chips, -1).astype(f32)

    gains = jnp.concatenate([norm_gain_part, ffn_gain_part, jnp.sum(qgain_part, axis=1), kgain_part[:, 0]])
    gains = sum_everywhere(gains.reshape(-1, BLOCK)).reshape(-1)
    return (
        output[None],
        input_grad[None],
        gains[:width],
        w_joint_grad[:, :, :key_at].reshape(held, -1),
        w_joint_grad[:, :, key_at:value_at].reshape(held, -1),
        w_joint_grad[:, :, value_at:].reshape(held, -1),
        w_out_grad,
        gains[2 * width : 2 * width + HS],
        gains[2 * width + HS :],
        gains[width : 2 * width],
        gate_up_grad[0],
        gate_up_grad[1],
        w_down_grad,
    )


def solution(mesh):
    return jax.shard_map(
        on_device,
        mesh=mesh,
        in_specs=(
            P("dp", ("sq", "hd"), None),
            P(),
            P(("sq", "hd"), None),
            P(("sq", "hd"), None),
            P(("sq", "hd"), None),
            P(("sq", "hd"), None),
            P(),
            P(),
            P(),
            P(("sq", "hd"), None),
            P(("sq", "hd"), None),
            P(("sq", "hd"), None),
            P("dp", ("sq", "hd"), None),
        ),
        out_specs=(
            P("dp", ("sq", "hd"), None),
            P("dp", ("sq", "hd"), None),
            P(),
            P(("sq", "hd"), None),
            P(("sq", "hd"), None),
            P(("sq", "hd"), None),
            P(("sq", "hd"), None),
            P(),
            P(),
            P(),
            P(("sq", "hd"), None),
            P(("sq", "hd"), None),
            P(("sq", "hd"), None),
        ),
        check_vma=False,
    )
```

```python
import jax
import jax.numpy as jnp
from jax import lax
from jax.experimental import pallas as pl
from jax.experimental.pallas import tpu as pltpu
from jax.sharding import Mesh, PartitionSpec as P

HQ = 24
HK = 8
HS = 64
GROUP = HQ // HK

EPSILON = 1e-05
ROPE_BASE = 1000000.0
SCORE_SCALE = 0.125

TEAM = ("hd", "y")
RING = 4
STEPS = (2, 1, 3)
BLOCK = 128
WIDE = 2 * BLOCK
ROWS = GROUP * WIDE


def rms_forward(values, gain):
    factor = lax.rsqrt(jnp.mean(values * values, axis=-1, keepdims=True) + EPSILON)
    return values * factor * gain


def rms_backward(values, gain, grad_out):
    factor = lax.rsqrt(jnp.mean(values * values, axis=-1, keepdims=True) + EPSILON)
    normal = values * factor
    scaled = grad_out * gain
    grad_in = factor * (scaled - normal * jnp.mean(scaled * normal, axis=-1, keepdims=True))
    grad_gain = jnp.sum(grad_out * normal, axis=0)
    return (grad_in, grad_gain)


def dot(left, right, contract):
    return lax.dot_general(
        left, right, (((contract[0],), (contract[1],)), ((), ())), preferred_element_type=jnp.float32
    )


def at(array, index, axis=0):
    return lax.dynamic_index_in_dim(array, index, axis, keepdims=False)


def put(whole, array, *index):
    lead = (1,) * len(index)
    return lax.dynamic_update_slice(whole, array.reshape(lead + array.shape), index + (0,) * array.ndim)


def fence(*values):
    return lax.optimization_barrier(values)


def ring(array, axis, step):
    return lax.ppermute(array, axis, [(i, (i + step) % RING) for i in range(RING)])


def ring_z(array, step):
    return ring(array, ("zh", "zl"), step)


def swap(array, axis):
    return lax.ppermute(array, axis, [(0, 1), (1, 0)])


def in_order(mine, other, axis_name, axis):
    first = lax.axis_index(axis_name) == 0
    return jnp.stack([jnp.where(first, mine, other), jnp.where(first, other, mine)], axis=axis)


def gather_tokens(block):
    y, hd = lax.axis_index("y"), lax.axis_index("hd")
    whole = jnp.zeros((RING, 2, *block.shape), block.dtype)
    blocks = [(y, block)] + [((y - step) % RING, ring(block, "y", step)) for step in STEPS]
    for source, came in blocks:
        whole = put(whole, came, source, hd)
        whole = put(whole, swap(came, "hd"), source, 1 - hd)
    return whole.reshape(-1, block.shape[-1])


def scatter_tokens(parts):
    y, hd = lax.axis_index("y"), lax.axis_index("hd")
    parts = parts.reshape(RING, 2, BLOCK, -1)
    chip = at(parts, hd, 1).astype(jnp.float32) + swap(at(parts, 1 - hd, 1), "hd").astype(jnp.float32)
    chip = chip.astype(jnp.bfloat16)
    arrived = [ring(at(chip, (y + step) % RING), "y", step) for step in STEPS]
    return sum((came.astype(jnp.float32) for came in arrived), at(chip, y).astype(jnp.float32))


def exchange_large(blocks):
    y, hd = lax.axis_index("y"), lax.axis_index("hd")
    came = jnp.zeros((RING, 2, *blocks.shape[2:]), blocks.dtype)
    came = put(came, at(blocks, y, 1), y)
    for step in STEPS:
        came = put(came, ring(at(blocks, (y + step) % RING, 1), "y", step), (y - step) % RING)
    return in_order(at(came, hd, 1), swap(at(came, 1 - hd, 1), "hd"), "hd", 0)


def exchange(blocks):
    return lax.all_to_all(blocks, TEAM, split_axis=0, concat_axis=0, tiled=True)


def whole_rows(blocks):
    other = jnp.stack([ring_z(blocks[0], 1), ring_z(blocks[1], 3)], axis=1)
    return in_order(blocks.swapaxes(0, 1), other, "zl", 0)


def sum_ring(pieces, index, move):
    arrived = [move(at(pieces, (index + step) % RING), step) for step in STEPS]
    total = sum((came.astype(jnp.float32) for came in arrived), at(pieces, index).astype(jnp.float32))
    return total.astype(jnp.bfloat16)


def sum_x(pieces):
    return sum_ring(pieces, lax.axis_index("x"), lambda a, step: ring(a, "x", step))


def sum_z(pieces):
    z = lax.axis_index("zh") * 2 + lax.axis_index("zl")
    return sum_ring(pieces, z, ring_z)


def spread(piece):
    x = lax.axis_index("x")
    pair = in_order(piece, swap(piece, "zh"), "zh", 0)
    whole = put(jnp.zeros((RING, *pair.shape), pair.dtype), pair, x)
    for step in STEPS:
        whole = put(whole, ring(pair, "x", step), (x - step) % RING)
    return whole


def sum_everywhere(terms):
    for axis, count in (("hd", 2), ("y", 4), ("zl", 2), ("zh", 2), ("x", 4)):
        step = 1
        while step < count:
            terms = terms + lax.ppermute(terms, axis, [(i, i ^ step) for i in range(count)])
            step *= 2
    return terms


def turn(values, cosine, sine):
    first, second = values[: HS // 2], values[HS // 2 :]
    return jnp.concatenate([first * cosine - second * sine, second * cosine + first * sine], axis=0)


def unturn(grads, cosine, sine):
    first, second = grads[: HS // 2], grads[HS // 2 :]
    return jnp.concatenate([first * cosine + second * sine, second * cosine - first * sine], axis=0)


def head_norm(values, gain):
    return values * lax.rsqrt(jnp.mean(values * values, axis=0, keepdims=True) + EPSILON) * gain


def head_norm_back(values, gain, grad_out):
    factor = lax.rsqrt(jnp.mean(values * values, axis=0, keepdims=True) + EPSILON)
    normal = values * factor
    scaled = grad_out * gain
    grad_in = factor * (scaled - normal * jnp.mean(scaled * normal, axis=0, keepdims=True))
    return grad_in, grad_out * normal


def allowed_keys():
    key = lax.broadcasted_iota(jnp.int32, (WIDE, ROWS), 0)
    query = lax.broadcasted_iota(jnp.int32, (WIDE, ROWS), 1) % WIDE
    return key <= query


def member(block):
    return block % 2 * RING + block // 2


def attend_kernel(
    half_ref, own_ref, other_ref, cos_ref, sin_ref, cos2_ref, sin2_ref, qgain_ref, kgain_ref,
    blocks_ref, att_ref, out_ref, lse_ref, q_ref, kt_ref, k_ref, v_ref, vt_ref, total_ref,
):
    seen = own_ref.shape[1]
    count = seen // WIDE
    qgain, kgain = qgain_ref[...], kgain_ref[...]
    vt_ref[HS:, :] = jnp.ones((HS, vt_ref.shape[1]), jnp.bfloat16)
    for c in range(count):
        cols = slice(c * WIDE, (c + 1) * WIDE)
        sides = (
            (own_ref[GROUP * HS :, cols], cos_ref[:, cols], sin_ref[:, cols]),
            (other_ref[:, cols], cos2_ref[:, cols], sin2_ref[:, cols]),
        )
        for side, (pair, cosine, sine) in enumerate(sides):
            pair = pair.astype(jnp.float32)
            place = slice(side * seen + c * WIDE, side * seen + (c + 1) * WIDE)
            key = turn(head_norm(pair[:HS], kgain), cosine, sine)
            kt_ref[:, place] = key.astype(jnp.bfloat16)
            k_ref[place, :] = key.T.astype(jnp.bfloat16)
            vt_ref[:HS, place] = pair[HS:].astype(jnp.bfloat16)
            v_ref[place, :] = pair[HS:].T.astype(jnp.bfloat16)
        for head in range(GROUP):
            query = own_ref[head * HS : (head + 1) * HS, cols].astype(jnp.float32)
            query = turn(head_norm(query, qgain), cos_ref[:, cols], sin_ref[:, cols])
            q_ref[c, :, head * WIDE : (head + 1) * WIDE] = (query * SCORE_SCALE).astype(jnp.bfloat16)
    allowed = allowed_keys()

    def terms(i, start, masked):
        keys = slice(start, start + WIDE)
        weights = jnp.exp(dot(k_ref[keys, :], q_ref[i], (1, 0)))
        if masked:
            weights = jnp.where(allowed, weights, 0.0)
        return dot(vt_ref[:, keys], weights.astype(jnp.bfloat16), (1, 0))

    for i in range(count):
        total_ref[i] = sum(terms(i, c * WIDE, c == i) for c in range(i + 1))

    @pl.when(half_ref[0] == 1)
    def _():
        for i in range(count):
            total_ref[i] += sum(terms(i, seen + c * WIDE, False) for c in range(count))

    for i in range(count):
        total = total_ref[i]
        norm = total[HS : HS + 1]
        result = total[:HS] / norm
        lse_ref[i : i + 1, :] = jnp.log(norm)
        out_ref[i] = result
        for head in range(GROUP):
            part = result[:, head * WIDE : (head + 1) * WIDE].astype(jnp.bfloat16)
            att_ref[head * HS : (head + 1) * HS, i * WIDE : (i + 1) * WIDE] = part
            for side in range(2):
                blocks_ref[member(2 * i + side), head * HS : (head + 1) * HS, :] = part[
                    :, side * BLOCK : (side + 1) * BLOCK
                ]


def attend_back_kernel(
    half_ref, own_ref, grad_ref, cos_ref, sin_ref, qgain_ref, out_ref, lse_ref, q_ref, kt_ref, k_ref, v_ref,
    qgrad_ref, kv_own_ref, kv_other_ref, gain_ref, dk_ref, dv_ref, dq_ref, g_ref, delta_ref,
):
    seen = own_ref.shape[1]
    count = seen // WIDE
    qgain = qgain_ref[...]
    allowed = allowed_keys()

    def terms(i, start, masked):
        keys = slice(start, start + WIDE)
        query, grad = q_ref[i], g_ref[i]
        weights = jnp.exp(dot(k_ref[keys, :], query, (1, 0)) - lse_ref[i : i + 1, :])
        if masked:
            weights = jnp.where(allowed, weights, 0.0)
        prob_grad = dot(v_ref[keys, :], grad, (1, 0))
        score_grad = (weights * (prob_grad - delta_ref[i : i + 1, :])).astype(jnp.bfloat16)
        dv_ref[keys, :] += dot(weights.astype(jnp.bfloat16), grad, (1, 1))
        dk_ref[keys, :] += dot(score_grad, query, (1, 1))
        return dot(kt_ref[:, keys], score_grad, (1, 0))

    dk_ref[...] = jnp.zeros_like(dk_ref)
    dv_ref[...] = jnp.zeros_like(dv_ref)
    for i in range(count):
        for head in range(GROUP):
            for side in range(2):
                place = slice(head * WIDE + side * BLOCK, head * WIDE + (side + 1) * BLOCK)
                g_ref[i, :, place] = grad_ref[member(2 * i + side), head * HS : (head + 1) * HS, :]
        delta_ref[i : i + 1, :] = jnp.sum(g_ref[i].astype(jnp.float32) * out_ref[i], axis=0, keepdims=True)
        dq_ref[i] = sum(terms(i, c * WIDE, c == i) for c in range(i + 1))

    @pl.when(half_ref[0] == 1)
    def _():
        for i in range(count):
            dq_ref[i] += sum(terms(i, seen + c * WIDE, False) for c in range(count))

    gain_total = jnp.zeros((HS, WIDE), jnp.float32)
    for i in range(count):
        cols = slice(i * WIDE, (i + 1) * WIDE)
        for head in range(GROUP):
            turned = dq_ref[i, :, head * WIDE : (head + 1) * WIDE] * SCORE_SCALE
            back = unturn(turned, cos_ref[:, cols], sin_ref[:, cols])
            rows = slice(head * HS, (head + 1) * HS)
            lin, gain_part = head_norm_back(own_ref[rows, cols].astype(jnp.float32), qgain, back)
            qgrad_ref[rows, cols] = lin.astype(jnp.bfloat16)
            gain_total = gain_total + gain_part
        for source, rows in ((dk_ref, slice(0, HS)), (dv_ref, slice(HS, 2 * HS))):
            kv_own_ref[rows, cols] = source[i * WIDE : (i + 1) * WIDE, :].T
            kv_other_ref[rows, cols] = source[seen + i * WIDE : seen + (i + 1) * WIDE, :].T.astype(jnp.bfloat16)
    gain_ref[...] = gain_total


def key_back_kernel(
    own_ref, kv_own_ref, kv_came_ref, cos_ref, sin_ref, kgain_ref, qgrad_ref, grad_ref, blocks_ref, gain_ref
):
    total = kv_own_ref[...] + kv_came_ref[...].astype(jnp.float32)
    back = unturn(total[:HS], cos_ref[...], sin_ref[...])
    key = own_ref[GROUP * HS : (GROUP + 1) * HS, :].astype(jnp.float32)
    lin, gain_part = head_norm_back(key, kgain_ref[...], back)
    grad_ref[: GROUP * HS, :] = qgrad_ref[...]
    grad_ref[GROUP * HS : (GROUP + 1) * HS, :] = lin.astype(jnp.bfloat16)
    grad_ref[(GROUP + 1) * HS :, :] = total[HS:].astype(jnp.bfloat16)
    for i in range(own_ref.shape[1] // BLOCK):
        blocks_ref[member(i)] = grad_ref[:, i * BLOCK : (i + 1) * BLOCK]
    gain_ref[...] = jnp.sum(gain_part, axis=1, keepdims=True)


def call(kernel, outs, scratch, args, flops):
    smem = pl.BlockSpec(memory_space=pltpu.SMEM)
    vmem = pl.BlockSpec(memory_space=pltpu.VMEM)
    return pl.pallas_call(
        kernel,
        out_shape=[jax.ShapeDtypeStruct(shape, dtype) for shape, dtype in outs],
        in_specs=[smem if a.dtype == jnp.int32 else vmem for a in args],
        out_specs=[vmem for _ in outs],
        scratch_shapes=scratch,
        compiler_params=pltpu.CompilerParams(vmem_limit_bytes=40 * 1024 * 1024),
        cost_estimate=pl.CostEstimate(flops=flops, bytes_accessed=8 * 1024 * 1024, transcendentals=0),
    )(*args)


def rope_tables(positions):
    half = HS // 2
    freqs = ROPE_BASE ** (-jnp.arange(half, dtype=jnp.float32) * 2.0 / HS)
    angles = freqs[:, None] * positions[None, :].astype(jnp.float32)
    return jnp.cos(angles), jnp.sin(angles)


def on_device(
    inputs,
    norm_gain,
    w_query,
    w_key,
    w_value,
    w_out,
    query_gain,
    key_gain,
    ffn_gain,
    w_gate,
    w_up,
    w_down,
    cotangent,
):
    f32, bf16 = jnp.float32, jnp.bfloat16
    tokens = inputs[0]
    out_grad = cotangent[0]
    rows, width = tokens.shape
    held = w_gate.shape[0]
    half_ffn = w_down.shape[0]
    ffn = 2 * half_ffn
    team = 2 * RING
    seen = team * rows
    quarter, few = width // 4, held // 4
    heads_width = GROUP * HS
    key_at, value_at = heads_width, heads_width + HS
    zl, hd = lax.axis_index("zl"), lax.axis_index("hd")
    tokens32 = tokens.astype(f32)

    normed = rms_forward(tokens32, norm_gain).astype(bf16)
    normed_all = gather_tokens(normed)

    by_head = lambda w: w.reshape(held, team, -1).transpose(1, 0, 2)
    joint_blocks = jnp.concatenate([by_head(w_query), by_head(w_key), by_head(w_value)], axis=2)
    w_joint = exchange(joint_blocks).reshape(2, RING, held, -1)
    w_joint = whole_rows(w_joint).reshape(width, -1)
    by_team = lambda w: w.reshape(held, 2, RING, 2, half_ffn).transpose(3, 2, 0, 1, 4).reshape(2, RING, held, ffn)
    gate_up_blocks = jnp.concatenate([by_team(w_gate), by_team(w_up)], axis=2)
    w_gate_up = whole_rows(exchange_large(gate_up_blocks))
    w_gate_own = w_gate_up[:, :, :, :held].reshape(width, ffn)
    w_up_own = w_gate_up[:, :, :, held:].reshape(width, ffn)
    down_other = jnp.concatenate([ring_z(w_down[: half_ffn // 2], 1), ring_z(w_down[half_ffn // 2 :], 3)])
    w_down_own = in_order(w_down, down_other, "zl", 0).reshape(ffn, width)

    w_out_all = lax.all_gather(w_out, ("zl", "y", "hd"), axis=0, tiled=True)
    grad_in, _ = fence(out_grad, w_out_all)
    grad_all = lax.all_gather(grad_in, ("y", "hd"), axis=0, tiled=True)

    joint = dot(w_joint, normed_all, (0, 1)).astype(bf16)
    other_kv = swap(joint[heads_width:], "zl")
    base = jnp.arange(seen, dtype=jnp.int32)
    cosine, sine = rope_tables(base + zl * seen)
    cosine2, sine2 = rope_tables(base + (1 - zl) * seen)
    half_flag = jnp.reshape(zl, (1,)).astype(jnp.int32)
    qgain, kgain = query_gain[:, None], key_gain[:, None]
    wide = seen // WIDE
    att_blocks, att, att32, lse, q_rot, kt_rot, k_rot, v_nat = call(
        attend_kernel,
        [
            ((team, heads_width, BLOCK), bf16),
            ((heads_width, seen), bf16),
            ((wide, HS, ROWS), f32),
            ((wide, ROWS), f32),
            ((wide, HS, ROWS), bf16),
            ((HS, 2 * seen), bf16),
            ((2 * seen, HS), bf16),
            ((2 * seen, HS), bf16),
        ],
        [pltpu.VMEM((2 * HS, 2 * seen), bf16), pltpu.VMEM((wide, 2 * HS, ROWS), f32)],
        (half_flag, joint, other_kv, cosine, sine, cosine2, sine2, qgain, kgain),
        10_000_000_000,
    )
    attended = exchange(att_blocks).reshape(team * heads_width, rows)

    middle = tokens32 + dot(attended, w_out_all, (0, 0))
    ffn_in = rms_forward(middle, ffn_gain).astype(bf16)
    ffn_all = gather_tokens(ffn_in)
    hidden_grad = lax.optimization_barrier(dot(grad_all, w_down_own, (1, 1)))
    w_joint_rows, _ = fence(jnp.concatenate([w_query, w_key, w_value], axis=1), ffn_all)
    w_joint_all = lax.all_gather(w_joint_rows, ("zl", "y", "hd"), axis=0, tiled=True)

    gate = dot(ffn_all, w_gate_own, (1, 0))
    up_val = dot(ffn_all, w_up_own, (1, 0))
    sigmoid = jax.nn.sigmoid(gate)
    hidden = (gate * sigmoid * up_val).astype(bf16)
    gate_grad = (hidden_grad * up_val * sigmoid * (1.0 + gate * (1.0 - sigmoid))).astype(bf16)
    up_grad = (hidden_grad * gate * sigmoid).astype(bf16)
    ffn_part = (dot(gate_grad, w_gate_own, (1, 1)) + dot(up_grad, w_up_own, (1, 1))).astype(bf16)
    ffn_in_grad = scatter_tokens(ffn_part)

    down_terms = dot(hidden, grad_all, (0, 0)).astype(bf16)
    down_pieces = down_terms.reshape(2, 2, half_ffn // 2, 4, quarter).transpose(1, 0, 3, 2, 4)
    down_pieces = sum_z(down_pieces.reshape(4, 4, half_ffn // 2, quarter))
    by_piece = lambda g: g.astype(bf16).reshape(2, RING, 2, 4, few, ffn).transpose(3, 0, 2, 1, 4, 5)
    gate_up_pieces = jnp.stack(
        [by_piece(dot(ffn_all, gate_grad, (0, 0))), by_piece(dot(ffn_all, up_grad, (0, 0)))], axis=1
    )
    gate_up_pieces = sum_x(gate_up_pieces)

    out_part = dot(hidden, w_down_own, (1, 0)).astype(bf16)
    out_sum = lax.psum_scatter(out_part, ("y", "hd"), scatter_dimension=0, tiled=True)
    output = (middle + out_sum.astype(f32)).astype(bf16)

    middle_part, ffn_gain_part = rms_backward(middle, ffn_gain, ffn_in_grad)
    middle_grad = out_grad.astype(f32) + middle_part
    branch_grad = middle_grad.astype(bf16)
    att_grad = dot(w_out_all, branch_grad, (1, 1)).astype(bf16).reshape(team, heads_width, rows)
    att_grad, down_pieces = fence(exchange(att_grad), down_pieces)

    q_grad, kv_own, kv_other, qgain_part = call(
        attend_back_kernel,
        [
            ((heads_width, seen), bf16),
            ((2 * HS, seen), f32),
            ((2 * HS, seen), bf16),
            ((HS, WIDE), f32),
        ],
        [
            pltpu.VMEM((2 * seen, HS), f32),
            pltpu.VMEM((2 * seen, HS), f32),
            pltpu.VMEM((wide, HS, ROWS), f32),
            pltpu.VMEM((wide, HS, ROWS), bf16),
            pltpu.VMEM((2 * wide, ROWS), f32),
        ],
        (half_flag, joint, att_grad, cosine, sine, qgain, att32, lse, q_rot, kt_rot, k_rot, v_nat),
        20_000_000_000,
    )
    down_pieces = sum_x(down_pieces)
    kv_came, gate_up_pieces, down_pieces = fence(swap(kv_other, "zl"), gate_up_pieces, down_pieces)
    joint_grad, joint_grad_blocks, kgain_part = call(
        key_back_kernel,
        [(joint.shape, bf16), ((team, joint.shape[0], BLOCK), bf16), ((HS, 1), f32)],
        [],
        (joint, kv_own, kv_came, cosine, sine, kgain, q_grad),
        1_000_000_000,
    )
    gate_up_mine = sum_z(gate_up_pieces.reshape(4, 2, RING, few, ffn))
    came = exchange(joint_grad_blocks)
    came = jnp.concatenate(
        [
            came[:, :key_at].reshape(-1, rows),
            came[:, key_at:value_at].reshape(-1, rows),
            came[:, value_at:].reshape(-1, rows),
        ]
    )
    came, gate_up_mine = fence(came, gate_up_mine)
    gate_up_mine = exchange(gate_up_mine.reshape(team, few, ffn))
    normed_grad = dot(came, w_joint_all, (0, 1))
    input_part, norm_gain_part = rms_backward(tokens32, norm_gain, normed_grad)
    input_grad = middle_grad + input_part

    branch_all = lax.all_gather(branch_grad, ("y", "hd"), axis=0, tiled=True)
    out_terms = dot(att, branch_all, (1, 0)).astype(bf16).reshape(2, held, width)
    out_terms = in_order(at(out_terms, hd), swap(at(out_terms, 1 - hd), "hd"), "hd", 0)
    out_pieces = out_terms.reshape(2, 2, held // 2, 4, quarter).transpose(3, 1, 0, 2, 4)
    out_mine = sum_z(sum_x(out_pieces).reshape(4, held // 2, quarter))
    joint_terms = dot(normed_all, joint_grad, (0, 1)).astype(bf16)
    joint_pieces = joint_terms.reshape(2, RING, 2, 4, 2, held // 8, -1).transpose(3, 4, 0, 2, 1, 5, 6)
    joint_mine = sum_z(sum_x(joint_pieces).reshape(4, team, held // 8, -1))
    joint_mine = exchange(joint_mine)

    w_down_grad = spread(down_pieces).transpose(1, 2, 0, 3).reshape(half_ffn, width).astype(f32)
    w_out_grad = spread(out_mine).transpose(1, 2, 0, 3).reshape(held, width).astype(f32)
    gate_up_grad = spread(gate_up_mine).reshape(4, 2, 2, RING, few, 2, half_ffn)
    gate_up_grad = gate_up_grad.transpose(1, 0, 4, 5, 3, 2, 6).reshape(2, held, -1).astype(f32)
    w_joint_grad = spread(joint_mine).reshape(team, team, held // 8, -1)
    w_joint_grad = w_joint_grad.transpose(0, 2, 1, 3).reshape(held, team, -1).astype(f32)

    gains = jnp.concatenate([norm_gain_part, ffn_gain_part, jnp.sum(qgain_part, axis=1), kgain_part[:, 0]])
    gains = sum_everywhere(gains.reshape(-1, BLOCK)).reshape(-1)
    return (
        output[None],
        input_grad[None],
        gains[:width],
        w_joint_grad[:, :, :key_at].reshape(held, -1),
        w_joint_grad[:, :, key_at:value_at].reshape(held, -1),
        w_joint_grad[:, :, value_at:].reshape(held, -1),
        w_out_grad,
        gains[2 * width : 2 * width + HS],
        gains[2 * width + HS :],
        gains[width : 2 * width],
        gate_up_grad[0],
        gate_up_grad[1],
        w_down_grad,
    )


def solution(mesh):
    fine = Mesh(mesh.devices.reshape(4, 2, 2, 4, 2), ("x", "zh", "zl", "y", "hd"))
    by_tokens = P(("x", "zh"), ("zl", "y", "hd"), None)
    by_rows = P(("zl", "y", "hd"), None)
    return jax.shard_map(
        on_device,
        mesh=fine,
        in_specs=(
            by_tokens, P(), by_rows, by_rows, by_rows, by_rows, P(), P(), P(), by_rows, by_rows, by_rows, by_tokens
        ),
        out_specs=(
            by_tokens, by_tokens, P(), by_rows, by_rows, by_rows, by_rows, P(), P(), P(), by_rows, by_rows, by_rows
        ),
        check_vma=False,
    )
```

```python
import jax
import jax.numpy as jnp
from jax import lax
from jax.experimental import pallas as pl
from jax.experimental.pallas import tpu as pltpu
from jax.sharding import Mesh, PartitionSpec as P

HQ = 24
HK = 8
HS = 64
GROUP = HQ // HK

EPSILON = 1e-05
ROPE_BASE = 1000000.0
SCORE_SCALE = 0.125

RING = 4
STEPS = (2, 1, 3)
BLOCK = 128
WIDE = 2 * BLOCK
ROWS = GROUP * WIDE


def rms_forward(values, gain):
    factor = lax.rsqrt(jnp.mean(values * values, axis=-1, keepdims=True) + EPSILON)
    return values * factor * gain


def rms_backward(values, gain, grad_out):
    factor = lax.rsqrt(jnp.mean(values * values, axis=-1, keepdims=True) + EPSILON)
    normal = values * factor
    scaled = grad_out * gain
    grad_in = factor * (scaled - normal * jnp.mean(scaled * normal, axis=-1, keepdims=True))
    grad_gain = jnp.sum(grad_out * normal, axis=0)
    return (grad_in, grad_gain)


def dot(left, right, contract):
    return lax.dot_general(
        left, right, (((contract[0],), (contract[1],)), ((), ())), preferred_element_type=jnp.float32
    )


SUMMED = ("x", "zh", "zl")
TEAM = ("y", "hd")


def at(array, index, axis=0):
    return lax.dynamic_index_in_dim(array, index, axis, keepdims=False)


def put(whole, array, *index):
    lead = (1,) * len(index)
    return lax.dynamic_update_slice(whole, array.reshape(lead + array.shape), index + (0,) * array.ndim)


def fence(*values):
    return lax.optimization_barrier(values)


def ring(array, axis, step):
    return lax.ppermute(array, axis, [(i, (i + step) % RING) for i in range(RING)])


def ring_z(array, step):
    return ring(array, ("zh", "zl"), step)


def swap(array, axis):
    return lax.ppermute(array, axis, [(0, 1), (1, 0)])


def in_order(mine, other, axis_name, axis):
    first = lax.axis_index(axis_name) == 0
    return jnp.stack([jnp.where(first, mine, other), jnp.where(first, other, mine)], axis=axis)


def gather_column(block):
    y = lax.axis_index("y")
    column = put(jnp.zeros((RING, *block.shape), block.dtype), block, y)
    for step in STEPS:
        column = put(column, ring(block, "y", step), (y - step) % RING)
    return column


def both_columns(column):
    return in_order(column, swap(column, "hd"), "hd", 1).reshape(-1, column.shape[-1])


def chip_sum(parts):
    hd = lax.axis_index("hd")
    parts = parts.reshape(RING, 2, BLOCK, -1)
    total = at(parts, hd, 1).astype(jnp.float32) + swap(at(parts, 1 - hd, 1), "hd").astype(jnp.float32)
    return total.astype(jnp.bfloat16)


def column_sum(chip):
    y = lax.axis_index("y")
    arrived = [ring(at(chip, (y + step) % RING), "y", step) for step in STEPS]
    return sum((came.astype(jnp.float32) for came in arrived), at(chip, y).astype(jnp.float32))


def exchange(blocks, axes):
    return lax.all_to_all(blocks, axes, split_axis=0, concat_axis=0, tiled=True)


def sum_x(pieces):
    x = lax.axis_index("x")
    arrived = [ring(at(pieces, (x + step) % RING), "x", step) for step in STEPS]
    return sum_first([at(pieces, x), *arrived])


def sum_first(arrived):
    return sum(arrived[i].astype(jnp.float32) for i in range(len(arrived))).astype(jnp.bfloat16)


def spread(piece):
    x = lax.axis_index("x")
    pair = in_order(piece, swap(piece, "zh"), "zh", 0)
    whole = put(jnp.zeros((RING, *pair.shape), pair.dtype), pair, x)
    for step in STEPS:
        whole = put(whole, ring(pair, "x", step), (x - step) % RING)
    return whole


def sum_everywhere(terms):
    terms = terms + swap(terms, "hd")
    for axis in ("y", ("zh", "zl"), "x"):
        far, after, before = [ring(terms, axis, step) for step in STEPS]
        terms = (terms + far) + (after + before)
    return terms


def turn(values, cosine, sine):
    first, second = values[: HS // 2], values[HS // 2 :]
    return jnp.concatenate([first * cosine - second * sine, second * cosine + first * sine], axis=0)


def unturn(grads, cosine, sine):
    first, second = grads[: HS // 2], grads[HS // 2 :]
    return jnp.concatenate([first * cosine + second * sine, second * cosine - first * sine], axis=0)


def head_norm(values, gain):
    return values * lax.rsqrt(jnp.mean(values * values, axis=0, keepdims=True) + EPSILON) * gain


def head_norm_back(values, gain, grad_out):
    factor = lax.rsqrt(jnp.mean(values * values, axis=0, keepdims=True) + EPSILON)
    normal = values * factor
    scaled = grad_out * gain
    grad_in = factor * (scaled - normal * jnp.mean(scaled * normal, axis=0, keepdims=True))
    return grad_in, grad_out * normal


def allowed_keys():
    key = lax.broadcasted_iota(jnp.int32, (WIDE, ROWS), 0)
    query = lax.broadcasted_iota(jnp.int32, (WIDE, ROWS), 1) % WIDE
    return key <= query


def place_of(head):
    return head % RING * 2 + head // RING


def attend_kernel(
    half_ref, own_ref, other_ref, cos_ref, sin_ref, cos2_ref, sin2_ref, qgain_ref, kgain_ref,
    att_ref, out_ref, lse_ref, q_ref, kt_ref, k_ref, v_ref, vt_ref, total_ref,
):
    seen = own_ref.shape[1]
    count = seen // WIDE
    qgain, kgain = qgain_ref[...], kgain_ref[...]
    vt_ref[HS:, :] = jnp.ones((HS, vt_ref.shape[1]), jnp.bfloat16)
    for c in range(count):
        cols = slice(c * WIDE, (c + 1) * WIDE)
        sides = (
            (own_ref[GROUP * HS :, cols], cos_ref[:, cols], sin_ref[:, cols]),
            (other_ref[:, cols], cos2_ref[:, cols], sin2_ref[:, cols]),
        )
        for side, (pair, cosine, sine) in enumerate(sides):
            pair = pair.astype(jnp.float32)
            place = slice(side * seen + c * WIDE, side * seen + (c + 1) * WIDE)
            key = turn(head_norm(pair[:HS], kgain), cosine, sine)
            kt_ref[:, place] = key.astype(jnp.bfloat16)
            k_ref[place, :] = key.T.astype(jnp.bfloat16)
            vt_ref[:HS, place] = pair[HS:].astype(jnp.bfloat16)
            v_ref[place, :] = pair[HS:].T.astype(jnp.bfloat16)
        for head in range(GROUP):
            query = own_ref[head * HS : (head + 1) * HS, cols].astype(jnp.float32)
            query = turn(head_norm(query, qgain), cos_ref[:, cols], sin_ref[:, cols])
            q_ref[c, :, head * WIDE : (head + 1) * WIDE] = (query * SCORE_SCALE).astype(jnp.bfloat16)
    allowed = allowed_keys()

    def terms(i, start, masked):
        keys = slice(start, start + WIDE)
        weights = jnp.exp(dot(k_ref[keys, :], q_ref[i], (1, 0)))
        if masked:
            weights = jnp.where(allowed, weights, 0.0)
        return dot(vt_ref[:, keys], weights.astype(jnp.bfloat16), (1, 0))

    for i in range(count):
        total_ref[i] = sum(terms(i, c * WIDE, c == i) for c in range(i + 1))

    @pl.when(half_ref[0] == 1)
    def _():
        for i in range(count):
            total_ref[i] += sum(terms(i, seen + c * WIDE, False) for c in range(count))

    for i in range(count):
        total = total_ref[i]
        norm = total[HS : HS + 1]
        result = total[:HS] / norm
        lse_ref[i : i + 1, :] = jnp.log(norm)
        out_ref[i] = result
        for head in range(GROUP):
            part = result[:, head * WIDE : (head + 1) * WIDE].astype(jnp.bfloat16)
            att_ref[head * HS : (head + 1) * HS, i * WIDE : (i + 1) * WIDE] = part


def attend_back_kernel(
    half_ref, own_ref, grad_ref, cos_ref, sin_ref, qgain_ref, out_ref, lse_ref, q_ref, kt_ref, k_ref, v_ref,
    qgrad_ref, kv_own_ref, kv_other_ref, gain_ref, dk_ref, dv_ref, dq_ref, g_ref, delta_ref,
):
    seen = own_ref.shape[1]
    count = seen // WIDE
    qgain = qgain_ref[...]
    allowed = allowed_keys()

    def terms(i, start, masked):
        keys = slice(start, start + WIDE)
        query, grad = q_ref[i], g_ref[i]
        weights = jnp.exp(dot(k_ref[keys, :], query, (1, 0)) - lse_ref[i : i + 1, :])
        if masked:
            weights = jnp.where(allowed, weights, 0.0)
        prob_grad = dot(v_ref[keys, :], grad, (1, 0))
        score_grad = (weights * (prob_grad - delta_ref[i : i + 1, :])).astype(jnp.bfloat16)
        dv_ref[keys, :] += dot(weights.astype(jnp.bfloat16), grad, (1, 1))
        dk_ref[keys, :] += dot(score_grad, query, (1, 1))
        return dot(kt_ref[:, keys], score_grad, (1, 0))

    dk_ref[...] = jnp.zeros_like(dk_ref)
    dv_ref[...] = jnp.zeros_like(dv_ref)
    for i in range(count):
        for head in range(GROUP):
            g_ref[i, :, head * WIDE : (head + 1) * WIDE] = grad_ref[
                head * HS : (head + 1) * HS, i * WIDE : (i + 1) * WIDE
            ]
        delta_ref[i : i + 1, :] = jnp.sum(g_ref[i].astype(jnp.float32) * out_ref[i], axis=0, keepdims=True)
        dq_ref[i] = sum(terms(i, c * WIDE, c == i) for c in range(i + 1))

    @pl.when(half_ref[0] == 1)
    def _():
        for i in range(count):
            dq_ref[i] += sum(terms(i, seen + c * WIDE, False) for c in range(count))

    gain_total = jnp.zeros((HS, WIDE), jnp.float32)
    for i in range(count):
        cols = slice(i * WIDE, (i + 1) * WIDE)
        for head in range(GROUP):
            turned = dq_ref[i, :, head * WIDE : (head + 1) * WIDE] * SCORE_SCALE
            back = unturn(turned, cos_ref[:, cols], sin_ref[:, cols])
            rows = slice(head * HS, (head + 1) * HS)
            lin, gain_part = head_norm_back(own_ref[rows, cols].astype(jnp.float32), qgain, back)
            qgrad_ref[rows, cols] = lin.astype(jnp.bfloat16)
            gain_total = gain_total + gain_part
        for source, rows in ((dk_ref, slice(0, HS)), (dv_ref, slice(HS, 2 * HS))):
            kv_own_ref[rows, cols] = source[i * WIDE : (i + 1) * WIDE, :].T
            kv_other_ref[rows, cols] = source[seen + i * WIDE : seen + (i + 1) * WIDE, :].T.astype(jnp.bfloat16)
    gain_ref[...] = gain_total


def key_back_kernel(
    own_ref, kv_own_ref, kv_came_ref, cos_ref, sin_ref, kgain_ref, qgrad_ref, grad_ref, gain_ref
):
    total = kv_own_ref[...] + kv_came_ref[...].astype(jnp.float32)
    back = unturn(total[:HS], cos_ref[...], sin_ref[...])
    key = own_ref[GROUP * HS : (GROUP + 1) * HS, :].astype(jnp.float32)
    lin, gain_part = head_norm_back(key, kgain_ref[...], back)
    grad_ref[: GROUP * HS, :] = qgrad_ref[...]
    grad_ref[GROUP * HS : (GROUP + 1) * HS, :] = lin.astype(jnp.bfloat16)
    grad_ref[(GROUP + 1) * HS :, :] = total[HS:].astype(jnp.bfloat16)
    gain_ref[...] = jnp.sum(gain_part, axis=1, keepdims=True)


def pack_kernel(gate_ref, up_ref, out_ref):
    count, rows, ffn = out_ref.shape
    team, half, few = count // 2, ffn // 2, rows // 2
    for ref, top in ((gate_ref, 0), (up_ref, few)):
        for place in range(team):
            parts = [
                ref[:, (zl * team + place) * half : (zl * team + place + 1) * half].astype(jnp.float32)
                for zl in range(2)
            ]
            block = jnp.concatenate(parts, axis=1).astype(jnp.bfloat16)
            out_ref[place, top : top + few, :] = block
            out_ref[team + place, top : top + few, :] = block


def gate_up_terms_kernel(ffn_ref, gate_ref, up_ref, out_ref):
    few, ffn = out_ref.shape[2:]
    chunk = RING * RING * few
    for c in range(ffn_ref.shape[1] // chunk):
        left = ffn_ref[:, c * chunk : (c + 1) * chunk]
        for side, ref in enumerate((gate_ref, up_ref)):
            terms = dot(left, ref[...], (0, 0)).reshape(RING, RING, few, ffn).astype(jnp.bfloat16)
            for row in range(RING):
                for quarter in range(RING):
                    out_ref[quarter, (side * 2 + c // 2) * 8 + c % 2 * RING + row] = terms[row, quarter]


def out_terms_kernel(hd_ref, att_ref, grad_ref, mine_ref, other_ref):
    pieces, few, _ = mine_ref.shape
    terms = dot(att_ref[...], grad_ref[...], (1, 0))
    for hd in range(2):
        for piece in range(pieces):
            start = (hd * pieces + piece) * few
            block = terms[start : start + few].astype(jnp.bfloat16)

            @pl.when(hd_ref[0] == hd)
            def _():
                mine_ref[piece] = block

            @pl.when(hd_ref[0] != hd)
            def _():
                other_ref[piece] = block


def joint_terms_kernel(normed_ref, grad_ref, out_ref):
    few = out_ref.shape[1]
    team, half = 2 * RING, normed_ref.shape[1] // 2
    for zl in range(2):
        terms = dot(normed_ref[:, zl * half : (zl + 1) * half], grad_ref[...], (0, 1))
        for place in range(team):
            for piece in range(8):
                start = (place * 8 + piece) * few
                out_ref[(piece * 2 + zl) * team + place] = terms[start : start + few].astype(jnp.bfloat16)


def unpack_ffn_kernel(pieces_ref, gate_ref, up_ref):
    team, few, ffn = pieces_ref.shape[2:]
    half = ffn // 2
    for side, ref in enumerate((gate_ref, up_ref)):
        blocks = [pieces_ref[0, side, place].astype(jnp.float32) for place in range(team)]
        ref[...] = jnp.concatenate(
            [block[:, zl * half : (zl + 1) * half] for zl in range(2) for block in blocks], axis=1
        )


def unpack_kernel(pieces_ref, w_down_ref, w_out_ref, w_query_ref, w_key_ref, w_value_ref):
    team, cols = 2 * RING, pieces_ref.shape[3]
    down, out, few = w_down_ref.shape[0] // 8, w_out_ref.shape[0] // 8, w_query_ref.shape[0] // 8
    rows = down + out
    down_rows, out_rows, joint_rows = [], [], []
    for x in range(RING):
        for zh in range(2):
            piece = pieces_ref[x, zh].astype(jnp.float32)
            ready = jnp.concatenate([piece[i * rows : (i + 1) * rows] for i in range(RING)], axis=1)
            down_rows.append(ready[:down])
            out_rows.append(ready[down:])
            heads = [RING * rows + place_of(head) * few for head in range(team)]
            joint_rows.append([piece[start : start + few] for start in heads])
    w_down_ref[...] = jnp.concatenate([down_rows[x * 2 + zh] for zh in range(2) for x in range(RING)], axis=0)
    w_out_ref[...] = jnp.concatenate(out_rows, axis=0)
    targets = (w_query_ref, 0, GROUP * HS), (w_key_ref, GROUP * HS, HS), (w_value_ref, (GROUP + 1) * HS, HS)
    for target, start, size in targets:
        parts = [
            jnp.concatenate([block[:, start : start + size] for block in blocks], axis=1) for blocks in joint_rows
        ]
        target[...] = jnp.concatenate(parts, axis=0)


def call(kernel, outs, scratch, args):
    smem = pl.BlockSpec(memory_space=pltpu.SMEM)
    vmem = pl.BlockSpec(memory_space=pltpu.VMEM)
    return pl.pallas_call(
        kernel,
        out_shape=[jax.ShapeDtypeStruct(shape, dtype) for shape, dtype in outs],
        in_specs=[smem if a.dtype == jnp.int32 else vmem for a in args],
        out_specs=[vmem for _ in outs],
        scratch_shapes=scratch,
        compiler_params=pltpu.CompilerParams(vmem_limit_bytes=40 * 1024 * 1024),
        cost_estimate=pl.CostEstimate(flops=1024, bytes_accessed=1024, transcendentals=0),
    )(*args)


def rope_tables(positions):
    half = HS // 2
    freqs = ROPE_BASE ** (-jnp.arange(half, dtype=jnp.float32) * 2.0 / HS)
    angles = freqs[:, None] * positions[None, :].astype(jnp.float32)
    return jnp.cos(angles), jnp.sin(angles)


def on_device(
    inputs,
    norm_gain,
    w_query,
    w_key,
    w_value,
    w_out,
    query_gain,
    key_gain,
    ffn_gain,
    w_gate,
    w_up,
    w_down,
    cotangent,
):
    f32, bf16 = jnp.float32, jnp.bfloat16
    tokens = inputs[0]
    out_grad = cotangent[0]
    rows, width = tokens.shape
    held = w_gate.shape[0]
    half_ffn = w_down.shape[0]
    ffn = 2 * half_ffn
    team = 2 * RING
    seen = team * rows
    quarter, few = width // 4, held // 4
    heads_width = GROUP * HS
    zl, hd = lax.axis_index("zl"), lax.axis_index("hd")
    tokens32 = tokens.astype(f32)

    by_head = lambda w: w.reshape(held, team, -1).transpose(1, 0, 2)
    joint_blocks = jnp.concatenate([by_head(w_query), by_head(w_key), by_head(w_value)], axis=2)
    joint_blocks = joint_blocks.reshape(2, RING, held, -1).swapaxes(0, 1).reshape(team, held, -1)
    joint_blocks = jnp.concatenate([joint_blocks, joint_blocks])
    normed = rms_forward(tokens32, norm_gain).astype(bf16)
    w_joint = exchange(joint_blocks, ("zl", "y", "hd"))
    normed_all = lax.all_gather(normed, TEAM, axis=0, tiled=True)
    my_rows = lambda w: lax.dynamic_slice_in_dim(w, lax.axis_index("x") * few, few, 0)
    gate_up_rows = call(pack_kernel, [((2 * team, 2 * few, ffn), bf16)], [], (my_rows(w_gate), my_rows(w_up)))[0]
    w_joint, gate_up_rows, grad_in = fence(w_joint, gate_up_rows, out_grad)
    w_joint = w_joint.reshape(width, -1)
    grad_all = lax.all_gather(grad_in, TEAM, axis=0, tiled=True)
    gate_up_rows = exchange(gate_up_rows, ("zl", "y", "hd"))
    down_other = jnp.concatenate([ring_z(w_down[: half_ffn // 2], 1), ring_z(w_down[half_ffn // 2 :], 3)])
    w_down_own = in_order(w_down, down_other, "zl", 0).reshape(ffn, width)
    out_rows = in_order(w_out, swap(w_out, "zl"), "zl", 0)
    w_out_own = in_order(at(out_rows, hd), swap(at(out_rows, 1 - hd), "hd"), "hd", 0).reshape(heads_width, width)

    joint = dot(w_joint, normed_all, (0, 1)).astype(bf16)
    other_kv = swap(joint[heads_width:], "zl")
    base = jnp.arange(seen, dtype=jnp.int32)
    cosine, sine = rope_tables(base + zl * seen)
    cosine2, sine2 = rope_tables(base + (1 - zl) * seen)
    half_flag = jnp.reshape(zl, (1,)).astype(jnp.int32)
    qgain, kgain = query_gain[:, None], key_gain[:, None]
    wide = seen // WIDE
    att, att32, lse, q_rot, kt_rot, k_rot, v_nat = call(
        attend_kernel,
        [
            ((heads_width, seen), bf16),
            ((wide, HS, ROWS), f32),
            ((wide, ROWS), f32),
            ((wide, HS, ROWS), bf16),
            ((HS, 2 * seen), bf16),
            ((2 * seen, HS), bf16),
            ((2 * seen, HS), bf16),
        ],
        [pltpu.VMEM((2 * HS, 2 * seen), bf16), pltpu.VMEM((wide, 2 * HS, ROWS), f32)],
        (half_flag, joint, other_kv, cosine, sine, cosine2, sine2, qgain, kgain),
    )
    att, gate_up_rows = fence(att, gate_up_rows)
    gate_up_all = lax.all_gather(gate_up_rows, "x", axis=0, tiled=False)
    chip = chip_sum(dot(att, w_out_own, (0, 0)).astype(bf16))
    middle = tokens32 + column_sum(chip)
    gate_up_all = gate_up_all.reshape(RING, 2 * team, 2, few, ffn).transpose(2, 1, 0, 3, 4).reshape(2, width, ffn)
    w_gate_own, w_up_own = gate_up_all[0], gate_up_all[1]
    ffn_in = rms_forward(middle, ffn_gain).astype(bf16)
    ffn_all = both_columns(gather_column(ffn_in))
    hidden_grad = dot(grad_all, w_down_own, (1, 1))
    gate = dot(ffn_all, w_gate_own, (1, 0))
    up_val = dot(ffn_all, w_up_own, (1, 0))
    sigmoid = jax.nn.sigmoid(gate)
    hidden = (gate * sigmoid * up_val).astype(bf16)
    gate_grad = (hidden_grad * up_val * sigmoid * (1.0 + gate * (1.0 - sigmoid))).astype(bf16)
    up_grad = (hidden_grad * gate * sigmoid).astype(bf16)
    ffn_part = (dot(gate_grad, w_gate_own, (1, 1)) + dot(up_grad, w_up_own, (1, 1))).astype(bf16)
    chip, gate_right, up_right, hidden_left = fence(chip_sum(ffn_part), gate_grad, up_grad, hidden)
    ffn_in_grad = column_sum(chip)

    gate_up_terms = call(
        gate_up_terms_kernel,
        [((RING, 4 * team, few, ffn), bf16)],
        [],
        (ffn_all, gate_right, up_right),
    )[0]
    gate_up_sum = lax.psum_scatter(gate_up_terms, "x", scatter_dimension=0, tiled=False)
    down_terms = dot(hidden_left, grad_all, (0, 0)).astype(bf16).reshape(4, half_ffn // 2, width)
    down_came = exchange(down_terms, ("zl", "zh"))
    ffn_in_grad, _, _, hidden_last = fence(ffn_in_grad, gate_up_terms, down_terms, hidden)

    middle_part, ffn_gain_part = rms_backward(middle, ffn_gain, ffn_in_grad)
    middle_grad = out_grad.astype(f32) + middle_part
    branch_grad = middle_grad.astype(bf16)
    out_part = dot(hidden_last, w_down_own, (1, 0)).astype(bf16)
    column, out_part, down_came = fence(gather_column(branch_grad), out_part, down_came)
    branch_all = both_columns(column)
    att_grad = dot(w_out_own, branch_all, (1, 1)).astype(bf16)

    q_grad, kv_own, kv_other, qgain_part = call(
        attend_back_kernel,
        [
            ((heads_width, seen), bf16),
            ((2 * HS, seen), f32),
            ((2 * HS, seen), bf16),
            ((HS, WIDE), f32),
        ],
        [
            pltpu.VMEM((2 * seen, HS), f32),
            pltpu.VMEM((2 * seen, HS), f32),
            pltpu.VMEM((wide, HS, ROWS), f32),
            pltpu.VMEM((wide, HS, ROWS), bf16),
            pltpu.VMEM((2 * wide, ROWS), f32),
        ],
        (half_flag, joint, att_grad, cosine, sine, qgain, att32, lse, q_rot, kt_rot, k_rot, v_nat),
    )
    out_mine, out_other = call(
        out_terms_kernel,
        [((8, held // 8, width), bf16)] * 2,
        [],
        (jnp.reshape(hd, (1,)).astype(jnp.int32), att, branch_all),
    )
    out_pieces = in_order(out_mine, swap(out_other, "hd"), "hd", 1)
    out_came = exchange(out_pieces.reshape(16, held // 8, width), SUMMED)
    kv_other, out_came, gate_up_sum = fence(kv_other, out_came, gate_up_sum)
    down_mine = sum_x(sum_first(down_came).reshape(4, half_ffn // 8, width))
    gate_up_came = exchange(gate_up_sum, ("zh", "zl") + TEAM)
    kv_came = swap(kv_other, "zl")
    joint_grad, kgain_part = call(
        key_back_kernel,
        [(joint.shape, bf16), ((HS, 1), f32)],
        [],
        (joint, kv_own, kv_came, cosine, sine, kgain, q_grad),
    )
    joint_pieces = call(
        joint_terms_kernel,
        [((16 * team, held // 8, joint.shape[0]), bf16)],
        [],
        (normed_all, joint_grad),
    )[0]
    normed_part = dot(joint_grad, w_joint, (0, 1))
    norm_gain_part = jnp.sum(normed_part * normed_all.astype(f32), axis=0) / norm_gain
    chip = chip_sum(normed_part.astype(bf16))
    chip, joint_pieces, gate_up_came, out_part = fence(chip, joint_pieces, gate_up_came, out_part)
    joint_came = exchange(joint_pieces, SUMMED + TEAM).reshape(16, team, held // 8, -1)
    gate_up_mine = sum_first(gate_up_came.reshape(4, team * few, ffn))
    gate_up_whole = lax.all_gather(gate_up_mine, ("x", "zh"), axis=0, tiled=False)
    gate_up_whole = gate_up_whole.reshape(RING, 2, team, few, ffn)
    out_sum = lax.psum_scatter(out_part, TEAM, scatter_dimension=0, tiled=True)
    output = (middle + out_sum.astype(f32)).astype(bf16)
    normed_grad = column_sum(chip)
    input_part, _ = rms_backward(tokens32, norm_gain, normed_grad)
    input_grad = middle_grad + input_part
    joint_came, norm_gain_part = fence(joint_came, norm_gain_part)
    joint_mine = sum_first(joint_came).reshape(held, -1)
    joint_mine = jnp.pad(joint_mine, ((0, 0), (0, quarter - joint_mine.shape[1])))
    ready = jnp.concatenate([down_mine, sum_first(out_came)])
    ready = [ready[:, i * quarter : (i + 1) * quarter] for i in range(4)]
    pieces = spread(jnp.concatenate([*ready, joint_mine]))
    block = lambda shape, index: pl.BlockSpec(shape, index)
    w_gate_grad, w_up_grad = pl.pallas_call(
        unpack_ffn_kernel,
        grid=(RING,),
        in_specs=[block((1, 2, team, few, ffn), lambda i: (i, 0, 0, 0, 0))],
        out_specs=[block((few, team * ffn), lambda i: (i, 0))] * 2,
        out_shape=[jax.ShapeDtypeStruct((held, team * ffn), f32)] * 2,
        compiler_params=pltpu.CompilerParams(vmem_limit_bytes=40 * 1024 * 1024),
    )(gate_up_whole)
    shapes = [(half_ffn, width), (held, width)] + [(held, w.shape[1]) for w in (w_query, w_key, w_value)]
    w_down_grad, w_out_grad, w_query_grad, w_key_grad, w_value_grad = call(
        unpack_kernel, [(shape, f32) for shape in shapes], [], (pieces,)
    )

    gains = jnp.concatenate([norm_gain_part, ffn_gain_part, jnp.sum(qgain_part, axis=1), kgain_part[:, 0]])
    gains = sum_everywhere(gains.reshape(-1, BLOCK)).reshape(-1)
    return (
        output[None],
        input_grad[None],
        gains[:width],
        w_query_grad,
        w_key_grad,
        w_value_grad,
        w_out_grad,
        gains[2 * width : 2 * width + HS],
        gains[2 * width + HS :],
        gains[width : 2 * width],
        w_gate_grad,
        w_up_grad,
        w_down_grad,
    )


def solution(mesh):
    fine = Mesh(mesh.devices.reshape(4, 2, 2, 4, 2), ("x", "zh", "zl", "y", "hd"))
    by_tokens = P(("x", "zh"), ("zl", "y", "hd"), None)
    by_rows = P(("zl", "y", "hd"), None)
    return jax.shard_map(
        on_device,
        mesh=fine,
        in_specs=(
            by_tokens, P(), by_rows, by_rows, by_rows, by_rows, P(), P(), P(), by_rows, by_rows, by_rows, by_tokens
        ),
        out_specs=(
            by_tokens, by_tokens, P(), by_rows, by_rows, by_rows, by_rows, P(), P(), P(), by_rows, by_rows, by_rows
        ),
        check_vma=False,
    )
```

```python
import jax
import jax.numpy as jnp
from jax import lax
from jax.experimental import pallas as pl
from jax.experimental.pallas import tpu as pltpu
from jax.sharding import Mesh, PartitionSpec as P

HQ = 24
HK = 8
HS = 64
GROUP = HQ // HK

EPSILON = 1e-05
ROPE_BASE = 1000000.0
SCORE_SCALE = 0.125

RING = 4
STEPS = (2, 1, 3)
BLOCK = 128
WIDE = 2 * BLOCK
ROWS = GROUP * WIDE


def rms_forward(values, gain):
    factor = lax.rsqrt(jnp.mean(values * values, axis=-1, keepdims=True) + EPSILON)
    return values * factor * gain


def rms_backward(values, gain, grad_out):
    factor = lax.rsqrt(jnp.mean(values * values, axis=-1, keepdims=True) + EPSILON)
    normal = values * factor
    scaled = grad_out * gain
    grad_in = factor * (scaled - normal * jnp.mean(scaled * normal, axis=-1, keepdims=True))
    grad_gain = jnp.sum(grad_out * normal, axis=0)
    return (grad_in, grad_gain)


def dot(left, right, contract):
    return lax.dot_general(
        left, right, (((contract[0],), (contract[1],)), ((), ())), preferred_element_type=jnp.float32
    )


SUMMED = ("x", "zh", "zl")
TEAM = ("y", "hd")


def at(array, index, axis=0):
    return lax.dynamic_index_in_dim(array, index, axis, keepdims=False)


def put(whole, array, *index):
    lead = (1,) * len(index)
    return lax.dynamic_update_slice(whole, array.reshape(lead + array.shape), index + (0,) * array.ndim)


def fence(*values):
    return lax.optimization_barrier(values)


def ring(array, axis, step):
    return lax.ppermute(array, axis, [(i, (i + step) % RING) for i in range(RING)])


def ring_z(array, step):
    return ring(array, ("zh", "zl"), step)


def swap(array, axis):
    return lax.ppermute(array, axis, [(0, 1), (1, 0)])


def in_order(mine, other, axis_name, axis):
    first = lax.axis_index(axis_name) == 0
    return jnp.stack([jnp.where(first, mine, other), jnp.where(first, other, mine)], axis=axis)


def gather_column(block):
    y = lax.axis_index("y")
    column = put(jnp.zeros((RING, *block.shape), block.dtype), block, y)
    for step in STEPS:
        column = put(column, ring(block, "y", step), (y - step) % RING)
    return column


def both_columns(column):
    return in_order(column, swap(column, "hd"), "hd", 1).reshape(-1, column.shape[-1])


def chip_sum(parts):
    hd = lax.axis_index("hd")
    parts = parts.reshape(RING, 2, BLOCK, -1)
    total = at(parts, hd, 1).astype(jnp.float32) + swap(at(parts, 1 - hd, 1), "hd").astype(jnp.float32)
    return total.astype(jnp.bfloat16)


def column_sum(chip):
    y = lax.axis_index("y")
    arrived = [ring(at(chip, (y + step) % RING), "y", step) for step in STEPS]
    return sum((came.astype(jnp.float32) for came in arrived), at(chip, y).astype(jnp.float32))


def exchange(blocks, axes):
    return lax.all_to_all(blocks, axes, split_axis=0, concat_axis=0, tiled=True)


def sum_x(pieces):
    x = lax.axis_index("x")
    arrived = [ring(at(pieces, (x + step) % RING), "x", step) for step in STEPS]
    return sum_first([at(pieces, x), *arrived])


def sum_first(arrived):
    return sum(arrived[i].astype(jnp.float32) for i in range(len(arrived))).astype(jnp.bfloat16)


def spread(piece, *beside):
    x = lax.axis_index("x")
    pair = in_order(piece, swap(piece, "zh"), "zh", 0)
    far, after, before = [ring(pair, "x", step) for step in STEPS]
    far, *beside = fence(far, *beside)
    whole = put(jnp.zeros((RING, *pair.shape), pair.dtype), pair, x)
    for step, block in zip(STEPS, (far, after, before)):
        whole = put(whole, block, (x - step) % RING)
    return whole, beside


def turn(values, cosine, sine):
    first, second = values[: HS // 2], values[HS // 2 :]
    return jnp.concatenate([first * cosine - second * sine, second * cosine + first * sine], axis=0)


def unturn(grads, cosine, sine):
    first, second = grads[: HS // 2], grads[HS // 2 :]
    return jnp.concatenate([first * cosine + second * sine, second * cosine - first * sine], axis=0)


def head_norm(values, gain):
    return values * lax.rsqrt(jnp.mean(values * values, axis=0, keepdims=True) + EPSILON) * gain


def head_norm_back(values, gain, grad_out):
    factor = lax.rsqrt(jnp.mean(values * values, axis=0, keepdims=True) + EPSILON)
    normal = values * factor
    scaled = grad_out * gain
    grad_in = factor * (scaled - normal * jnp.mean(scaled * normal, axis=0, keepdims=True))
    return grad_in, grad_out * normal


def allowed_keys():
    key = lax.broadcasted_iota(jnp.int32, (WIDE, ROWS), 0)
    query = lax.broadcasted_iota(jnp.int32, (WIDE, ROWS), 1) % WIDE
    return key <= query


def place_of(head):
    return head % RING * 2 + head // RING


def attend_kernel(
    half_ref, own_ref, other_ref, cos_ref, sin_ref, cos2_ref, sin2_ref, qgain_ref, kgain_ref,
    att_ref, out_ref, lse_ref, q_ref, kt_ref, k_ref, v_ref, vt_ref, total_ref,
):
    seen = own_ref.shape[1]
    count = seen // WIDE
    qgain, kgain = qgain_ref[...], kgain_ref[...]
    vt_ref[HS:, :] = jnp.ones((HS, vt_ref.shape[1]), jnp.bfloat16)
    for c in range(count):
        cols = slice(c * WIDE, (c + 1) * WIDE)
        sides = (
            (own_ref[GROUP * HS :, cols], cos_ref[:, cols], sin_ref[:, cols]),
            (other_ref[:, cols], cos2_ref[:, cols], sin2_ref[:, cols]),
        )
        for side, (pair, cosine, sine) in enumerate(sides):
            pair = pair.astype(jnp.float32)
            place = slice(side * seen + c * WIDE, side * seen + (c + 1) * WIDE)
            key = turn(head_norm(pair[:HS], kgain), cosine, sine)
            kt_ref[:, place] = key.astype(jnp.bfloat16)
            k_ref[place, :] = key.T.astype(jnp.bfloat16)
            vt_ref[:HS, place] = pair[HS:].astype(jnp.bfloat16)
            v_ref[place, :] = pair[HS:].T.astype(jnp.bfloat16)
        for head in range(GROUP):
            query = own_ref[head * HS : (head + 1) * HS, cols].astype(jnp.float32)
            query = turn(head_norm(query, qgain), cos_ref[:, cols], sin_ref[:, cols])
            q_ref[c, :, head * WIDE : (head + 1) * WIDE] = (query * SCORE_SCALE).astype(jnp.bfloat16)
    allowed = allowed_keys()

    def terms(i, start, masked):
        keys = slice(start, start + WIDE)
        weights = jnp.exp(dot(k_ref[keys, :], q_ref[i], (1, 0)))
        if masked:
            weights = jnp.where(allowed, weights, 0.0)
        return dot(vt_ref[:, keys], weights.astype(jnp.bfloat16), (1, 0))

    for i in range(count):
        total_ref[i] = sum(terms(i, c * WIDE, c == i) for c in range(i + 1))

    @pl.when(half_ref[0] == 1)
    def _():
        for i in range(count):
            total_ref[i] += sum(terms(i, seen + c * WIDE, False) for c in range(count))

    for i in range(count):
        total = total_ref[i]
        norm = total[HS : HS + 1]
        result = total[:HS] / norm
        lse_ref[i : i + 1, :] = jnp.log(norm)
        out_ref[i] = result
        for head in range(GROUP):
            part = result[:, head * WIDE : (head + 1) * WIDE].astype(jnp.bfloat16)
            att_ref[head * HS : (head + 1) * HS, i * WIDE : (i + 1) * WIDE] = part


def attend_back_kernel(
    half_ref, own_ref, grad_ref, cos_ref, sin_ref, qgain_ref, out_ref, lse_ref, q_ref, kt_ref, k_ref, v_ref,
    qgrad_ref, kv_own_ref, kv_other_ref, gain_ref, dk_ref, dv_ref, dq_ref, g_ref, delta_ref,
):
    seen = own_ref.shape[1]
    count = seen // WIDE
    qgain = qgain_ref[...]
    allowed = allowed_keys()

    def terms(i, start, masked):
        keys = slice(start, start + WIDE)
        query, grad = q_ref[i], g_ref[i]
        weights = jnp.exp(dot(k_ref[keys, :], query, (1, 0)) - lse_ref[i : i + 1, :])
        if masked:
            weights = jnp.where(allowed, weights, 0.0)
        prob_grad = dot(v_ref[keys, :], grad, (1, 0))
        score_grad = (weights * (prob_grad - delta_ref[i : i + 1, :])).astype(jnp.bfloat16)
        dv_ref[keys, :] += dot(weights.astype(jnp.bfloat16), grad, (1, 1))
        dk_ref[keys, :] += dot(score_grad, query, (1, 1))
        return dot(kt_ref[:, keys], score_grad, (1, 0))

    dk_ref[...] = jnp.zeros_like(dk_ref)
    dv_ref[...] = jnp.zeros_like(dv_ref)
    for i in range(count):
        for head in range(GROUP):
            g_ref[i, :, head * WIDE : (head + 1) * WIDE] = grad_ref[
                head * HS : (head + 1) * HS, i * WIDE : (i + 1) * WIDE
            ]
        delta_ref[i : i + 1, :] = jnp.sum(g_ref[i].astype(jnp.float32) * out_ref[i], axis=0, keepdims=True)
        dq_ref[i] = sum(terms(i, c * WIDE, c == i) for c in range(i + 1))

    @pl.when(half_ref[0] == 1)
    def _():
        for i in range(count):
            dq_ref[i] += sum(terms(i, seen + c * WIDE, False) for c in range(count))

    gain_total = jnp.zeros((HS, WIDE), jnp.float32)
    for i in range(count):
        cols = slice(i * WIDE, (i + 1) * WIDE)
        for head in range(GROUP):
            turned = dq_ref[i, :, head * WIDE : (head + 1) * WIDE] * SCORE_SCALE
            back = unturn(turned, cos_ref[:, cols], sin_ref[:, cols])
            rows = slice(head * HS, (head + 1) * HS)
            lin, gain_part = head_norm_back(own_ref[rows, cols].astype(jnp.float32), qgain, back)
            qgrad_ref[rows, cols] = lin.astype(jnp.bfloat16)
            gain_total = gain_total + gain_part
        for source, rows in ((dk_ref, slice(0, HS)), (dv_ref, slice(HS, 2 * HS))):
            kv_own_ref[rows, cols] = source[i * WIDE : (i + 1) * WIDE, :].T
            kv_other_ref[rows, cols] = source[seen + i * WIDE : seen + (i + 1) * WIDE, :].T.astype(jnp.bfloat16)
    gain_ref[...] = gain_total


def key_back_kernel(
    own_ref, kv_own_ref, kv_came_ref, cos_ref, sin_ref, kgain_ref, qgrad_ref, grad_ref, gain_ref
):
    total = kv_own_ref[...] + kv_came_ref[...].astype(jnp.float32)
    back = unturn(total[:HS], cos_ref[...], sin_ref[...])
    key = own_ref[GROUP * HS : (GROUP + 1) * HS, :].astype(jnp.float32)
    lin, gain_part = head_norm_back(key, kgain_ref[...], back)
    grad_ref[: GROUP * HS, :] = qgrad_ref[...]
    grad_ref[GROUP * HS : (GROUP + 1) * HS, :] = lin.astype(jnp.bfloat16)
    grad_ref[(GROUP + 1) * HS :, :] = total[HS:].astype(jnp.bfloat16)
    gain_ref[...] = jnp.sum(gain_part, axis=1, keepdims=True)


def pack_kernel(gate_ref, up_ref, out_ref):
    count, rows, ffn = out_ref.shape
    team, half, few = count // 2, ffn // 2, rows // 2
    for ref, top in ((gate_ref, 0), (up_ref, few)):
        for place in range(team):
            parts = [
                ref[:, (zl * team + place) * half : (zl * team + place + 1) * half].astype(jnp.float32)
                for zl in range(2)
            ]
            block = jnp.concatenate(parts, axis=1).astype(jnp.bfloat16)
            out_ref[place, top : top + few, :] = block
            out_ref[team + place, top : top + few, :] = block


def gate_up_terms_kernel(ffn_ref, gate_ref, up_ref, out_ref):
    few, ffn = out_ref.shape[2:]
    chunk = RING * RING * few
    for c in range(ffn_ref.shape[1] // chunk):
        left = ffn_ref[:, c * chunk : (c + 1) * chunk]
        for side, ref in enumerate((gate_ref, up_ref)):
            terms = dot(left, ref[...], (0, 0)).reshape(RING, RING, few, ffn).astype(jnp.bfloat16)
            for row in range(RING):
                for quarter in range(RING):
                    out_ref[quarter, (side * 2 + c // 2) * 8 + c % 2 * RING + row] = terms[row, quarter]


def out_terms_kernel(hd_ref, att_ref, grad_ref, mine_ref, other_ref):
    pieces, few, _ = mine_ref.shape
    terms = dot(att_ref[...], grad_ref[...], (1, 0))
    for hd in range(2):
        for piece in range(pieces):
            start = (hd * pieces + piece) * few
            block = terms[start : start + few].astype(jnp.bfloat16)

            @pl.when(hd_ref[0] == hd)
            def _():
                mine_ref[piece] = block

            @pl.when(hd_ref[0] != hd)
            def _():
                other_ref[piece] = block


def joint_terms_kernel(normed_ref, grad_ref, gains_ref, out_ref):
    team, half = 2 * RING, normed_ref.shape[1] // 2
    few = half // (8 * team)
    for zl in range(2):
        terms = dot(normed_ref[:, zl * half : (zl + 1) * half], grad_ref[...], (0, 1))
        for place in range(team):
            for piece in range(8):
                start = (place * 8 + piece) * few
                block = jnp.concatenate([terms[start : start + few], gains_ref[piece]], axis=0)
                out_ref[(piece * 2 + zl) * team + place] = block.astype(jnp.bfloat16)


def joint_sum_kernel(came_ref, out_ref):
    count, rows, cols = came_ref.shape
    team = 2 * RING
    few = rows - 4
    gains = jnp.zeros((4, cols), jnp.float32)
    parts = []
    for place in range(team):
        total = came_ref[place].astype(jnp.float32)
        for source in range(1, count // team):
            total = total + came_ref[source * team + place].astype(jnp.float32)
        parts.append(total[:few])
        gains = gains + total[few:]
    gains = gains[:2] + gains[2:]
    high = gains.astype(jnp.bfloat16).astype(jnp.float32)
    parts += [high, gains - high, jnp.zeros((4, cols), jnp.float32)]
    whole = jnp.concatenate(parts, axis=0)
    spare = jnp.zeros((whole.shape[0], out_ref.shape[1] - cols), jnp.float32)
    out_ref[...] = jnp.concatenate([whole, spare], axis=1).astype(jnp.bfloat16)


def unpack_ffn_kernel(pieces_ref, gate_ref, up_ref):
    team, few, ffn = pieces_ref.shape[2:]
    half = ffn // 2
    for side, ref in enumerate((gate_ref, up_ref)):
        blocks = [pieces_ref[0, side, place].astype(jnp.float32) for place in range(team)]
        ref[...] = jnp.concatenate(
            [block[:, zl * half : (zl + 1) * half] for zl in range(2) for block in blocks], axis=1
        )


def unpack_kernel(pieces_ref, w_down_ref, w_out_ref, w_query_ref, w_key_ref, w_value_ref, gains_ref):
    team, cols = 2 * RING, gains_ref.shape[2]
    down, out, few = w_down_ref.shape[0] // 8, w_out_ref.shape[0] // 8, w_query_ref.shape[0] // 8
    rows = down + out
    down_rows, out_rows, joint_rows = [], [], []
    for x in range(RING):
        for zh in range(2):
            piece = pieces_ref[x, zh].astype(jnp.float32)
            ready = jnp.concatenate([piece[i * rows : (i + 1) * rows] for i in range(RING)], axis=1)
            down_rows.append(ready[:down])
            out_rows.append(ready[down:])
            heads = [RING * rows + place_of(head) * few for head in range(team)]
            joint_rows.append([piece[start : start + few] for start in heads])
            gains = piece[RING * rows + team * few :, :cols]
            gains_ref[x * 2 + zh] = gains[:2] + gains[2:4]
    w_down_ref[...] = jnp.concatenate([down_rows[x * 2 + zh] for zh in range(2) for x in range(RING)], axis=0)
    w_out_ref[...] = jnp.concatenate(out_rows, axis=0)
    targets = (w_query_ref, 0, GROUP * HS), (w_key_ref, GROUP * HS, HS), (w_value_ref, (GROUP + 1) * HS, HS)
    for target, start, size in targets:
        parts = [
            jnp.concatenate([block[:, start : start + size] for block in blocks], axis=1) for blocks in joint_rows
        ]
        target[...] = jnp.concatenate(parts, axis=0)


def call(kernel, outs, scratch, args):
    smem = pl.BlockSpec(memory_space=pltpu.SMEM)
    vmem = pl.BlockSpec(memory_space=pltpu.VMEM)
    return pl.pallas_call(
        kernel,
        out_shape=[jax.ShapeDtypeStruct(shape, dtype) for shape, dtype in outs],
        in_specs=[smem if a.dtype == jnp.int32 else vmem for a in args],
        out_specs=[vmem for _ in outs],
        scratch_shapes=scratch,
        compiler_params=pltpu.CompilerParams(vmem_limit_bytes=40 * 1024 * 1024),
        cost_estimate=pl.CostEstimate(flops=1024, bytes_accessed=1024, transcendentals=0),
    )(*args)


def rope_tables(positions):
    half = HS // 2
    freqs = ROPE_BASE ** (-jnp.arange(half, dtype=jnp.float32) * 2.0 / HS)
    angles = freqs[:, None] * positions[None, :].astype(jnp.float32)
    return jnp.cos(angles), jnp.sin(angles)


def on_device(
    inputs,
    norm_gain,
    w_query,
    w_key,
    w_value,
    w_out,
    query_gain,
    key_gain,
    ffn_gain,
    w_gate,
    w_up,
    w_down,
    cotangent,
):
    f32, bf16 = jnp.float32, jnp.bfloat16
    tokens = inputs[0]
    out_grad = cotangent[0]
    rows, width = tokens.shape
    held = w_gate.shape[0]
    half_ffn = w_down.shape[0]
    ffn = 2 * half_ffn
    team = 2 * RING
    seen = team * rows
    quarter, few = width // 4, held // 4
    heads_width = GROUP * HS
    zl, hd = lax.axis_index("zl"), lax.axis_index("hd")
    tokens32 = tokens.astype(f32)

    by_head = lambda w: w.reshape(held, team, -1).transpose(1, 0, 2)
    joint_blocks = jnp.concatenate([by_head(w_query), by_head(w_key), by_head(w_value)], axis=2)
    joint_blocks = joint_blocks.reshape(2, RING, held, -1).swapaxes(0, 1).reshape(team, held, -1)
    joint_blocks = jnp.concatenate([joint_blocks, joint_blocks])
    normed = rms_forward(tokens32, norm_gain).astype(bf16)
    w_joint = exchange(joint_blocks, ("zl", "y", "hd"))
    normed_all = lax.all_gather(normed, TEAM, axis=0, tiled=True)
    my_rows = lambda w: lax.dynamic_slice_in_dim(w, lax.axis_index("x") * few, few, 0)
    gate_up_rows = call(pack_kernel, [((2 * team, 2 * few, ffn), bf16)], [], (my_rows(w_gate), my_rows(w_up)))[0]
    out_rows = in_order(w_out, swap(w_out, "zl"), "zl", 0)
    w_out_own = in_order(at(out_rows, hd), swap(at(out_rows, 1 - hd), "hd"), "hd", 0).reshape(heads_width, width)
    w_joint, w_out_own, gate_up_rows, grad_in = fence(w_joint, w_out_own, gate_up_rows, out_grad)
    w_joint = w_joint.reshape(width, -1)
    grad_all = lax.all_gather(grad_in, TEAM, axis=0, tiled=True)
    gate_up_rows = exchange(gate_up_rows, ("zl", "y", "hd"))
    down_other = jnp.concatenate([ring_z(w_down[: half_ffn // 2], 1), ring_z(w_down[half_ffn // 2 :], 3)])
    w_down_own = in_order(w_down, down_other, "zl", 0).reshape(ffn, width)

    joint = dot(w_joint, normed_all, (0, 1)).astype(bf16)
    other_kv = swap(joint[heads_width:], "zl")
    base = jnp.arange(seen, dtype=jnp.int32)
    cosine, sine = rope_tables(base + zl * seen)
    cosine2, sine2 = rope_tables(base + (1 - zl) * seen)
    half_flag = jnp.reshape(zl, (1,)).astype(jnp.int32)
    qgain, kgain = query_gain[:, None], key_gain[:, None]
    wide = seen // WIDE
    att, att32, lse, q_rot, kt_rot, k_rot, v_nat = call(
        attend_kernel,
        [
            ((heads_width, seen), bf16),
            ((wide, HS, ROWS), f32),
            ((wide, ROWS), f32),
            ((wide, HS, ROWS), bf16),
            ((HS, 2 * seen), bf16),
            ((2 * seen, HS), bf16),
            ((2 * seen, HS), bf16),
        ],
        [pltpu.VMEM((2 * HS, 2 * seen), bf16), pltpu.VMEM((wide, 2 * HS, ROWS), f32)],
        (half_flag, joint, other_kv, cosine, sine, cosine2, sine2, qgain, kgain),
    )
    att, gate_up_rows = fence(att, gate_up_rows)
    gate_up_all = lax.all_gather(gate_up_rows, "x", axis=0, tiled=False)
    chip = chip_sum(dot(att, w_out_own, (0, 0)).astype(bf16))
    middle = tokens32 + column_sum(chip)
    gate_up_all = gate_up_all.reshape(RING, 2 * team, 2, few, ffn).transpose(2, 1, 0, 3, 4).reshape(2, width, ffn)
    w_gate_own, w_up_own = gate_up_all[0], gate_up_all[1]
    ffn_in = rms_forward(middle, ffn_gain).astype(bf16)
    ffn_all = both_columns(gather_column(ffn_in))
    hidden_grad = dot(grad_all, w_down_own, (1, 1))
    gate = dot(ffn_all, w_gate_own, (1, 0))
    up_val = dot(ffn_all, w_up_own, (1, 0))
    sigmoid = jax.nn.sigmoid(gate)
    hidden = (gate * sigmoid * up_val).astype(bf16)
    gate_grad = (hidden_grad * up_val * sigmoid * (1.0 + gate * (1.0 - sigmoid))).astype(bf16)
    up_grad = (hidden_grad * gate * sigmoid).astype(bf16)
    ffn_part = (dot(gate_grad, w_gate_own, (1, 1)) + dot(up_grad, w_up_own, (1, 1))).astype(bf16)
    chip, gate_right, up_right, hidden_left = fence(chip_sum(ffn_part), gate_grad, up_grad, hidden)
    ffn_in_grad = column_sum(chip)

    gate_up_terms = call(
        gate_up_terms_kernel,
        [((RING, 4 * team, few, ffn), bf16)],
        [],
        (ffn_all, gate_right, up_right),
    )[0]
    gate_up_sum = lax.psum_scatter(gate_up_terms, "x", scatter_dimension=0, tiled=False)
    down_terms = dot(hidden_left, grad_all, (0, 0)).astype(bf16).reshape(4, half_ffn // 2, width)
    down_came = exchange(down_terms, ("zl", "zh"))
    ffn_in_grad, _, _, hidden_last = fence(ffn_in_grad, gate_up_terms, down_terms, hidden)

    middle_part, ffn_gain_part = rms_backward(middle, ffn_gain, ffn_in_grad)
    middle_grad = out_grad.astype(f32) + middle_part
    branch_grad = middle_grad.astype(bf16)
    out_part = dot(hidden_last, w_down_own, (1, 0)).astype(bf16)
    column, out_part, down_came = fence(gather_column(branch_grad), out_part, down_came)
    out_sum = lax.psum_scatter(out_part, TEAM, scatter_dimension=0, tiled=True)
    branch_all = both_columns(column)
    att_grad = dot(w_out_own, branch_all, (1, 1)).astype(bf16)

    out_mine, out_other = call(
        out_terms_kernel,
        [((8, held // 8, width), bf16)] * 2,
        [],
        (jnp.reshape(hd, (1,)).astype(jnp.int32), att, branch_all),
    )
    out_pieces = in_order(out_mine, swap(out_other, "hd"), "hd", 1)
    att_grad, out_pieces = fence(att_grad, out_pieces)
    out_came = exchange(out_pieces.reshape(16, held // 8, width), SUMMED)
    q_grad, kv_own, kv_other, qgain_part = call(
        attend_back_kernel,
        [
            ((heads_width, seen), bf16),
            ((2 * HS, seen), f32),
            ((2 * HS, seen), bf16),
            ((HS, WIDE), f32),
        ],
        [
            pltpu.VMEM((2 * seen, HS), f32),
            pltpu.VMEM((2 * seen, HS), f32),
            pltpu.VMEM((wide, HS, ROWS), f32),
            pltpu.VMEM((wide, HS, ROWS), bf16),
            pltpu.VMEM((2 * wide, ROWS), f32),
        ],
        (half_flag, joint, att_grad, cosine, sine, qgain, att32, lse, q_rot, kt_rot, k_rot, v_nat),
    )
    gate_up_came = exchange(gate_up_sum, ("zh", "zl") + TEAM)
    kv_came, gate_up_came, att, down_came = fence(swap(kv_other, "zl"), gate_up_came, att, down_came)
    joint_grad, kgain_part = call(
        key_back_kernel,
        [(joint.shape, bf16), ((HS, 1), f32)],
        [],
        (joint, kv_own, kv_came, cosine, sine, kgain, q_grad),
    )
    normed_part = dot(joint_grad, w_joint, (0, 1))
    norm_gain_part = jnp.sum(normed_part * normed_all.astype(f32), axis=0) / norm_gain
    normed_part = normed_part.astype(bf16)
    gains = [norm_gain_part, ffn_gain_part, jnp.sum(qgain_part, axis=1), kgain_part[:, 0]]
    joint_width = joint.shape[0]
    gains = jnp.concatenate([*gains, jnp.zeros((16 * joint_width - 2 * width - 2 * HS,), f32)])
    gains = gains.reshape(8, 2, joint_width)
    high = lax.optimization_barrier(gains.astype(bf16)).astype(f32)
    joint_pieces = call(
        joint_terms_kernel,
        [((16 * team, held // 8 + 4, joint_width), bf16)],
        [],
        (normed_all, joint_grad, jnp.concatenate([high, gains - high], axis=1)),
    )[0]
    joint_pieces, gate_up_came, out_came, normed_part, down_came = fence(
        joint_pieces, gate_up_came, out_came, normed_part, down_came
    )
    joint_came = exchange(joint_pieces, SUMMED + TEAM)
    gate_up_mine = sum_first(gate_up_came.reshape(4, team * few, ffn))
    gate_up_whole = lax.all_gather(gate_up_mine, ("x", "zh"), axis=0, tiled=False)
    gate_up_whole = gate_up_whole.reshape(RING, 2, team, few, ffn)
    down_mine = sum_x(sum_first(down_came).reshape(4, half_ffn // 8, width))
    ready = jnp.concatenate([down_mine, sum_first(out_came)])
    ready = jnp.concatenate([ready[:, i * quarter : (i + 1) * quarter] for i in range(4)])
    joint_came, ready, chip = fence(joint_came, ready, chip_sum(normed_part))
    joint_mine = call(joint_sum_kernel, [((held + 8, quarter), bf16)], [], (joint_came,))[0]
    pieces, (normed_grad,) = spread(jnp.concatenate([ready, joint_mine]), column_sum(chip))
    output = (middle + out_sum.astype(f32)).astype(bf16)
    input_part, _ = rms_backward(tokens32, norm_gain, normed_grad)
    input_grad = middle_grad + input_part
    block = lambda shape, index: pl.BlockSpec(shape, index)
    w_gate_grad, w_up_grad = pl.pallas_call(
        unpack_ffn_kernel,
        grid=(RING,),
        in_specs=[block((1, 2, team, few, ffn), lambda i: (i, 0, 0, 0, 0))],
        out_specs=[block((few, team * ffn), lambda i: (i, 0))] * 2,
        out_shape=[jax.ShapeDtypeStruct((held, team * ffn), f32)] * 2,
        compiler_params=pltpu.CompilerParams(vmem_limit_bytes=40 * 1024 * 1024),
    )(gate_up_whole)
    shapes = [(half_ffn, width), (held, width)] + [(held, w.shape[1]) for w in (w_query, w_key, w_value)]
    shapes.append((8, 2, joint_width))
    w_down_grad, w_out_grad, w_query_grad, w_key_grad, w_value_grad, gains = call(
        unpack_kernel, [(shape, f32) for shape in shapes], [], (pieces,)
    )

    gains = gains.reshape(-1)
    return (
        output[None],
        input_grad[None],
        gains[:width],
        w_query_grad,
        w_key_grad,
        w_value_grad,
        w_out_grad,
        gains[2 * width : 2 * width + HS],
        gains[2 * width + HS : 2 * width + 2 * HS],
        gains[width : 2 * width],
        w_gate_grad,
        w_up_grad,
        w_down_grad,
    )


def solution(mesh):
    fine = Mesh(mesh.devices.reshape(4, 2, 2, 4, 2), ("x", "zh", "zl", "y", "hd"))
    by_tokens = P(("x", "zh"), ("zl", "y", "hd"), None)
    by_rows = P(("zl", "y", "hd"), None)
    return jax.shard_map(
        on_device,
        mesh=fine,
        in_specs=(
            by_tokens, P(), by_rows, by_rows, by_rows, by_rows, P(), P(), P(), by_rows, by_rows, by_rows, by_tokens
        ),
        out_specs=(
            by_tokens, by_tokens, P(), by_rows, by_rows, by_rows, by_rows, P(), P(), P(), by_rows, by_rows, by_rows
        ),
        check_vma=False,
    )
```

```python
import jax
import jax.numpy as jnp
from jax import lax
from jax.experimental import pallas as pl
from jax.experimental.pallas import tpu as pltpu
from jax.sharding import Mesh, PartitionSpec as P

HQ = 24
HK = 8
HS = 64
GROUP = HQ // HK

EPSILON = 1e-05
ROPE_BASE = 1000000.0
SCORE_SCALE = 0.125

RING = 4
STEPS = (2, 1, 3)
BLOCK = 128
WIDE = 2 * BLOCK
ROWS = GROUP * WIDE


def rms_forward(values, gain):
    factor = lax.rsqrt(jnp.mean(values * values, axis=-1, keepdims=True) + EPSILON)
    return values * factor * gain


def rms_backward(values, gain, grad_out):
    factor = lax.rsqrt(jnp.mean(values * values, axis=-1, keepdims=True) + EPSILON)
    normal = values * factor
    scaled = grad_out * gain
    grad_in = factor * (scaled - normal * jnp.mean(scaled * normal, axis=-1, keepdims=True))
    grad_gain = jnp.sum(grad_out * normal, axis=0)
    return (grad_in, grad_gain)


def dot(left, right, contract):
    return lax.dot_general(
        left, right, (((contract[0],), (contract[1],)), ((), ())), preferred_element_type=jnp.float32
    )


SUMMED = ("x", "zh", "zl")
TEAM = ("y", "hd")


def at(array, index, axis=0):
    return lax.dynamic_index_in_dim(array, index, axis, keepdims=False)


def put(whole, array, *index):
    lead = (1,) * len(index)
    return lax.dynamic_update_slice(whole, array.reshape(lead + array.shape), index + (0,) * array.ndim)


def fence(*values):
    return lax.optimization_barrier(values)


def ring(array, axis, step):
    return lax.ppermute(array, axis, [(i, (i + step) % RING) for i in range(RING)])


def ring_z(array, step):
    return ring(array, ("zh", "zl"), step)


def swap(array, axis):
    return lax.ppermute(array, axis, [(0, 1), (1, 0)])


def in_order(mine, other, axis_name, axis):
    first = lax.axis_index(axis_name) == 0
    return jnp.stack([jnp.where(first, mine, other), jnp.where(first, other, mine)], axis=axis)


def gather_column(block):
    y = lax.axis_index("y")
    column = put(jnp.zeros((RING, *block.shape), block.dtype), block, y)
    for step in STEPS:
        column = put(column, ring(block, "y", step), (y - step) % RING)
    return column


def both_columns(column):
    return in_order(column, swap(column, "hd"), "hd", 1).reshape(-1, column.shape[-1])


def chip_sum(parts):
    hd = lax.axis_index("hd")
    parts = parts.reshape(RING, 2, BLOCK, -1)
    total = at(parts, hd, 1).astype(jnp.float32) + swap(at(parts, 1 - hd, 1), "hd").astype(jnp.float32)
    return total.astype(jnp.bfloat16)


def column_sum(chip):
    y = lax.axis_index("y")
    arrived = [ring(at(chip, (y + step) % RING), "y", step) for step in STEPS]
    return sum((came.astype(jnp.float32) for came in arrived), at(chip, y).astype(jnp.float32))


def exchange(blocks, axes):
    return lax.all_to_all(blocks, axes, split_axis=0, concat_axis=0, tiled=True)


def sum_x(pieces):
    x = lax.axis_index("x")
    arrived = [ring(at(pieces, (x + step) % RING), "x", step) for step in STEPS]
    return sum_first([at(pieces, x), *arrived])


def sum_first(arrived):
    return sum(arrived[i].astype(jnp.float32) for i in range(len(arrived))).astype(jnp.bfloat16)


def spread(piece, *beside):
    x = lax.axis_index("x")
    pair = in_order(piece, swap(piece, "zh"), "zh", 0)
    far, after, before = [ring(pair, "x", step) for step in STEPS]
    far, *beside = fence(far, *beside)
    whole = put(jnp.zeros((RING, *pair.shape), pair.dtype), pair, x)
    for step, block in zip(STEPS, (far, after, before)):
        whole = put(whole, block, (x - step) % RING)
    return whole, beside


def turn(values, cosine, sine):
    first, second = values[: HS // 2], values[HS // 2 :]
    return jnp.concatenate([first * cosine - second * sine, second * cosine + first * sine], axis=0)


def unturn(grads, cosine, sine):
    first, second = grads[: HS // 2], grads[HS // 2 :]
    return jnp.concatenate([first * cosine + second * sine, second * cosine - first * sine], axis=0)


def head_norm(values, gain):
    return values * lax.rsqrt(jnp.mean(values * values, axis=0, keepdims=True) + EPSILON) * gain


def head_norm_back(values, gain, grad_out):
    factor = lax.rsqrt(jnp.mean(values * values, axis=0, keepdims=True) + EPSILON)
    normal = values * factor
    scaled = grad_out * gain
    grad_in = factor * (scaled - normal * jnp.mean(scaled * normal, axis=0, keepdims=True))
    return grad_in, grad_out * normal


def allowed_keys():
    key = lax.broadcasted_iota(jnp.int32, (WIDE, ROWS), 0)
    query = lax.broadcasted_iota(jnp.int32, (WIDE, ROWS), 1) % WIDE
    return key <= query


def place_of(head):
    return head % RING * 2 + head // RING


def attend_kernel(
    half_ref, own_ref, other_ref, cos_ref, sin_ref, cos2_ref, sin2_ref, qgain_ref, kgain_ref,
    att_ref, out_ref, lse_ref, q_ref, kt_ref, k_ref, v_ref, vt_ref, total_ref,
):
    seen = own_ref.shape[1]
    count = seen // WIDE
    qgain, kgain = qgain_ref[...], kgain_ref[...]
    vt_ref[HS:, :] = jnp.ones((HS, vt_ref.shape[1]), jnp.bfloat16)
    for c in range(count):
        cols = slice(c * WIDE, (c + 1) * WIDE)
        sides = (
            (own_ref[GROUP * HS :, cols], cos_ref[:, cols], sin_ref[:, cols]),
            (other_ref[:, cols], cos2_ref[:, cols], sin2_ref[:, cols]),
        )
        for side, (pair, cosine, sine) in enumerate(sides):
            pair = pair.astype(jnp.float32)
            place = slice(side * seen + c * WIDE, side * seen + (c + 1) * WIDE)
            key = turn(head_norm(pair[:HS], kgain), cosine, sine)
            kt_ref[:, place] = key.astype(jnp.bfloat16)
            k_ref[place, :] = key.T.astype(jnp.bfloat16)
            vt_ref[:HS, place] = pair[HS:].astype(jnp.bfloat16)
            v_ref[place, :] = pair[HS:].T.astype(jnp.bfloat16)
        for head in range(GROUP):
            query = own_ref[head * HS : (head + 1) * HS, cols].astype(jnp.float32)
            query = turn(head_norm(query, qgain), cos_ref[:, cols], sin_ref[:, cols])
            q_ref[c, :, head * WIDE : (head + 1) * WIDE] = (query * SCORE_SCALE).astype(jnp.bfloat16)
    allowed = allowed_keys()

    def terms(i, start, masked):
        keys = slice(start, start + WIDE)
        weights = jnp.exp(dot(k_ref[keys, :], q_ref[i], (1, 0)))
        if masked:
            weights = jnp.where(allowed, weights, 0.0)
        return dot(vt_ref[:, keys], weights.astype(jnp.bfloat16), (1, 0))

    for i in range(count):
        total_ref[i] = sum(terms(i, c * WIDE, c == i) for c in range(i + 1))

    @pl.when(half_ref[0] == 1)
    def _():
        for i in range(count):
            total_ref[i] += sum(terms(i, seen + c * WIDE, False) for c in range(count))

    for i in range(count):
        total = total_ref[i]
        norm = total[HS : HS + 1]
        result = total[:HS] / norm
        lse_ref[i : i + 1, :] = jnp.log(norm)
        out_ref[i] = result
        for head in range(GROUP):
            part = result[:, head * WIDE : (head + 1) * WIDE].astype(jnp.bfloat16)
            att_ref[head * HS : (head + 1) * HS, i * WIDE : (i + 1) * WIDE] = part


def attend_back_kernel(
    half_ref, own_ref, grad_ref, cos_ref, sin_ref, qgain_ref, out_ref, lse_ref, q_ref, kt_ref, k_ref, v_ref,
    qgrad_ref, kv_own_ref, kv_other_ref, gain_ref, dk_ref, dv_ref, dq_ref, g_ref, delta_ref,
):
    seen = own_ref.shape[1]
    count = seen // WIDE
    qgain = qgain_ref[...]
    allowed = allowed_keys()

    def terms(i, start, masked):
        keys = slice(start, start + WIDE)
        query, grad = q_ref[i], g_ref[i]
        weights = jnp.exp(dot(k_ref[keys, :], query, (1, 0)) - lse_ref[i : i + 1, :])
        if masked:
            weights = jnp.where(allowed, weights, 0.0)
        prob_grad = dot(v_ref[keys, :], grad, (1, 0))
        score_grad = (weights * (prob_grad - delta_ref[i : i + 1, :])).astype(jnp.bfloat16)
        dv_ref[keys, :] += dot(weights.astype(jnp.bfloat16), grad, (1, 1))
        dk_ref[keys, :] += dot(score_grad, query, (1, 1))
        return dot(kt_ref[:, keys], score_grad, (1, 0))

    dk_ref[...] = jnp.zeros_like(dk_ref)
    dv_ref[...] = jnp.zeros_like(dv_ref)
    for i in range(count):
        for head in range(GROUP):
            g_ref[i, :, head * WIDE : (head + 1) * WIDE] = grad_ref[
                head * HS : (head + 1) * HS, i * WIDE : (i + 1) * WIDE
            ]
        delta_ref[i : i + 1, :] = jnp.sum(g_ref[i].astype(jnp.float32) * out_ref[i], axis=0, keepdims=True)
        dq_ref[i] = sum(terms(i, c * WIDE, c == i) for c in range(i + 1))

    @pl.when(half_ref[0] == 1)
    def _():
        for i in range(count):
            dq_ref[i] += sum(terms(i, seen + c * WIDE, False) for c in range(count))

    gain_total = jnp.zeros((HS, WIDE), jnp.float32)
    for i in range(count):
        cols = slice(i * WIDE, (i + 1) * WIDE)
        for head in range(GROUP):
            turned = dq_ref[i, :, head * WIDE : (head + 1) * WIDE] * SCORE_SCALE
            back = unturn(turned, cos_ref[:, cols], sin_ref[:, cols])
            rows = slice(head * HS, (head + 1) * HS)
            lin, gain_part = head_norm_back(own_ref[rows, cols].astype(jnp.float32), qgain, back)
            qgrad_ref[rows, cols] = lin.astype(jnp.bfloat16)
            gain_total = gain_total + gain_part
        for source, rows in ((dk_ref, slice(0, HS)), (dv_ref, slice(HS, 2 * HS))):
            kv_own_ref[rows, cols] = source[i * WIDE : (i + 1) * WIDE, :].T
            kv_other_ref[rows, cols] = source[seen + i * WIDE : seen + (i + 1) * WIDE, :].T.astype(jnp.bfloat16)
    gain_ref[...] = gain_total


def key_back_kernel(
    own_ref, kv_own_ref, kv_came_ref, cos_ref, sin_ref, kgain_ref, qgrad_ref, grad_ref, gain_ref
):
    total = kv_own_ref[...] + kv_came_ref[...].astype(jnp.float32)
    back = unturn(total[:HS], cos_ref[...], sin_ref[...])
    key = own_ref[GROUP * HS : (GROUP + 1) * HS, :].astype(jnp.float32)
    lin, gain_part = head_norm_back(key, kgain_ref[...], back)
    grad_ref[: GROUP * HS, :] = qgrad_ref[...]
    grad_ref[GROUP * HS : (GROUP + 1) * HS, :] = lin.astype(jnp.bfloat16)
    grad_ref[(GROUP + 1) * HS :, :] = total[HS:].astype(jnp.bfloat16)
    gain_ref[...] = jnp.sum(gain_part, axis=1, keepdims=True)


def pack_kernel(gate_ref, up_ref, out_ref):
    count, rows, ffn = out_ref.shape
    team, half, few = count // 2, ffn // 2, rows // 2
    for ref, top in ((gate_ref, 0), (up_ref, few)):
        for place in range(team):
            parts = [
                ref[:, (zl * team + place) * half : (zl * team + place + 1) * half].astype(jnp.float32)
                for zl in range(2)
            ]
            block = jnp.concatenate(parts, axis=1).astype(jnp.bfloat16)
            out_ref[place, top : top + few, :] = block
            out_ref[team + place, top : top + few, :] = block


def gate_up_terms_kernel(ffn_ref, gate_ref, up_ref, out_ref):
    few, ffn = out_ref.shape[2:]
    chunk = RING * RING * few
    for c in range(ffn_ref.shape[1] // chunk):
        left = ffn_ref[:, c * chunk : (c + 1) * chunk]
        for side, ref in enumerate((gate_ref, up_ref)):
            terms = dot(left, ref[...], (0, 0)).reshape(RING, RING, few, ffn).astype(jnp.bfloat16)
            for row in range(RING):
                for quarter in range(RING):
                    out_ref[quarter, (side * 2 + c // 2) * 8 + c % 2 * RING + row] = terms[row, quarter]


def out_terms_kernel(hd_ref, att_ref, grad_ref, mine_ref, other_ref):
    pieces, few, _ = mine_ref.shape
    terms = dot(att_ref[...], grad_ref[...], (1, 0))
    for hd in range(2):
        for piece in range(pieces):
            start = (hd * pieces + piece) * few
            block = terms[start : start + few].astype(jnp.bfloat16)

            @pl.when(hd_ref[0] == hd)
            def _():
                mine_ref[piece] = block

            @pl.when(hd_ref[0] != hd)
            def _():
                other_ref[piece] = block


def joint_terms_kernel(normed_ref, grad_ref, gains_ref, out_ref):
    team, half = 2 * RING, normed_ref.shape[1] // 2
    few = half // (8 * team)
    for zl in range(2):
        terms = dot(normed_ref[:, zl * half : (zl + 1) * half], grad_ref[...], (0, 1))
        for place in range(team):
            for piece in range(8):
                start = (place * 8 + piece) * few
                block = jnp.concatenate([terms[start : start + few], gains_ref[piece]], axis=0)
                out_ref[(piece * 2 + zl) * team + place] = block.astype(jnp.bfloat16)


def joint_sum_kernel(came_ref, out_ref):
    count, rows, cols = came_ref.shape
    team = 2 * RING
    few = rows - 4
    gains = jnp.zeros((4, cols), jnp.float32)
    parts = []
    for place in range(team):
        total = came_ref[place].astype(jnp.float32)
        for source in range(1, count // team):
            total = total + came_ref[source * team + place].astype(jnp.float32)
        parts.append(total[:few])
        gains = gains + total[few:]
    gains = gains[:2] + gains[2:]
    high = gains.astype(jnp.bfloat16).astype(jnp.float32)
    parts += [high, gains - high, jnp.zeros((4, cols), jnp.float32)]
    whole = jnp.concatenate(parts, axis=0)
    spare = jnp.zeros((whole.shape[0], out_ref.shape[1] - cols), jnp.float32)
    out_ref[...] = jnp.concatenate([whole, spare], axis=1).astype(jnp.bfloat16)


def unpack_ffn_kernel(pieces_ref, gate_ref, up_ref):
    team, few, ffn = pieces_ref.shape[2:]
    half = ffn // 2
    for side, ref in enumerate((gate_ref, up_ref)):
        blocks = [pieces_ref[0, side, place].astype(jnp.float32) for place in range(team)]
        ref[...] = jnp.concatenate(
            [block[:, zl * half : (zl + 1) * half] for zl in range(2) for block in blocks], axis=1
        )


def unpack_kernel(pieces_ref, w_down_ref, w_out_ref, w_query_ref, w_key_ref, w_value_ref, gains_ref):
    team, cols = 2 * RING, gains_ref.shape[2]
    down, out, few = w_down_ref.shape[0] // 8, w_out_ref.shape[0] // 8, w_query_ref.shape[0] // 8
    rows = down + out
    down_rows, out_rows, joint_rows = [], [], []
    for x in range(RING):
        for zh in range(2):
            piece = pieces_ref[x, zh].astype(jnp.float32)
            ready = jnp.concatenate([piece[i * rows : (i + 1) * rows] for i in range(RING)], axis=1)
            down_rows.append(ready[:down])
            out_rows.append(ready[down:])
            heads = [RING * rows + place_of(head) * few for head in range(team)]
            joint_rows.append([piece[start : start + few] for start in heads])
            gains = piece[RING * rows + team * few :, :cols]
            gains_ref[x * 2 + zh] = gains[:2] + gains[2:4]
    w_down_ref[...] = jnp.concatenate([down_rows[x * 2 + zh] for zh in range(2) for x in range(RING)], axis=0)
    w_out_ref[...] = jnp.concatenate(out_rows, axis=0)
    targets = (w_query_ref, 0, GROUP * HS), (w_key_ref, GROUP * HS, HS), (w_value_ref, (GROUP + 1) * HS, HS)
    for target, start, size in targets:
        parts = [
            jnp.concatenate([block[:, start : start + size] for block in blocks], axis=1) for blocks in joint_rows
        ]
        target[...] = jnp.concatenate(parts, axis=0)


def call(kernel, outs, scratch, args):
    smem = pl.BlockSpec(memory_space=pltpu.SMEM)
    vmem = pl.BlockSpec(memory_space=pltpu.VMEM)
    return pl.pallas_call(
        kernel,
        out_shape=[jax.ShapeDtypeStruct(shape, dtype) for shape, dtype in outs],
        in_specs=[smem if a.dtype == jnp.int32 else vmem for a in args],
        out_specs=[vmem for _ in outs],
        scratch_shapes=scratch,
        compiler_params=pltpu.CompilerParams(vmem_limit_bytes=40 * 1024 * 1024),
        cost_estimate=pl.CostEstimate(flops=1024, bytes_accessed=1024, transcendentals=0),
    )(*args)


def rope_tables(positions):
    half = HS // 2
    freqs = ROPE_BASE ** (-jnp.arange(half, dtype=jnp.float32) * 2.0 / HS)
    angles = freqs[:, None] * positions[None, :].astype(jnp.float32)
    return jnp.cos(angles), jnp.sin(angles)


def on_device(
    inputs,
    norm_gain,
    w_query,
    w_key,
    w_value,
    w_out,
    query_gain,
    key_gain,
    ffn_gain,
    w_gate,
    w_up,
    w_down,
    cotangent,
):
    f32, bf16 = jnp.float32, jnp.bfloat16
    tokens = inputs[0]
    out_grad = cotangent[0]
    rows, width = tokens.shape
    held = w_gate.shape[0]
    half_ffn = w_down.shape[0]
    ffn = 2 * half_ffn
    team = 2 * RING
    seen = team * rows
    quarter, few = width // 4, held // 4
    heads_width = GROUP * HS
    zl, hd = lax.axis_index("zl"), lax.axis_index("hd")
    tokens32 = tokens.astype(f32)

    by_head = lambda w: w.reshape(held, team, -1).transpose(1, 0, 2)
    joint_blocks = jnp.concatenate([by_head(w_query), by_head(w_key), by_head(w_value)], axis=2)
    joint_blocks = joint_blocks.reshape(2, RING, held, -1).swapaxes(0, 1).reshape(team, held, -1)
    joint_blocks = jnp.concatenate([joint_blocks, joint_blocks])
    normed = rms_forward(tokens32, norm_gain).astype(bf16)
    w_joint = exchange(joint_blocks, ("zl", "y", "hd"))
    normed_all = both_columns(gather_column(normed))
    grad_all = lax.all_gather(out_grad, TEAM, axis=0, tiled=True)
    my_rows = lambda w: lax.dynamic_slice_in_dim(w, lax.axis_index("x") * few, few, 0)
    gate_up_rows = call(pack_kernel, [((2 * team, 2 * few, ffn), bf16)], [], (my_rows(w_gate), my_rows(w_up)))[0]
    out_rows = in_order(w_out, swap(w_out, "zl"), "zl", 0)
    w_out_own = in_order(at(out_rows, hd), swap(at(out_rows, 1 - hd), "hd"), "hd", 0).reshape(heads_width, width)
    w_joint, w_out_own, gate_up_rows, normed_all = fence(w_joint, w_out_own, gate_up_rows, normed_all)
    w_joint = w_joint.reshape(width, -1)
    gate_up_rows = exchange(gate_up_rows, ("zl", "y", "hd"))
    down_other = jnp.concatenate([ring_z(w_down[: half_ffn // 2], 1), ring_z(w_down[half_ffn // 2 :], 3)])
    w_down_own = in_order(w_down, down_other, "zl", 0).reshape(ffn, width)

    joint = dot(w_joint, normed_all, (0, 1)).astype(bf16)
    other_kv, gate_up_rows = fence(swap(joint[heads_width:], "zl"), gate_up_rows)
    base = jnp.arange(seen, dtype=jnp.int32)
    cosine, sine = rope_tables(base + zl * seen)
    cosine2, sine2 = rope_tables(base + (1 - zl) * seen)
    half_flag = jnp.reshape(zl, (1,)).astype(jnp.int32)
    qgain, kgain = query_gain[:, None], key_gain[:, None]
    wide = seen // WIDE
    att, att32, lse, q_rot, kt_rot, k_rot, v_nat = call(
        attend_kernel,
        [
            ((heads_width, seen), bf16),
            ((wide, HS, ROWS), f32),
            ((wide, ROWS), f32),
            ((wide, HS, ROWS), bf16),
            ((HS, 2 * seen), bf16),
            ((2 * seen, HS), bf16),
            ((2 * seen, HS), bf16),
        ],
        [pltpu.VMEM((2 * HS, 2 * seen), bf16), pltpu.VMEM((wide, 2 * HS, ROWS), f32)],
        (half_flag, joint, other_kv, cosine, sine, cosine2, sine2, qgain, kgain),
    )
    gate_up_all = lax.all_gather(gate_up_rows, "x", axis=0, tiled=False)
    chip = chip_sum(dot(att, w_out_own, (0, 0)).astype(bf16))
    middle = tokens32 + column_sum(chip)
    gate_up_all = gate_up_all.reshape(RING, 2 * team, 2, few, ffn).transpose(2, 1, 0, 3, 4).reshape(2, width, ffn)
    w_gate_own, w_up_own = gate_up_all[0], gate_up_all[1]
    ffn_in = rms_forward(middle, ffn_gain).astype(bf16)
    ffn_all = both_columns(gather_column(ffn_in))
    hidden_grad = dot(grad_all, w_down_own, (1, 1))
    gate = dot(ffn_all, w_gate_own, (1, 0))
    up_val = dot(ffn_all, w_up_own, (1, 0))
    sigmoid = jax.nn.sigmoid(gate)
    hidden = (gate * sigmoid * up_val).astype(bf16)
    gate_grad = (hidden_grad * up_val * sigmoid * (1.0 + gate * (1.0 - sigmoid))).astype(bf16)
    up_grad = (hidden_grad * gate * sigmoid).astype(bf16)
    ffn_part = (dot(gate_grad, w_gate_own, (1, 1)) + dot(up_grad, w_up_own, (1, 1))).astype(bf16)
    chip, gate_right, up_right, hidden_left = fence(chip_sum(ffn_part), gate_grad, up_grad, hidden)
    ffn_in_grad = column_sum(chip)

    gate_up_terms = call(
        gate_up_terms_kernel,
        [((RING, 4 * team, few, ffn), bf16)],
        [],
        (ffn_all, gate_right, up_right),
    )[0]
    gate_up_sum = lax.psum_scatter(gate_up_terms, "x", scatter_dimension=0, tiled=False)
    down_terms = dot(hidden_left, grad_all, (0, 0)).astype(bf16).reshape(4, half_ffn // 2, width)
    down_came = exchange(down_terms, ("zl", "zh"))
    ffn_in_grad, _, _, hidden_last = fence(ffn_in_grad, gate_up_terms, down_terms, hidden)

    middle_part, ffn_gain_part = rms_backward(middle, ffn_gain, ffn_in_grad)
    middle_grad = out_grad.astype(f32) + middle_part
    branch_grad = middle_grad.astype(bf16)
    out_part = dot(hidden_last, w_down_own, (1, 0)).astype(bf16)
    column, out_part, down_came = fence(gather_column(branch_grad), out_part, down_came)
    out_sum = lax.psum_scatter(out_part, TEAM, scatter_dimension=0, tiled=True)
    branch_all = both_columns(column)
    att_grad = dot(w_out_own, branch_all, (1, 1)).astype(bf16)

    out_mine, out_other = call(
        out_terms_kernel,
        [((8, held // 8, width), bf16)] * 2,
        [],
        (jnp.reshape(hd, (1,)).astype(jnp.int32), att, branch_all),
    )
    out_pieces = in_order(out_mine, swap(out_other, "hd"), "hd", 1)
    att_grad, out_pieces = fence(att_grad, out_pieces)
    out_came = exchange(out_pieces.reshape(16, held // 8, width), SUMMED)
    q_grad, kv_own, kv_other, qgain_part = call(
        attend_back_kernel,
        [
            ((heads_width, seen), bf16),
            ((2 * HS, seen), f32),
            ((2 * HS, seen), bf16),
            ((HS, WIDE), f32),
        ],
        [
            pltpu.VMEM((2 * seen, HS), f32),
            pltpu.VMEM((2 * seen, HS), f32),
            pltpu.VMEM((wide, HS, ROWS), f32),
            pltpu.VMEM((wide, HS, ROWS), bf16),
            pltpu.VMEM((2 * wide, ROWS), f32),
        ],
        (half_flag, joint, att_grad, cosine, sine, qgain, att32, lse, q_rot, kt_rot, k_rot, v_nat),
    )
    gate_up_came = exchange(gate_up_sum, ("zh", "zl") + TEAM)
    kv_came, gate_up_came, att, down_came = fence(swap(kv_other, "zl"), gate_up_came, att, down_came)
    joint_grad, kgain_part = call(
        key_back_kernel,
        [(joint.shape, bf16), ((HS, 1), f32)],
        [],
        (joint, kv_own, kv_came, cosine, sine, kgain, q_grad),
    )
    normed_part = dot(joint_grad, w_joint, (0, 1))
    norm_gain_part = jnp.sum(normed_part * normed_all.astype(f32), axis=0) / norm_gain
    normed_part = normed_part.astype(bf16)
    gains = [norm_gain_part, ffn_gain_part, jnp.sum(qgain_part, axis=1), kgain_part[:, 0]]
    joint_width = joint.shape[0]
    gains = jnp.concatenate([*gains, jnp.zeros((16 * joint_width - 2 * width - 2 * HS,), f32)])
    gains = gains.reshape(8, 2, joint_width)
    high = lax.optimization_barrier(gains.astype(bf16)).astype(f32)
    joint_pieces = call(
        joint_terms_kernel,
        [((16 * team, held // 8 + 4, joint_width), bf16)],
        [],
        (normed_all, joint_grad, jnp.concatenate([high, gains - high], axis=1)),
    )[0]
    joint_pieces, gate_up_came, out_came, normed_part, down_came = fence(
        joint_pieces, gate_up_came, out_came, normed_part, down_came
    )
    joint_came = exchange(joint_pieces, SUMMED + TEAM)
    gate_up_mine = sum_first(gate_up_came.reshape(4, team * few, ffn))
    gate_up_whole = lax.all_gather(gate_up_mine, ("x", "zh"), axis=0, tiled=False)
    gate_up_whole = gate_up_whole.reshape(RING, 2, team, few, ffn)
    down_mine = sum_x(sum_first(down_came).reshape(4, half_ffn // 8, width))
    ready = jnp.concatenate([down_mine, sum_first(out_came)])
    ready = jnp.concatenate([ready[:, i * quarter : (i + 1) * quarter] for i in range(4)])
    joint_came, ready, chip = fence(joint_came, ready, chip_sum(normed_part))
    joint_mine = call(joint_sum_kernel, [((held + 8, quarter), bf16)], [], (joint_came,))[0]
    pieces, (normed_grad,) = spread(jnp.concatenate([ready, joint_mine]), column_sum(chip))
    output = (middle + out_sum.astype(f32)).astype(bf16)
    input_part, _ = rms_backward(tokens32, norm_gain, normed_grad)
    input_grad = middle_grad + input_part
    block = lambda shape, index: pl.BlockSpec(shape, index)
    w_gate_grad, w_up_grad = pl.pallas_call(
        unpack_ffn_kernel,
        grid=(RING,),
        in_specs=[block((1, 2, team, few, ffn), lambda i: (i, 0, 0, 0, 0))],
        out_specs=[block((few, team * ffn), lambda i: (i, 0))] * 2,
        out_shape=[jax.ShapeDtypeStruct((held, team * ffn), f32)] * 2,
        compiler_params=pltpu.CompilerParams(vmem_limit_bytes=40 * 1024 * 1024),
    )(gate_up_whole)
    shapes = [(half_ffn, width), (held, width)] + [(held, w.shape[1]) for w in (w_query, w_key, w_value)]
    shapes.append((8, 2, joint_width))
    w_down_grad, w_out_grad, w_query_grad, w_key_grad, w_value_grad, gains = call(
        unpack_kernel, [(shape, f32) for shape in shapes], [], (pieces,)
    )

    gains = gains.reshape(-1)
    return (
        output[None],
        input_grad[None],
        gains[:width],
        w_query_grad,
        w_key_grad,
        w_value_grad,
        w_out_grad,
        gains[2 * width : 2 * width + HS],
        gains[2 * width + HS : 2 * width + 2 * HS],
        gains[width : 2 * width],
        w_gate_grad,
        w_up_grad,
        w_down_grad,
    )


def solution(mesh):
    fine = Mesh(mesh.devices.reshape(4, 2, 2, 4, 2), ("x", "zh", "zl", "y", "hd"))
    by_tokens = P(("x", "zh"), ("zl", "y", "hd"), None)
    by_rows = P(("zl", "y", "hd"), None)
    return jax.shard_map(
        on_device,
        mesh=fine,
        in_specs=(
            by_tokens, P(), by_rows, by_rows, by_rows, by_rows, P(), P(), P(), by_rows, by_rows, by_rows, by_tokens
        ),
        out_specs=(
            by_tokens, by_tokens, P(), by_rows, by_rows, by_rows, by_rows, P(), P(), P(), by_rows, by_rows, by_rows
        ),
        check_vma=False,
    )
```

```python
import jax
import jax.numpy as jnp
from jax import lax
from jax.experimental import pallas as pl
from jax.experimental.pallas import tpu as pltpu
from jax.sharding import Mesh, PartitionSpec as P

HQ = 24
HK = 8
HS = 64
GROUP = HQ // HK

EPSILON = 1e-05
ROPE_BASE = 1000000.0
SCORE_SCALE = 0.125

RING = 4
STEPS = (2, 1, 3)
BLOCK = 128
WIDE = 2 * BLOCK
ROWS = GROUP * WIDE


def rms_forward(values, gain):
    factor = lax.rsqrt(jnp.mean(values * values, axis=-1, keepdims=True) + EPSILON)
    return values * factor * gain


def rms_backward(values, gain, grad_out):
    factor = lax.rsqrt(jnp.mean(values * values, axis=-1, keepdims=True) + EPSILON)
    normal = values * factor
    scaled = grad_out * gain
    grad_in = factor * (scaled - normal * jnp.mean(scaled * normal, axis=-1, keepdims=True))
    grad_gain = jnp.sum(grad_out * normal, axis=0)
    return (grad_in, grad_gain)


def dot(left, right, contract):
    return lax.dot_general(
        left, right, (((contract[0],), (contract[1],)), ((), ())), preferred_element_type=jnp.float32
    )


SUMMED = ("x", "zh", "zl")
TEAM = ("y", "hd")


def at(array, index, axis=0):
    return lax.dynamic_index_in_dim(array, index, axis, keepdims=False)


def put(whole, array, *index):
    lead = (1,) * len(index)
    return lax.dynamic_update_slice(whole, array.reshape(lead + array.shape), index + (0,) * array.ndim)


def fence(*values):
    return lax.optimization_barrier(values)


def ring(array, axis, step):
    return lax.ppermute(array, axis, [(i, (i + step) % RING) for i in range(RING)])


def ring_z(array, step):
    return ring(array, ("zh", "zl"), step)


def swap(array, axis):
    return lax.ppermute(array, axis, [(0, 1), (1, 0)])


def in_order(mine, other, axis_name, axis):
    first = lax.axis_index(axis_name) == 0
    return jnp.stack([jnp.where(first, mine, other), jnp.where(first, other, mine)], axis=axis)


def gather_column(block):
    y = lax.axis_index("y")
    column = put(jnp.zeros((RING, *block.shape), block.dtype), block, y)
    for step in STEPS:
        column = put(column, ring(block, "y", step), (y - step) % RING)
    return column


def both_columns(column):
    return in_order(column, swap(column, "hd"), "hd", 1).reshape(-1, column.shape[-1])


def chip_sum(parts):
    hd = lax.axis_index("hd")
    parts = parts.reshape(RING, 2, BLOCK, -1)
    total = at(parts, hd, 1).astype(jnp.float32) + swap(at(parts, 1 - hd, 1), "hd").astype(jnp.float32)
    return total.astype(jnp.bfloat16)


def column_sum(chip):
    y = lax.axis_index("y")
    arrived = [ring(at(chip, (y + step) % RING), "y", step) for step in STEPS]
    return sum((came.astype(jnp.float32) for came in arrived), at(chip, y).astype(jnp.float32))


def exchange(blocks, axes):
    return lax.all_to_all(blocks, axes, split_axis=0, concat_axis=0, tiled=True)


def sum_x(pieces):
    x = lax.axis_index("x")
    arrived = [ring(at(pieces, (x + step) % RING), "x", step) for step in STEPS]
    return sum_first([at(pieces, x), *arrived])


def sum_first(arrived):
    return sum(arrived[i].astype(jnp.float32) for i in range(len(arrived))).astype(jnp.bfloat16)


def both_zh(piece):
    return in_order(piece, swap(piece, "zh"), "zh", 0)


def spread(piece, *beside):
    x = lax.axis_index("x")
    pair = both_zh(piece)
    far, after, before = [ring(pair, "x", step) for step in STEPS]
    far, *beside = fence(far, *beside)
    whole = put(jnp.zeros((RING, *pair.shape), pair.dtype), pair, x)
    for step, block in zip(STEPS, (far, after, before)):
        whole = put(whole, block, (x - step) % RING)
    return whole, beside


def turn(values, cosine, sine):
    first, second = values[: HS // 2], values[HS // 2 :]
    return jnp.concatenate([first * cosine - second * sine, second * cosine + first * sine], axis=0)


def unturn(grads, cosine, sine):
    first, second = grads[: HS // 2], grads[HS // 2 :]
    return jnp.concatenate([first * cosine + second * sine, second * cosine - first * sine], axis=0)


def head_norm(values, gain):
    return values * lax.rsqrt(jnp.mean(values * values, axis=0, keepdims=True) + EPSILON) * gain


def head_norm_back(values, gain, grad_out):
    factor = lax.rsqrt(jnp.mean(values * values, axis=0, keepdims=True) + EPSILON)
    normal = values * factor
    scaled = grad_out * gain
    grad_in = factor * (scaled - normal * jnp.mean(scaled * normal, axis=0, keepdims=True))
    return grad_in, grad_out * normal


def allowed_keys():
    key = lax.broadcasted_iota(jnp.int32, (WIDE, ROWS), 0)
    query = lax.broadcasted_iota(jnp.int32, (WIDE, ROWS), 1) % WIDE
    return key <= query


def place_of(head):
    return head % RING * 2 + head // RING


def attend_kernel(
    half_ref, own_ref, other_ref, cos_ref, sin_ref, cos2_ref, sin2_ref, qgain_ref, kgain_ref,
    att_ref, out_ref, lse_ref, q_ref, kt_ref, k_ref, v_ref, vt_ref, total_ref,
):
    seen = own_ref.shape[1]
    count = seen // WIDE
    qgain, kgain = qgain_ref[...], kgain_ref[...]
    vt_ref[HS:, :] = jnp.ones((HS, vt_ref.shape[1]), jnp.bfloat16)
    for c in range(count):
        cols = slice(c * WIDE, (c + 1) * WIDE)
        sides = (
            (own_ref[GROUP * HS :, cols], cos_ref[:, cols], sin_ref[:, cols]),
            (other_ref[:, cols], cos2_ref[:, cols], sin2_ref[:, cols]),
        )
        for side, (pair, cosine, sine) in enumerate(sides):
            pair = pair.astype(jnp.float32)
            place = slice(side * seen + c * WIDE, side * seen + (c + 1) * WIDE)
            key = turn(head_norm(pair[:HS], kgain), cosine, sine)
            kt_ref[:, place] = key.astype(jnp.bfloat16)
            k_ref[place, :] = key.T.astype(jnp.bfloat16)
            vt_ref[:HS, place] = pair[HS:].astype(jnp.bfloat16)
            v_ref[place, :] = pair[HS:].T.astype(jnp.bfloat16)
        for head in range(GROUP):
            query = own_ref[head * HS : (head + 1) * HS, cols].astype(jnp.float32)
            query = turn(head_norm(query, qgain), cos_ref[:, cols], sin_ref[:, cols])
            q_ref[c, :, head * WIDE : (head + 1) * WIDE] = (query * SCORE_SCALE).astype(jnp.bfloat16)
    allowed = allowed_keys()

    def terms(i, start, masked):
        keys = slice(start, start + WIDE)
        weights = jnp.exp(dot(k_ref[keys, :], q_ref[i], (1, 0)))
        if masked:
            weights = jnp.where(allowed, weights, 0.0)
        return dot(vt_ref[:, keys], weights.astype(jnp.bfloat16), (1, 0))

    for i in range(count):
        total_ref[i] = sum(terms(i, c * WIDE, c == i) for c in range(i + 1))

    @pl.when(half_ref[0] == 1)
    def _():
        for i in range(count):
            total_ref[i] += sum(terms(i, seen + c * WIDE, False) for c in range(count))

    for i in range(count):
        total = total_ref[i]
        norm = total[HS : HS + 1]
        result = total[:HS] / norm
        lse_ref[i : i + 1, :] = jnp.log(norm)
        out_ref[i] = result
        for head in range(GROUP):
            part = result[:, head * WIDE : (head + 1) * WIDE].astype(jnp.bfloat16)
            att_ref[head * HS : (head + 1) * HS, i * WIDE : (i + 1) * WIDE] = part


def attend_back_kernel(
    half_ref, own_ref, grad_ref, cos_ref, sin_ref, qgain_ref, out_ref, lse_ref, q_ref, kt_ref, k_ref, v_ref,
    qgrad_ref, kv_own_ref, kv_other_ref, gain_ref, dk_ref, dv_ref, dq_ref, g_ref, delta_ref,
):
    seen = own_ref.shape[1]
    count = seen // WIDE
    qgain = qgain_ref[...]
    allowed = allowed_keys()

    def terms(i, start, masked):
        keys = slice(start, start + WIDE)
        query, grad = q_ref[i], g_ref[i]
        weights = jnp.exp(dot(k_ref[keys, :], query, (1, 0)) - lse_ref[i : i + 1, :])
        if masked:
            weights = jnp.where(allowed, weights, 0.0)
        prob_grad = dot(v_ref[keys, :], grad, (1, 0))
        score_grad = (weights * (prob_grad - delta_ref[i : i + 1, :])).astype(jnp.bfloat16)
        dv_ref[keys, :] += dot(weights.astype(jnp.bfloat16), grad, (1, 1))
        dk_ref[keys, :] += dot(score_grad, query, (1, 1))
        return dot(kt_ref[:, keys], score_grad, (1, 0))

    dk_ref[...] = jnp.zeros_like(dk_ref)
    dv_ref[...] = jnp.zeros_like(dv_ref)
    for i in range(count):
        for head in range(GROUP):
            g_ref[i, :, head * WIDE : (head + 1) * WIDE] = grad_ref[
                head * HS : (head + 1) * HS, i * WIDE : (i + 1) * WIDE
            ]
        delta_ref[i : i + 1, :] = jnp.sum(g_ref[i].astype(jnp.float32) * out_ref[i], axis=0, keepdims=True)
        dq_ref[i] = sum(terms(i, c * WIDE, c == i) for c in range(i + 1))

    @pl.when(half_ref[0] == 1)
    def _():
        for i in range(count):
            dq_ref[i] += sum(terms(i, seen + c * WIDE, False) for c in range(count))

    gain_total = jnp.zeros((HS, WIDE), jnp.float32)
    for i in range(count):
        cols = slice(i * WIDE, (i + 1) * WIDE)
        for head in range(GROUP):
            turned = dq_ref[i, :, head * WIDE : (head + 1) * WIDE] * SCORE_SCALE
            back = unturn(turned, cos_ref[:, cols], sin_ref[:, cols])
            rows = slice(head * HS, (head + 1) * HS)
            lin, gain_part = head_norm_back(own_ref[rows, cols].astype(jnp.float32), qgain, back)
            qgrad_ref[rows, cols] = lin.astype(jnp.bfloat16)
            gain_total = gain_total + gain_part
        for source, rows in ((dk_ref, slice(0, HS)), (dv_ref, slice(HS, 2 * HS))):
            kv_own_ref[rows, cols] = source[i * WIDE : (i + 1) * WIDE, :].T
            kv_other_ref[rows, cols] = source[seen + i * WIDE : seen + (i + 1) * WIDE, :].T.astype(jnp.bfloat16)
    gain_ref[...] = gain_total


def key_back_kernel(
    own_ref, kv_own_ref, kv_came_ref, cos_ref, sin_ref, kgain_ref, qgrad_ref, grad_ref, gain_ref
):
    total = kv_own_ref[...] + kv_came_ref[...].astype(jnp.float32)
    back = unturn(total[:HS], cos_ref[...], sin_ref[...])
    key = own_ref[GROUP * HS : (GROUP + 1) * HS, :].astype(jnp.float32)
    lin, gain_part = head_norm_back(key, kgain_ref[...], back)
    grad_ref[: GROUP * HS, :] = qgrad_ref[...]
    grad_ref[GROUP * HS : (GROUP + 1) * HS, :] = lin.astype(jnp.bfloat16)
    grad_ref[(GROUP + 1) * HS :, :] = total[HS:].astype(jnp.bfloat16)
    gain_ref[...] = jnp.sum(gain_part, axis=1, keepdims=True)


def pack_kernel(gate_ref, up_ref, out_ref):
    count, rows, ffn = out_ref.shape
    team, half, few = count // 2, ffn // 2, rows // 2
    for ref, top in ((gate_ref, 0), (up_ref, few)):
        for place in range(team):
            parts = [
                ref[:, (zl * team + place) * half : (zl * team + place + 1) * half].astype(jnp.float32)
                for zl in range(2)
            ]
            block = jnp.concatenate(parts, axis=1).astype(jnp.bfloat16)
            out_ref[place, top : top + few, :] = block
            out_ref[team + place, top : top + few, :] = block


def gate_up_terms_kernel(ffn_ref, gate_ref, up_ref, out_ref):
    few, ffn = out_ref.shape[2:]
    chunk = RING * RING * few
    for c in range(ffn_ref.shape[1] // chunk):
        left = ffn_ref[:, c * chunk : (c + 1) * chunk]
        for side, ref in enumerate((gate_ref, up_ref)):
            terms = dot(left, ref[...], (0, 0)).reshape(RING, RING, few, ffn).astype(jnp.bfloat16)
            for row in range(RING):
                for quarter in range(RING):
                    out_ref[quarter, (side * 2 + c // 2) * 8 + c % 2 * RING + row] = terms[row, quarter]


def out_terms_kernel(hd_ref, att_ref, grad_ref, mine_ref, other_ref):
    pieces, few, _ = mine_ref.shape
    terms = dot(att_ref[...], grad_ref[...], (1, 0))
    for hd in range(2):
        for piece in range(pieces):
            start = (hd * pieces + piece) * few
            block = terms[start : start + few].astype(jnp.bfloat16)

            @pl.when(hd_ref[0] == hd)
            def _():
                mine_ref[piece] = block

            @pl.when(hd_ref[0] != hd)
            def _():
                other_ref[piece] = block


def joint_terms_kernel(normed_ref, grad_ref, gains_ref, out_ref):
    team, half = 2 * RING, normed_ref.shape[1] // 2
    few = half // (8 * team)
    for zl in range(2):
        terms = dot(normed_ref[:, zl * half : (zl + 1) * half], grad_ref[...], (0, 1))
        for place in range(team):
            for piece in range(8):
                start = (place * 8 + piece) * few
                block = jnp.concatenate([terms[start : start + few], gains_ref[piece]], axis=0)
                out_ref[(piece * 2 + zl) * team + place] = block.astype(jnp.bfloat16)


def joint_sum_kernel(came_ref, out_ref):
    count, rows, cols = came_ref.shape
    team = 2 * RING
    few = rows - 4
    gains = jnp.zeros((4, cols), jnp.float32)
    parts = []
    for place in range(team):
        total = came_ref[place].astype(jnp.float32)
        for source in range(1, count // team):
            total = total + came_ref[source * team + place].astype(jnp.float32)
        parts.append(total[:few])
        gains = gains + total[few:]
    gains = gains[:2] + gains[2:]
    high = gains.astype(jnp.bfloat16).astype(jnp.float32)
    parts += [high, gains - high, jnp.zeros((4, cols), jnp.float32)]
    whole = jnp.concatenate(parts, axis=0)
    spare = jnp.zeros((whole.shape[0], out_ref.shape[1] - cols), jnp.float32)
    out_ref[...] = jnp.concatenate([whole, spare], axis=1).astype(jnp.bfloat16)


def unpack_ffn_kernel(pieces_ref, gate_ref, up_ref):
    team, few, ffn = pieces_ref.shape[2:]
    half = ffn // 2
    for side, ref in enumerate((gate_ref, up_ref)):
        blocks = [pieces_ref[0, side, place].astype(jnp.float32) for place in range(team)]
        ref[...] = jnp.concatenate(
            [block[:, zl * half : (zl + 1) * half] for zl in range(2) for block in blocks], axis=1
        )


def unpack_kernel(pieces_ref, w_down_ref, w_out_ref, w_query_ref, w_key_ref, w_value_ref, gains_ref):
    team, cols = 2 * RING, gains_ref.shape[2]
    down, out, few = w_down_ref.shape[0] // 8, w_out_ref.shape[0] // 8, w_query_ref.shape[0] // 8
    rows = down + out
    down_rows, out_rows, joint_rows = [], [], []
    for x in range(RING):
        for zh in range(2):
            piece = pieces_ref[x, zh].astype(jnp.float32)
            ready = jnp.concatenate([piece[i * rows : (i + 1) * rows] for i in range(RING)], axis=1)
            down_rows.append(ready[:down])
            out_rows.append(ready[down:])
            heads = [RING * rows + place_of(head) * few for head in range(team)]
            joint_rows.append([piece[start : start + few] for start in heads])
            gains = piece[RING * rows + team * few :, :cols]
            gains_ref[x * 2 + zh] = gains[:2] + gains[2:4]
    w_down_ref[...] = jnp.concatenate([down_rows[x * 2 + zh] for zh in range(2) for x in range(RING)], axis=0)
    w_out_ref[...] = jnp.concatenate(out_rows, axis=0)
    targets = (w_query_ref, 0, GROUP * HS), (w_key_ref, GROUP * HS, HS), (w_value_ref, (GROUP + 1) * HS, HS)
    for target, start, size in targets:
        parts = [
            jnp.concatenate([block[:, start : start + size] for block in blocks], axis=1) for blocks in joint_rows
        ]
        target[...] = jnp.concatenate(parts, axis=0)


def call(kernel, outs, scratch, args):
    smem = pl.BlockSpec(memory_space=pltpu.SMEM)
    vmem = pl.BlockSpec(memory_space=pltpu.VMEM)
    return pl.pallas_call(
        kernel,
        out_shape=[jax.ShapeDtypeStruct(shape, dtype) for shape, dtype in outs],
        in_specs=[smem if a.dtype == jnp.int32 else vmem for a in args],
        out_specs=[vmem for _ in outs],
        scratch_shapes=scratch,
        compiler_params=pltpu.CompilerParams(vmem_limit_bytes=40 * 1024 * 1024),
        cost_estimate=pl.CostEstimate(flops=1024, bytes_accessed=1024, transcendentals=0),
    )(*args)


def rope_tables(positions):
    half = HS // 2
    freqs = ROPE_BASE ** (-jnp.arange(half, dtype=jnp.float32) * 2.0 / HS)
    angles = freqs[:, None] * positions[None, :].astype(jnp.float32)
    return jnp.cos(angles), jnp.sin(angles)


def on_device(
    inputs,
    norm_gain,
    w_query,
    w_key,
    w_value,
    w_out,
    query_gain,
    key_gain,
    ffn_gain,
    w_gate,
    w_up,
    w_down,
    cotangent,
):
    f32, bf16 = jnp.float32, jnp.bfloat16
    tokens = inputs[0]
    out_grad = cotangent[0]
    rows, width = tokens.shape
    held = w_gate.shape[0]
    half_ffn = w_down.shape[0]
    ffn = 2 * half_ffn
    team = 2 * RING
    seen = team * rows
    quarter, few = width // 4, held // 4
    heads_width = GROUP * HS
    zl, hd = lax.axis_index("zl"), lax.axis_index("hd")
    tokens32 = tokens.astype(f32)

    by_head = lambda w: w.reshape(held, team, -1).transpose(1, 0, 2)
    joint_blocks = jnp.concatenate([by_head(w_query), by_head(w_key), by_head(w_value)], axis=2)
    joint_blocks = joint_blocks.reshape(2, RING, held, -1).swapaxes(0, 1).reshape(team, held, -1)
    joint_blocks = jnp.concatenate([joint_blocks, joint_blocks])
    normed = rms_forward(tokens32, norm_gain).astype(bf16)
    w_joint = exchange(joint_blocks, ("zl", "y", "hd"))
    normed_all = both_columns(gather_column(normed))
    grad_all = lax.all_gather(out_grad, TEAM, axis=0, tiled=True)
    my_rows = lambda w: lax.dynamic_slice_in_dim(w, lax.axis_index("x") * few, few, 0)
    gate_up_rows = call(pack_kernel, [((2 * team, 2 * few, ffn), bf16)], [], (my_rows(w_gate), my_rows(w_up)))[0]
    out_rows = in_order(w_out, swap(w_out, "zl"), "zl", 0)
    w_out_own = in_order(at(out_rows, hd), swap(at(out_rows, 1 - hd), "hd"), "hd", 0).reshape(heads_width, width)
    w_joint, w_out_own, gate_up_rows, normed_all = fence(w_joint, w_out_own, gate_up_rows, normed_all)
    w_joint = w_joint.reshape(width, -1)
    gate_up_rows = exchange(gate_up_rows, ("zl", "y", "hd"))
    down_other = jnp.concatenate([ring_z(w_down[: half_ffn // 2], 1), ring_z(w_down[half_ffn // 2 :], 3)])
    w_down_own = in_order(w_down, down_other, "zl", 0).reshape(ffn, width)

    joint = dot(w_joint, normed_all, (0, 1)).astype(bf16)
    other_kv, gate_up_rows = fence(swap(joint[heads_width:], "zl"), gate_up_rows)
    base = jnp.arange(seen, dtype=jnp.int32)
    cosine, sine = rope_tables(base + zl * seen)
    cosine2, sine2 = rope_tables(base + (1 - zl) * seen)
    half_flag = jnp.reshape(zl, (1,)).astype(jnp.int32)
    qgain, kgain = query_gain[:, None], key_gain[:, None]
    wide = seen // WIDE
    att, att32, lse, q_rot, kt_rot, k_rot, v_nat = call(
        attend_kernel,
        [
            ((heads_width, seen), bf16),
            ((wide, HS, ROWS), f32),
            ((wide, ROWS), f32),
            ((wide, HS, ROWS), bf16),
            ((HS, 2 * seen), bf16),
            ((2 * seen, HS), bf16),
            ((2 * seen, HS), bf16),
        ],
        [pltpu.VMEM((2 * HS, 2 * seen), bf16), pltpu.VMEM((wide, 2 * HS, ROWS), f32)],
        (half_flag, joint, other_kv, cosine, sine, cosine2, sine2, qgain, kgain),
    )
    gate_up_all = lax.all_gather(gate_up_rows, "x", axis=0, tiled=False)
    chip = chip_sum(dot(att, w_out_own, (0, 0)).astype(bf16))
    middle = tokens32 + column_sum(chip)
    gate_up_all = gate_up_all.reshape(RING, 2 * team, 2, few, ffn).transpose(2, 1, 0, 3, 4).reshape(2, width, ffn)
    w_gate_own, w_up_own = gate_up_all[0], gate_up_all[1]
    ffn_in = rms_forward(middle, ffn_gain).astype(bf16)
    ffn_all = both_columns(gather_column(ffn_in))
    hidden_grad = dot(grad_all, w_down_own, (1, 1))
    gate = dot(ffn_all, w_gate_own, (1, 0))
    up_val = dot(ffn_all, w_up_own, (1, 0))
    sigmoid = jax.nn.sigmoid(gate)
    hidden = (gate * sigmoid * up_val).astype(bf16)
    gate_grad = (hidden_grad * up_val * sigmoid * (1.0 + gate * (1.0 - sigmoid))).astype(bf16)
    up_grad = (hidden_grad * gate * sigmoid).astype(bf16)
    ffn_part = (dot(gate_grad, w_gate_own, (1, 1)) + dot(up_grad, w_up_own, (1, 1))).astype(bf16)
    chip, gate_right, up_right, hidden_left = fence(chip_sum(ffn_part), gate_grad, up_grad, hidden)
    ffn_in_grad = column_sum(chip)

    gate_up_terms = call(
        gate_up_terms_kernel,
        [((RING, 4 * team, few, ffn), bf16)],
        [],
        (ffn_all, gate_right, up_right),
    )[0]
    gate_up_sum = lax.psum_scatter(gate_up_terms, "x", scatter_dimension=0, tiled=False)
    down_terms = dot(hidden_left, grad_all, (0, 0)).astype(bf16).reshape(4, half_ffn // 2, width)
    down_came = exchange(down_terms, ("zl", "zh"))
    ffn_in_grad, _, _, hidden_last = fence(ffn_in_grad, gate_up_terms, down_terms, hidden)

    middle_part, ffn_gain_part = rms_backward(middle, ffn_gain, ffn_in_grad)
    middle_grad = out_grad.astype(f32) + middle_part
    branch_grad = middle_grad.astype(bf16)
    out_part = dot(hidden_last, w_down_own, (1, 0)).astype(bf16)
    column, out_part, down_came = fence(gather_column(branch_grad), out_part, down_came)
    out_sum = lax.psum_scatter(out_part, TEAM, scatter_dimension=0, tiled=True)
    branch_all = both_columns(column)
    att_grad = dot(w_out_own, branch_all, (1, 1)).astype(bf16)

    out_mine, out_other = call(
        out_terms_kernel,
        [((8, held // 8, width), bf16)] * 2,
        [],
        (jnp.reshape(hd, (1,)).astype(jnp.int32), att, branch_all),
    )
    out_pieces = in_order(out_mine, swap(out_other, "hd"), "hd", 1)
    att_grad, out_pieces = fence(att_grad, out_pieces)
    out_came = exchange(out_pieces.reshape(16, held // 8, width), SUMMED)
    q_grad, kv_own, kv_other, qgain_part = call(
        attend_back_kernel,
        [
            ((heads_width, seen), bf16),
            ((2 * HS, seen), f32),
            ((2 * HS, seen), bf16),
            ((HS, WIDE), f32),
        ],
        [
            pltpu.VMEM((2 * seen, HS), f32),
            pltpu.VMEM((2 * seen, HS), f32),
            pltpu.VMEM((wide, HS, ROWS), f32),
            pltpu.VMEM((wide, HS, ROWS), bf16),
            pltpu.VMEM((2 * wide, ROWS), f32),
        ],
        (half_flag, joint, att_grad, cosine, sine, qgain, att32, lse, q_rot, kt_rot, k_rot, v_nat),
    )
    gate_up_came = exchange(gate_up_sum, ("zh", "zl") + TEAM)
    kv_came, gate_up_came, att, down_came = fence(swap(kv_other, "zl"), gate_up_came, att, down_came)
    joint_grad, kgain_part = call(
        key_back_kernel,
        [(joint.shape, bf16), ((HS, 1), f32)],
        [],
        (joint, kv_own, kv_came, cosine, sine, kgain, q_grad),
    )
    normed_part = dot(joint_grad, w_joint, (0, 1))
    norm_gain_part = jnp.sum(normed_part * normed_all.astype(f32), axis=0) / norm_gain
    normed_part = normed_part.astype(bf16)
    gains = [norm_gain_part, ffn_gain_part, jnp.sum(qgain_part, axis=1), kgain_part[:, 0]]
    joint_width = joint.shape[0]
    gains = jnp.concatenate([*gains, jnp.zeros((16 * joint_width - 2 * width - 2 * HS,), f32)])
    gains = gains.reshape(8, 2, joint_width)
    high = lax.optimization_barrier(gains.astype(bf16)).astype(f32)
    joint_pieces = call(
        joint_terms_kernel,
        [((16 * team, held // 8 + 4, joint_width), bf16)],
        [],
        (normed_all, joint_grad, jnp.concatenate([high, gains - high], axis=1)),
    )[0]
    joint_pieces, gate_up_came, out_came, normed_part, down_came = fence(
        joint_pieces, gate_up_came, out_came, normed_part, down_came
    )
    joint_came = exchange(joint_pieces, SUMMED + TEAM)
    gate_up_mine = sum_first(gate_up_came.reshape(4, team * few, ffn))
    gate_up_whole = lax.all_gather(both_zh(gate_up_mine), "x", axis=0, tiled=False)
    gate_up_whole = gate_up_whole.reshape(RING, 2, team, few, ffn)
    down_mine = sum_x(sum_first(down_came).reshape(4, half_ffn // 8, width))
    ready = jnp.concatenate([down_mine, sum_first(out_came)])
    ready = jnp.concatenate([ready[:, i * quarter : (i + 1) * quarter] for i in range(4)])
    joint_came, ready, chip = fence(joint_came, ready, chip_sum(normed_part))
    joint_mine = call(joint_sum_kernel, [((held + 8, quarter), bf16)], [], (joint_came,))[0]
    input_part, _ = rms_backward(tokens32, norm_gain, column_sum(chip))
    output = (middle + out_sum.astype(f32)).astype(bf16)
    pieces, (input_grad, output) = spread(
        jnp.concatenate([ready, joint_mine]), middle_grad + input_part, output
    )
    block = lambda shape, index: pl.BlockSpec(shape, index)
    w_gate_grad, w_up_grad = pl.pallas_call(
        unpack_ffn_kernel,
        grid=(RING,),
        in_specs=[block((1, 2, team, few, ffn), lambda i: (i, 0, 0, 0, 0))],
        out_specs=[block((few, team * ffn), lambda i: (i, 0))] * 2,
        out_shape=[jax.ShapeDtypeStruct((held, team * ffn), f32)] * 2,
        compiler_params=pltpu.CompilerParams(vmem_limit_bytes=40 * 1024 * 1024),
    )(gate_up_whole)
    shapes = [(half_ffn, width), (held, width)] + [(held, w.shape[1]) for w in (w_query, w_key, w_value)]
    shapes.append((8, 2, joint_width))
    w_down_grad, w_out_grad, w_query_grad, w_key_grad, w_value_grad, gains = call(
        unpack_kernel, [(shape, f32) for shape in shapes], [], (pieces,)
    )

    gains = gains.reshape(-1)
    return (
        output[None],
        input_grad[None],
        gains[:width],
        w_query_grad,
        w_key_grad,
        w_value_grad,
        w_out_grad,
        gains[2 * width : 2 * width + HS],
        gains[2 * width + HS : 2 * width + 2 * HS],
        gains[width : 2 * width],
        w_gate_grad,
        w_up_grad,
        w_down_grad,
    )


def solution(mesh):
    fine = Mesh(mesh.devices.reshape(4, 2, 2, 4, 2), ("x", "zh", "zl", "y", "hd"))
    by_tokens = P(("x", "zh"), ("zl", "y", "hd"), None)
    by_rows = P(("zl", "y", "hd"), None)
    return jax.shard_map(
        on_device,
        mesh=fine,
        in_specs=(
            by_tokens, P(), by_rows, by_rows, by_rows, by_rows, P(), P(), P(), by_rows, by_rows, by_rows, by_tokens
        ),
        out_specs=(
            by_tokens, by_tokens, P(), by_rows, by_rows, by_rows, by_rows, P(), P(), P(), by_rows, by_rows, by_rows
        ),
        check_vma=False,
    )
```

```python
import jax
import jax.numpy as jnp
from jax import lax
from jax.experimental import pallas as pl
from jax.experimental.pallas import tpu as pltpu
from jax.sharding import Mesh, PartitionSpec as P

HQ = 24
HK = 8
HS = 64
GROUP = HQ // HK

EPSILON = 1e-05
ROPE_BASE = 1000000.0
SCORE_SCALE = 0.125

RING = 4
STEPS = (2, 1, 3)
BLOCK = 128
WIDE = 2 * BLOCK
ROWS = GROUP * WIDE


def rms_forward(values, gain):
    factor = lax.rsqrt(jnp.mean(values * values, axis=-1, keepdims=True) + EPSILON)
    return values * factor * gain


def rms_backward(values, gain, grad_out):
    factor = lax.rsqrt(jnp.mean(values * values, axis=-1, keepdims=True) + EPSILON)
    normal = values * factor
    scaled = grad_out * gain
    grad_in = factor * (scaled - normal * jnp.mean(scaled * normal, axis=-1, keepdims=True))
    grad_gain = jnp.sum(grad_out * normal, axis=0)
    return (grad_in, grad_gain)


def dot(left, right, contract):
    return lax.dot_general(
        left, right, (((contract[0],), (contract[1],)), ((), ())), preferred_element_type=jnp.float32
    )


SUMMED = ("x", "zh", "zl")
TEAM = ("y", "hd")


def at(array, index, axis=0):
    return lax.dynamic_index_in_dim(array, index, axis, keepdims=False)


def put(whole, array, *index):
    lead = (1,) * len(index)
    return lax.dynamic_update_slice(whole, array.reshape(lead + array.shape), index + (0,) * array.ndim)


def fence(*values):
    return lax.optimization_barrier(values)


def ring(array, axis, step):
    return lax.ppermute(array, axis, [(i, (i + step) % RING) for i in range(RING)])


def ring_z(array, step):
    return ring(array, ("zh", "zl"), step)


def swap(array, axis):
    return lax.ppermute(array, axis, [(0, 1), (1, 0)])


def in_order(mine, other, axis_name, axis):
    first = lax.axis_index(axis_name) == 0
    return jnp.stack([jnp.where(first, mine, other), jnp.where(first, other, mine)], axis=axis)


def gather_column(block):
    y = lax.axis_index("y")
    column = put(jnp.zeros((RING, *block.shape), block.dtype), block, y)
    for step in STEPS:
        column = put(column, ring(block, "y", step), (y - step) % RING)
    return column


def both_columns(column):
    return in_order(column, swap(column, "hd"), "hd", 1).reshape(-1, column.shape[-1])


def chip_sum(parts):
    hd = lax.axis_index("hd")
    parts = parts.reshape(RING, 2, BLOCK, -1)
    total = at(parts, hd, 1).astype(jnp.float32) + swap(at(parts, 1 - hd, 1), "hd").astype(jnp.float32)
    return total.astype(jnp.bfloat16)


def column_sum(chip):
    y = lax.axis_index("y")
    arrived = [ring(at(chip, (y + step) % RING), "y", step) for step in STEPS]
    return sum((came.astype(jnp.float32) for came in arrived), at(chip, y).astype(jnp.float32))


def exchange(blocks, axes):
    return lax.all_to_all(blocks, axes, split_axis=0, concat_axis=0, tiled=True)


def sum_x(pieces):
    x = lax.axis_index("x")
    arrived = [ring(at(pieces, (x + step) % RING), "x", step) for step in STEPS]
    return sum_first([at(pieces, x), *arrived])


def sum_first(arrived):
    return sum(arrived[i].astype(jnp.float32) for i in range(len(arrived))).astype(jnp.bfloat16)


def both_zh(piece):
    return in_order(piece, swap(piece, "zh"), "zh", 0)


def spread(piece, *beside):
    x = lax.axis_index("x")
    pair = both_zh(piece)
    far, after, before = [ring(pair, "x", step) for step in STEPS]
    far, *beside = fence(far, *beside)
    whole = put(jnp.zeros((RING, *pair.shape), pair.dtype), pair, x)
    for step, block in zip(STEPS, (far, after, before)):
        whole = put(whole, block, (x - step) % RING)
    return whole, beside


def turn(values, cosine, sine):
    first, second = values[: HS // 2], values[HS // 2 :]
    return jnp.concatenate([first * cosine - second * sine, second * cosine + first * sine], axis=0)


def unturn(grads, cosine, sine):
    first, second = grads[: HS // 2], grads[HS // 2 :]
    return jnp.concatenate([first * cosine + second * sine, second * cosine - first * sine], axis=0)


def head_norm(values, gain):
    return values * lax.rsqrt(jnp.mean(values * values, axis=0, keepdims=True) + EPSILON) * gain


def head_norm_back(values, gain, grad_out):
    factor = lax.rsqrt(jnp.mean(values * values, axis=0, keepdims=True) + EPSILON)
    normal = values * factor
    scaled = grad_out * gain
    grad_in = factor * (scaled - normal * jnp.mean(scaled * normal, axis=0, keepdims=True))
    return grad_in, grad_out * normal


def allowed_keys():
    key = lax.broadcasted_iota(jnp.int32, (WIDE, ROWS), 0)
    query = lax.broadcasted_iota(jnp.int32, (WIDE, ROWS), 1) % WIDE
    return key <= query


def place_of(head):
    return head % RING * 2 + head // RING


def attend_kernel(
    half_ref, own_ref, other_ref, cos_ref, sin_ref, cos2_ref, sin2_ref, qgain_ref, kgain_ref,
    att_ref, out_ref, lse_ref, q_ref, kt_ref, k_ref, v_ref, vt_ref, total_ref,
):
    seen = own_ref.shape[1]
    count = seen // WIDE
    qgain, kgain = qgain_ref[...], kgain_ref[...]
    vt_ref[HS:, :] = jnp.ones((HS, vt_ref.shape[1]), jnp.bfloat16)
    for c in range(count):
        cols = slice(c * WIDE, (c + 1) * WIDE)
        sides = (
            (own_ref[GROUP * HS :, cols], cos_ref[:, cols], sin_ref[:, cols]),
            (other_ref[:, cols], cos2_ref[:, cols], sin2_ref[:, cols]),
        )
        for side, (pair, cosine, sine) in enumerate(sides):
            pair = pair.astype(jnp.float32)
            place = slice(side * seen + c * WIDE, side * seen + (c + 1) * WIDE)
            key = turn(head_norm(pair[:HS], kgain), cosine, sine)
            kt_ref[:, place] = key.astype(jnp.bfloat16)
            k_ref[place, :] = key.T.astype(jnp.bfloat16)
            vt_ref[:HS, place] = pair[HS:].astype(jnp.bfloat16)
            v_ref[place, :] = pair[HS:].T.astype(jnp.bfloat16)
        for head in range(GROUP):
            query = own_ref[head * HS : (head + 1) * HS, cols].astype(jnp.float32)
            query = turn(head_norm(query, qgain), cos_ref[:, cols], sin_ref[:, cols])
            q_ref[c, :, head * WIDE : (head + 1) * WIDE] = (query * SCORE_SCALE).astype(jnp.bfloat16)
    allowed = allowed_keys()

    def terms(i, start, masked):
        keys = slice(start, start + WIDE)
        weights = jnp.exp(dot(k_ref[keys, :], q_ref[i], (1, 0)))
        if masked:
            weights = jnp.where(allowed, weights, 0.0)
        return dot(vt_ref[:, keys], weights.astype(jnp.bfloat16), (1, 0))

    for i in range(count):
        total_ref[i] = sum(terms(i, c * WIDE, c == i) for c in range(i + 1))

    @pl.when(half_ref[0] == 1)
    def _():
        for i in range(count):
            total_ref[i] += sum(terms(i, seen + c * WIDE, False) for c in range(count))

    for i in range(count):
        total = total_ref[i]
        norm = total[HS : HS + 1]
        result = total[:HS] / norm
        lse_ref[i : i + 1, :] = jnp.log(norm)
        out_ref[i] = result
        for head in range(GROUP):
            part = result[:, head * WIDE : (head + 1) * WIDE].astype(jnp.bfloat16)
            att_ref[head * HS : (head + 1) * HS, i * WIDE : (i + 1) * WIDE] = part


def attend_back_kernel(
    half_ref, own_ref, grad_ref, cos_ref, sin_ref, qgain_ref, out_ref, lse_ref, q_ref, kt_ref, k_ref, v_ref,
    qgrad_ref, kv_own_ref, kv_other_ref, gain_ref, dk_ref, dv_ref, dq_ref, g_ref, delta_ref,
):
    seen = own_ref.shape[1]
    count = seen // WIDE
    qgain = qgain_ref[...]
    allowed = allowed_keys()

    def terms(i, start, masked):
        keys = slice(start, start + WIDE)
        query, grad = q_ref[i], g_ref[i]
        weights = jnp.exp(dot(k_ref[keys, :], query, (1, 0)) - lse_ref[i : i + 1, :])
        if masked:
            weights = jnp.where(allowed, weights, 0.0)
        prob_grad = dot(v_ref[keys, :], grad, (1, 0))
        score_grad = (weights * (prob_grad - delta_ref[i : i + 1, :])).astype(jnp.bfloat16)
        dv_ref[keys, :] += dot(weights.astype(jnp.bfloat16), grad, (1, 1))
        dk_ref[keys, :] += dot(score_grad, query, (1, 1))
        return dot(kt_ref[:, keys], score_grad, (1, 0))

    dk_ref[...] = jnp.zeros_like(dk_ref)
    dv_ref[...] = jnp.zeros_like(dv_ref)
    for i in range(count):
        for head in range(GROUP):
            g_ref[i, :, head * WIDE : (head + 1) * WIDE] = grad_ref[
                head * HS : (head + 1) * HS, i * WIDE : (i + 1) * WIDE
            ]
        delta_ref[i : i + 1, :] = jnp.sum(g_ref[i].astype(jnp.float32) * out_ref[i], axis=0, keepdims=True)
        dq_ref[i] = sum(terms(i, c * WIDE, c == i) for c in range(i + 1))

    @pl.when(half_ref[0] == 1)
    def _():
        for i in range(count):
            dq_ref[i] += sum(terms(i, seen + c * WIDE, False) for c in range(count))

    gain_total = jnp.zeros((HS, WIDE), jnp.float32)
    for i in range(count):
        cols = slice(i * WIDE, (i + 1) * WIDE)
        for head in range(GROUP):
            turned = dq_ref[i, :, head * WIDE : (head + 1) * WIDE] * SCORE_SCALE
            back = unturn(turned, cos_ref[:, cols], sin_ref[:, cols])
            rows = slice(head * HS, (head + 1) * HS)
            lin, gain_part = head_norm_back(own_ref[rows, cols].astype(jnp.float32), qgain, back)
            qgrad_ref[rows, cols] = lin.astype(jnp.bfloat16)
            gain_total = gain_total + gain_part
        for source, rows in ((dk_ref, slice(0, HS)), (dv_ref, slice(HS, 2 * HS))):
            kv_own_ref[rows, cols] = source[i * WIDE : (i + 1) * WIDE, :].T
            kv_other_ref[rows, cols] = source[seen + i * WIDE : seen + (i + 1) * WIDE, :].T.astype(jnp.bfloat16)
    gain_ref[...] = gain_total


def key_back_kernel(
    own_ref, kv_own_ref, kv_came_ref, cos_ref, sin_ref, kgain_ref, qgrad_ref, grad_ref, gain_ref
):
    total = kv_own_ref[...] + kv_came_ref[...].astype(jnp.float32)
    back = unturn(total[:HS], cos_ref[...], sin_ref[...])
    key = own_ref[GROUP * HS : (GROUP + 1) * HS, :].astype(jnp.float32)
    lin, gain_part = head_norm_back(key, kgain_ref[...], back)
    grad_ref[: GROUP * HS, :] = qgrad_ref[...]
    grad_ref[GROUP * HS : (GROUP + 1) * HS, :] = lin.astype(jnp.bfloat16)
    grad_ref[(GROUP + 1) * HS :, :] = total[HS:].astype(jnp.bfloat16)
    gain_ref[...] = jnp.sum(gain_part, axis=1, keepdims=True)


def pack_kernel(gate_ref, up_ref, out_ref):
    count, _, ffn = out_ref.shape
    team, half = count // 2, ffn // 2
    for place in range(team):
        blocks = []
        for ref in (gate_ref, up_ref):
            parts = [
                ref[:, (zl * team + place) * half : (zl * team + place + 1) * half].astype(jnp.float32)
                for zl in range(2)
            ]
            blocks.append(jnp.concatenate(parts, axis=1))
        block = jnp.concatenate(blocks, axis=0).astype(jnp.bfloat16)
        out_ref[place] = block
        out_ref[team + place] = block


def gate_up_terms_kernel(ffn_ref, gate_ref, up_ref, out_ref):
    few, ffn = out_ref.shape[2:]
    chunk = RING * RING * few
    for c in range(ffn_ref.shape[1] // chunk):
        left = ffn_ref[:, c * chunk : (c + 1) * chunk]
        for side, ref in enumerate((gate_ref, up_ref)):
            terms = dot(left, ref[...], (0, 0)).reshape(RING, RING, few, ffn).astype(jnp.bfloat16)
            for row in range(RING):
                for quarter in range(RING):
                    out_ref[quarter, (side * 2 + c // 2) * 8 + c % 2 * RING + row] = terms[row, quarter]


def out_terms_kernel(hd_ref, att_ref, grad_ref, mine_ref, other_ref):
    pieces, few, _ = mine_ref.shape
    terms = dot(att_ref[...], grad_ref[...], (1, 0))
    for hd in range(2):
        for piece in range(pieces):
            start = (hd * pieces + piece) * few
            block = terms[start : start + few].astype(jnp.bfloat16)

            @pl.when(hd_ref[0] == hd)
            def _():
                mine_ref[piece] = block

            @pl.when(hd_ref[0] != hd)
            def _():
                other_ref[piece] = block


def joint_terms_kernel(normed_ref, grad_ref, gains_ref, out_ref):
    team, half = 2 * RING, normed_ref.shape[1] // 2
    few = half // (8 * team)
    for zl in range(2):
        terms = dot(normed_ref[:, zl * half : (zl + 1) * half], grad_ref[...], (0, 1))
        for place in range(team):
            for piece in range(8):
                start = (place * 8 + piece) * few
                block = jnp.concatenate([terms[start : start + few], gains_ref[piece]], axis=0)
                out_ref[(piece * 2 + zl) * team + place] = block.astype(jnp.bfloat16)


def joint_sum_kernel(came_ref, out_ref):
    count, rows, cols = came_ref.shape
    team = 2 * RING
    few = rows - 4
    gains = jnp.zeros((4, cols), jnp.float32)
    parts = []
    for place in range(team):
        total = came_ref[place].astype(jnp.float32)
        for source in range(1, count // team):
            total = total + came_ref[source * team + place].astype(jnp.float32)
        parts.append(total[:few])
        gains = gains + total[few:]
    gains = gains[:2] + gains[2:]
    high = gains.astype(jnp.bfloat16).astype(jnp.float32)
    parts += [high, gains - high, jnp.zeros((4, cols), jnp.float32)]
    whole = jnp.concatenate(parts, axis=0)
    spare = jnp.zeros((whole.shape[0], out_ref.shape[1] - cols), jnp.float32)
    out_ref[...] = jnp.concatenate([whole, spare], axis=1).astype(jnp.bfloat16)


def unpack_ffn_kernel(pieces_ref, gate_ref, up_ref):
    team, few, ffn = pieces_ref.shape[2:]
    half = ffn // 2
    for side, ref in enumerate((gate_ref, up_ref)):
        blocks = [pieces_ref[0, side, place].astype(jnp.float32) for place in range(team)]
        ref[...] = jnp.concatenate(
            [block[:, zl * half : (zl + 1) * half] for zl in range(2) for block in blocks], axis=1
        )


def unpack_kernel(pieces_ref, w_down_ref, w_out_ref, w_query_ref, w_key_ref, w_value_ref, gains_ref):
    team, cols = 2 * RING, gains_ref.shape[2]
    down, out, few = w_down_ref.shape[0] // 8, w_out_ref.shape[0] // 8, w_query_ref.shape[0] // 8
    rows = down + out
    down_rows, out_rows, joint_rows = [], [], []
    for x in range(RING):
        for zh in range(2):
            piece = pieces_ref[x, zh].astype(jnp.float32)
            ready = jnp.concatenate([piece[i * rows : (i + 1) * rows] for i in range(RING)], axis=1)
            down_rows.append(ready[:down])
            out_rows.append(ready[down:])
            heads = [RING * rows + place_of(head) * few for head in range(team)]
            joint_rows.append([piece[start : start + few] for start in heads])
            gains = piece[RING * rows + team * few :, :cols]
            gains_ref[x * 2 + zh] = gains[:2] + gains[2:4]
    w_down_ref[...] = jnp.concatenate([down_rows[x * 2 + zh] for zh in range(2) for x in range(RING)], axis=0)
    w_out_ref[...] = jnp.concatenate(out_rows, axis=0)
    targets = (w_query_ref, 0, GROUP * HS), (w_key_ref, GROUP * HS, HS), (w_value_ref, (GROUP + 1) * HS, HS)
    for target, start, size in targets:
        parts = [
            jnp.concatenate([block[:, start : start + size] for block in blocks], axis=1) for blocks in joint_rows
        ]
        target[...] = jnp.concatenate(parts, axis=0)


def call(kernel, outs, scratch, args):
    smem = pl.BlockSpec(memory_space=pltpu.SMEM)
    vmem = pl.BlockSpec(memory_space=pltpu.VMEM)
    return pl.pallas_call(
        kernel,
        out_shape=[jax.ShapeDtypeStruct(shape, dtype) for shape, dtype in outs],
        in_specs=[smem if a.dtype == jnp.int32 else vmem for a in args],
        out_specs=[vmem for _ in outs],
        scratch_shapes=scratch,
        compiler_params=pltpu.CompilerParams(vmem_limit_bytes=40 * 1024 * 1024),
        cost_estimate=pl.CostEstimate(flops=1024, bytes_accessed=1024, transcendentals=0),
    )(*args)


def rope_tables(positions):
    half = HS // 2
    freqs = ROPE_BASE ** (-jnp.arange(half, dtype=jnp.float32) * 2.0 / HS)
    angles = freqs[:, None] * positions[None, :].astype(jnp.float32)
    return jnp.cos(angles), jnp.sin(angles)


def on_device(
    inputs,
    norm_gain,
    w_query,
    w_key,
    w_value,
    w_out,
    query_gain,
    key_gain,
    ffn_gain,
    w_gate,
    w_up,
    w_down,
    cotangent,
):
    f32, bf16 = jnp.float32, jnp.bfloat16
    tokens = inputs[0]
    out_grad = cotangent[0]
    rows, width = tokens.shape
    held = w_gate.shape[0]
    half_ffn = w_down.shape[0]
    ffn = 2 * half_ffn
    team = 2 * RING
    seen = team * rows
    quarter, few = width // 4, held // 4
    heads_width = GROUP * HS
    zl, hd = lax.axis_index("zl"), lax.axis_index("hd")
    tokens32 = tokens.astype(f32)

    by_head = lambda w: w.reshape(held, team, -1).transpose(1, 0, 2)
    joint_blocks = jnp.concatenate([by_head(w_query), by_head(w_key), by_head(w_value)], axis=2)
    joint_blocks = joint_blocks.reshape(2, RING, held, -1).swapaxes(0, 1).reshape(team, held, -1)
    joint_blocks = jnp.concatenate([joint_blocks, joint_blocks])
    normed = rms_forward(tokens32, norm_gain).astype(bf16)
    w_joint = exchange(joint_blocks, ("zl", "y", "hd"))
    normed_all = both_columns(gather_column(normed))
    grad_all = lax.all_gather(out_grad, TEAM, axis=0, tiled=True)
    my_rows = lambda w: lax.dynamic_slice_in_dim(w, lax.axis_index("x") * few, few, 0)
    gate_up_rows = call(pack_kernel, [((2 * team, 2 * few, ffn), bf16)], [], (my_rows(w_gate), my_rows(w_up)))[0]
    out_rows = in_order(w_out, swap(w_out, "zl"), "zl", 0)
    w_out_own = in_order(at(out_rows, hd), swap(at(out_rows, 1 - hd), "hd"), "hd", 0).reshape(heads_width, width)
    w_joint, w_out_own, gate_up_rows, normed_all = fence(w_joint, w_out_own, gate_up_rows, normed_all)
    w_joint = w_joint.reshape(width, -1)
    gate_up_rows = exchange(gate_up_rows, ("zl", "y", "hd"))
    down_other = jnp.concatenate([ring_z(w_down[: half_ffn // 2], 1), ring_z(w_down[half_ffn // 2 :], 3)])
    w_down_own = in_order(w_down, down_other, "zl", 0).reshape(ffn, width)

    joint = dot(w_joint, normed_all, (0, 1)).astype(bf16)
    other_kv, gate_up_rows = fence(swap(joint[heads_width:], "zl"), gate_up_rows)
    base = jnp.arange(seen, dtype=jnp.int32)
    cosine, sine = rope_tables(base + zl * seen)
    cosine2, sine2 = rope_tables(base + (1 - zl) * seen)
    half_flag = jnp.reshape(zl, (1,)).astype(jnp.int32)
    qgain, kgain = query_gain[:, None], key_gain[:, None]
    wide = seen // WIDE
    att, att32, lse, q_rot, kt_rot, k_rot, v_nat = call(
        attend_kernel,
        [
            ((heads_width, seen), bf16),
            ((wide, HS, ROWS), f32),
            ((wide, ROWS), f32),
            ((wide, HS, ROWS), bf16),
            ((HS, 2 * seen), bf16),
            ((2 * seen, HS), bf16),
            ((2 * seen, HS), bf16),
        ],
        [pltpu.VMEM((2 * HS, 2 * seen), bf16), pltpu.VMEM((wide, 2 * HS, ROWS), f32)],
        (half_flag, joint, other_kv, cosine, sine, cosine2, sine2, qgain, kgain),
    )
    gate_up_all = lax.all_gather(gate_up_rows, "x", axis=0, tiled=False)
    chip = chip_sum(dot(att, w_out_own, (0, 0)).astype(bf16))
    middle = tokens32 + column_sum(chip)
    gate_up_all = gate_up_all.reshape(RING, 2 * team, 2, few, ffn).transpose(2, 1, 0, 3, 4).reshape(2, width, ffn)
    w_gate_own, w_up_own = gate_up_all[0], gate_up_all[1]
    ffn_in = rms_forward(middle, ffn_gain).astype(bf16)
    ffn_all = both_columns(gather_column(ffn_in))
    hidden_grad = dot(grad_all, w_down_own, (1, 1))
    gate = dot(ffn_all, w_gate_own, (1, 0))
    up_val = dot(ffn_all, w_up_own, (1, 0))
    sigmoid = jax.nn.sigmoid(gate)
    hidden = (gate * sigmoid * up_val).astype(bf16)
    gate_grad = (hidden_grad * up_val * sigmoid * (1.0 + gate * (1.0 - sigmoid))).astype(bf16)
    up_grad = (hidden_grad * gate * sigmoid).astype(bf16)
    ffn_part = (dot(gate_grad, w_gate_own, (1, 1)) + dot(up_grad, w_up_own, (1, 1))).astype(bf16)
    chip, gate_right, up_right, hidden_left = fence(chip_sum(ffn_part), gate_grad, up_grad, hidden)
    ffn_in_grad = column_sum(chip)

    gate_up_terms = call(
        gate_up_terms_kernel,
        [((RING, 4 * team, few, ffn), bf16)],
        [],
        (ffn_all, gate_right, up_right),
    )[0]
    gate_up_sum = lax.psum_scatter(gate_up_terms, "x", scatter_dimension=0, tiled=False)
    down_terms = dot(hidden_left, grad_all, (0, 0)).astype(bf16).reshape(4, half_ffn // 2, width)
    down_came = exchange(down_terms, ("zl", "zh"))
    ffn_in_grad, _, _, hidden_last = fence(ffn_in_grad, gate_up_terms, down_terms, hidden)

    middle_part, ffn_gain_part = rms_backward(middle, ffn_gain, ffn_in_grad)
    middle_grad = out_grad.astype(f32) + middle_part
    branch_grad = middle_grad.astype(bf16)
    out_part = dot(hidden_last, w_down_own, (1, 0)).astype(bf16)
    column, out_part, down_came = fence(gather_column(branch_grad), out_part, down_came)
    out_sum = lax.psum_scatter(out_part, TEAM, scatter_dimension=0, tiled=True)
    branch_all = both_columns(column)
    att_grad = dot(w_out_own, branch_all, (1, 1)).astype(bf16)

    out_mine, out_other = call(
        out_terms_kernel,
        [((8, held // 8, width), bf16)] * 2,
        [],
        (jnp.reshape(hd, (1,)).astype(jnp.int32), att, branch_all),
    )
    out_pieces = in_order(out_mine, swap(out_other, "hd"), "hd", 1)
    att_grad, out_pieces = fence(att_grad, out_pieces)
    out_came = exchange(out_pieces.reshape(16, held // 8, width), SUMMED)
    q_grad, kv_own, kv_other, qgain_part = call(
        attend_back_kernel,
        [
            ((heads_width, seen), bf16),
            ((2 * HS, seen), f32),
            ((2 * HS, seen), bf16),
            ((HS, WIDE), f32),
        ],
        [
            pltpu.VMEM((2 * seen, HS), f32),
            pltpu.VMEM((2 * seen, HS), f32),
            pltpu.VMEM((wide, HS, ROWS), f32),
            pltpu.VMEM((wide, HS, ROWS), bf16),
            pltpu.VMEM((2 * wide, ROWS), f32),
        ],
        (half_flag, joint, att_grad, cosine, sine, qgain, att32, lse, q_rot, kt_rot, k_rot, v_nat),
    )
    gate_up_came = exchange(gate_up_sum, ("zh", "zl") + TEAM)
    kv_came, gate_up_came, att, down_came = fence(swap(kv_other, "zl"), gate_up_came, att, down_came)
    joint_grad, kgain_part = call(
        key_back_kernel,
        [(joint.shape, bf16), ((HS, 1), f32)],
        [],
        (joint, kv_own, kv_came, cosine, sine, kgain, q_grad),
    )
    normed_part = dot(joint_grad, w_joint, (0, 1))
    norm_gain_part = jnp.sum(normed_part * normed_all.astype(f32), axis=0) / norm_gain
    normed_part = normed_part.astype(bf16)
    gains = [norm_gain_part, ffn_gain_part, jnp.sum(qgain_part, axis=1), kgain_part[:, 0]]
    joint_width = joint.shape[0]
    gains = jnp.concatenate([*gains, jnp.zeros((16 * joint_width - 2 * width - 2 * HS,), f32)])
    gains = gains.reshape(8, 2, joint_width)
    high = lax.optimization_barrier(gains.astype(bf16)).astype(f32)
    joint_pieces = call(
        joint_terms_kernel,
        [((16 * team, held // 8 + 4, joint_width), bf16)],
        [],
        (normed_all, joint_grad, jnp.concatenate([high, gains - high], axis=1)),
    )[0]
    joint_pieces, gate_up_came, out_came, normed_part, down_came = fence(
        joint_pieces, gate_up_came, out_came, normed_part, down_came
    )
    joint_came = exchange(joint_pieces, SUMMED + TEAM)
    gate_up_mine = sum_first(gate_up_came.reshape(4, team * few, ffn))
    gate_up_whole = lax.all_gather(both_zh(gate_up_mine), "x", axis=0, tiled=False)
    gate_up_whole = gate_up_whole.reshape(RING, 2, team, few, ffn)
    down_mine = sum_x(sum_first(down_came).reshape(4, half_ffn // 8, width))
    ready = jnp.concatenate([down_mine, sum_first(out_came)])
    ready = jnp.concatenate([ready[:, i * quarter : (i + 1) * quarter] for i in range(4)])
    joint_came, ready, chip = fence(joint_came, ready, chip_sum(normed_part))
    joint_mine = call(joint_sum_kernel, [((held + 8, quarter), bf16)], [], (joint_came,))[0]
    input_part, _ = rms_backward(tokens32, norm_gain, column_sum(chip))
    output = (middle + out_sum.astype(f32)).astype(bf16)
    pieces, (input_grad, output) = spread(
        jnp.concatenate([ready, joint_mine]), middle_grad + input_part, output
    )
    block = lambda shape, index: pl.BlockSpec(shape, index)
    w_gate_grad, w_up_grad = pl.pallas_call(
        unpack_ffn_kernel,
        grid=(RING,),
        in_specs=[block((1, 2, team, few, ffn), lambda i: (i, 0, 0, 0, 0))],
        out_specs=[block((few, team * ffn), lambda i: (i, 0))] * 2,
        out_shape=[jax.ShapeDtypeStruct((held, team * ffn), f32)] * 2,
        compiler_params=pltpu.CompilerParams(vmem_limit_bytes=40 * 1024 * 1024),
    )(gate_up_whole)
    shapes = [(half_ffn, width), (held, width)] + [(held, w.shape[1]) for w in (w_query, w_key, w_value)]
    shapes.append((8, 2, joint_width))
    w_down_grad, w_out_grad, w_query_grad, w_key_grad, w_value_grad, gains = call(
        unpack_kernel, [(shape, f32) for shape in shapes], [], (pieces,)
    )

    gains = gains.reshape(-1)
    return (
        output[None],
        input_grad[None],
        gains[:width],
        w_query_grad,
        w_key_grad,
        w_value_grad,
        w_out_grad,
        gains[2 * width : 2 * width + HS],
        gains[2 * width + HS : 2 * width + 2 * HS],
        gains[width : 2 * width],
        w_gate_grad,
        w_up_grad,
        w_down_grad,
    )


def solution(mesh):
    fine = Mesh(mesh.devices.reshape(4, 2, 2, 4, 2), ("x", "zh", "zl", "y", "hd"))
    by_tokens = P(("x", "zh"), ("zl", "y", "hd"), None)
    by_rows = P(("zl", "y", "hd"), None)
    return jax.shard_map(
        on_device,
        mesh=fine,
        in_specs=(
            by_tokens, P(), by_rows, by_rows, by_rows, by_rows, P(), P(), P(), by_rows, by_rows, by_rows, by_tokens
        ),
        out_specs=(
            by_tokens, by_tokens, P(), by_rows, by_rows, by_rows, by_rows, P(), P(), P(), by_rows, by_rows, by_rows
        ),
        check_vma=False,
    )
```
